32 devices in a mesh: dp: 4 (over z), row: 2 (over core), col: 4 (over y, x).
Axes of the slice: x: 2, y: 2, z: 4, core: 2. Of those that a mesh axis runs over, the one named last changes fastest.
Arguments:
- x_input: bfloat16 [4, 32, 64, 640], P('dp', 'row', 'col'), may hold values from -6 to 6
- pre_act: bfloat16 [4, 32, 64, 640], P('dp', 'row', 'col'), may hold values from -6 to 6
- out_grad: bfloat16 [4, 32, 64, 640], P('dp', 'row', 'col'), may hold values from -0.15625 to 0.15625
- conv_weight: bfloat16 [3, 3, 640, 640], replicated, may hold values from -0.078125 to 0.078125
- q_prev: float32 [5760, 2, 64], replicated, may hold values from -6 to 6
Outputs:
- p_basis: float32 [640, 2, 64], P('dp')
- q_next: float32 [5760, 2, 64], P('dp')
The draws below stay inside these ranges and needn't reach their ends.
All inputs are finite; a program needn't handle non-finite values.
Results may differ from the reference program's by a relative error of at most 0.0036.
Values may be sent and summed in bfloat16 or wider, within the bound.
No kernel may reach another device: no remote copies, remote signals or barrier semaphores. Data moves between devices by JAX's collectives and lax.ppermute only.
A program may use at most 128 MiB of HBM per device.

```python
import jax
import jax.numpy as jnp
from jax import lax

C = 640
RANK = 64
IMAGES = 4
HIMG = 32
WIMG = 64
KROWS = 5760


def block_scale(key, shape, cuts, least, high):
    factor_of = 1.0
    for position, blocks in cuts:
        steps = jax.random.uniform(jax.random.fold_in(jax.random.fold_in(key, 6), position), (blocks,), jnp.float32, least / len(cuts), high / len(cuts))
        factor_of = factor_of * jnp.repeat(jnp.exp(steps), shape[position] // blocks).reshape((-1,) + (1,) * (len(shape) - 1 - position))
    return factor_of


def noise(own_key, dims, width, reach, cuts=(), dtype=jnp.bfloat16):
    array = width * jax.random.normal(own_key, dims, jnp.float32)
    if cuts:
        array = array * block_scale(own_key, dims, cuts, -0.22, 0.18)
    return jnp.clip(array, -reach, reach).astype(dtype)


def setup_inputs(seed: int = 0) -> dict:
    key_of = jax.random.split(jax.random.key(seed), 6)
    x_input = noise(key_of[0], (IMAGES, HIMG, WIMG, C), 1.0, 6.0, ((0, 4), (1, 2), (2, 4)))
    pre_act = noise(key_of[1], (IMAGES, HIMG, WIMG, C), 1.0, 6.0, ((0, 4), (1, 2), (2, 4)))
    out_grad = noise(key_of[2], (IMAGES, HIMG, WIMG, C), 0.01, 0.15625, ((0, 4), (1, 2), (2, 4)))
    conv_weight = noise(key_of[3], (3, 3, C, C), (9 * C) ** -0.5, 0.078125)
    q_prev = noise(key_of[4], (KROWS, 2, RANK), 1.0, 6.0, (), jnp.float32)
    return {"x_input": x_input, "pre_act": pre_act, "out_grad": out_grad, "conv_weight": conv_weight, "q_prev": q_prev}


def silu_slope(pre_float):
    sigma = jax.nn.sigmoid(pre_float)
    return sigma * (1.0 + pre_float * (1.0 - sigma))

def contract_first(left, right, exact):
    if exact:
        return lax.dot_general(left.astype(jnp.float32), right.astype(jnp.float32), (((0,), (0,)), ((), ())), precision=lax.Precision.HIGHEST, preferred_element_type=jnp.float32)
    return lax.dot_general(left.astype(jnp.float32), right.astype(jnp.float32), (((0,), (0,)), ((), ())), preferred_element_type=jnp.float32)

def reference(x_input, pre_act, out_grad, conv_weight, q_prev):
    images, height, breadth, channels = x_input.shape
    pixels = images * height * breadth
    padding = ((0, 0), (1, 1), (1, 1), (0, 0))
    pre_float = pre_act.astype(jnp.float32)
    hidden = jax.nn.silu(pre_float).astype(jnp.bfloat16)
    hidden_flat = hidden.reshape(pixels, channels)
    grad_pad = jnp.pad(out_grad, padding)
    back_grad = jnp.zeros((pixels, channels), jnp.float32)
    second_taps = []
    for shift_row in (-1, 0, 1):
        for shift_col in (-1, 0, 1):
            window = grad_pad[:, 1 - shift_row:1 - shift_row + height, 1 - shift_col:1 - shift_col + breadth, :].reshape(pixels, channels)
            back_grad = back_grad + lax.dot_general(window.astype(jnp.float32), conv_weight[shift_row + 1, shift_col + 1].astype(jnp.float32), (((1,), (1,)), ((), ())), preferred_element_type=jnp.float32)
            second_taps.append(contract_first(hidden_flat, window, False))
    pre_grad = (back_grad * silu_slope(pre_float.reshape(pixels, channels))).astype(jnp.bfloat16)
    deriv_pad = jnp.pad(pre_grad.reshape(images, height, breadth, channels), padding)
    input_flat = x_input.reshape(pixels, channels)
    first_taps = []
    for shift_row in (-1, 0, 1):
        for shift_col in (-1, 0, 1):
            window = deriv_pad[:, 1 - shift_row:1 - shift_row + height, 1 - shift_col:1 - shift_col + breadth, :].reshape(pixels, channels)
            first_taps.append(contract_first(input_flat, window, False))
    moments = [jnp.stack(first_taps).reshape(9 * channels, channels), jnp.stack(second_taps).reshape(9 * channels, channels)]
    bases = []
    nexts = []
    for layer in range(2):
        power_raw = contract_first(moments[layer], q_prev[:, layer, :], True)
        gram_matrix = jnp.dot(power_raw.T.astype(jnp.float32), power_raw.astype(jnp.float32), precision=lax.Precision.HIGHEST, preferred_element_type=jnp.float32)
        lower = jnp.linalg.cholesky(gram_matrix)
        ortho_basis = lax.linalg.triangular_solve(lower, power_raw, left_side=False, lower=True, transpose_a=True)
        bases.append(ortho_basis)
        nexts.append(jnp.dot(moments[layer].astype(jnp.float32), ortho_basis.astype(jnp.float32), precision=lax.Precision.HIGHEST, preferred_element_type=jnp.float32))
    return (jnp.stack(bases, axis=1), jnp.stack(nexts, axis=1))
```

```python
import jax
import jax.numpy as jnp
from jax import lax
from jax.sharding import PartitionSpec as P

PLANE = ("row", "col")
ALL = ("dp", "row", "col")
TAPS = [(a, b) for a in (-1, 0, 1) for b in (-1, 0, 1)]
BF = jnp.bfloat16
F32 = jnp.float32


def dot(left, right, dims):
    return lax.dot_general(left, right, (dims, ((), ())), preferred_element_type=F32)


def halves(value):
    high = lax.reduce_precision(value, 8, 7)
    return high.astype(BF), (value - high).astype(BF)


def exchange(chunks, axes):
    return lax.all_to_all(chunks, axes, 0, 0, tiled=True)


def rim_exchange(tile):
    height, width, channels = tile.shape
    rows, cols = lax.axis_size("row"), lax.axis_size("col")
    row, col = lax.axis_index("row"), lax.axis_index("col")
    edge = jnp.where(row == 0, tile[-1], tile[0])
    first, last = tile[:, 0], tile[:, -1]
    none = jnp.zeros_like(edge)
    chunks = []
    for r in range(rows):
        for c in range(cols):
            step = c - col
            along = jnp.where(step == 1, last, jnp.where(step == -1, first, none))
            cross = jnp.where(
                step == 0,
                edge,
                jnp.where(step == 1, edge[-1:], jnp.where(step == -1, edge[:1], none)),
            )
            chunks.append(jnp.where(row == r, along, cross))
    got = exchange(jnp.stack(chunks), PLANE).reshape(rows, cols, height, channels)
    other = rows - 1 - row
    west, east = jnp.maximum(col - 1, 0), jnp.minimum(col + 1, cols - 1)
    has_west, has_east = col > 0, col < cols - 1
    zero = jnp.zeros_like(edge)
    left = jnp.where(has_west, got[row, west], zero)
    right = jnp.where(has_east, got[row, east], zero)
    beside = got[other, col]
    corner_w = jnp.where(has_west, got[other, west][:1], zero[:1])
    corner_e = jnp.where(has_east, got[other, east][:1], zero[:1])
    line = jnp.concatenate([corner_w, beside, corner_e], axis=0)
    top = jnp.where(row == 0, jnp.zeros_like(line), line)[None]
    bottom = jnp.where(row == 0, line, jnp.zeros_like(line))[None]
    middle = jnp.concatenate([left[:, None], tile, right[:, None]], axis=1)
    return jnp.concatenate([top, middle, bottom], axis=0)


def on_device(x_input, pre_act, out_grad, conv_weight, q_prev):
    height, width, channels = x_input.shape[1:]
    pixels = height * width
    rank = q_prev.shape[2]
    images, rows, cols = (lax.axis_size(a) for a in ALL)
    z, row, col = (lax.axis_index(a) for a in ALL)
    plane = rows * cols
    share = channels // cols
    x_tile, act_tile, g_tile = (
        v.reshape(height, width, channels) for v in (x_input, pre_act, out_grad)
    )
    act = act_tile.astype(F32)
    sigma = jax.nn.sigmoid(act)
    hidden = (act * sigma).astype(BF)

    padded = rim_exchange(jnp.concatenate([x_tile, g_tile], axis=-1))
    x_pad, g_pad = padded[..., :channels], padded[..., channels:]

    both = jnp.stack(
        [x_tile.reshape(pixels, channels).T, hidden.reshape(pixels, channels).T]
    ).reshape(plane, share, pixels)
    slices = exchange(both, PLANE)

    back = jnp.zeros((pixels, channels), F32)
    for a, b in TAPS:
        window = g_pad[1 - a : 1 - a + height, 1 - b : 1 - b + width].reshape(pixels, channels)
        back = back + dot(window, conv_weight[a + 1, b + 1], ((1,), (1,)))
    slope = sigma * (1.0 + act * (1.0 - sigma))
    pre_grad = (back * slope.reshape(pixels, channels)).astype(BF)

    q_t = q_prev.transpose(1, 2, 0)
    q_hl = jnp.concatenate(halves(q_t), axis=1).reshape(2, 2 * rank, 9, channels)
    y_one = jnp.einsum(
        "yxi,mti->yxtm", x_pad, q_hl[0], preferred_element_type=F32
    )
    y_two = jnp.einsum("yxi,mti->yxtm", hidden, q_hl[1], preferred_element_type=F32)
    y_two = jnp.pad(y_two, ((2, 2), (2, 2), (0, 0), (0, 0)))
    z_one = jnp.zeros((height, width, 2 * rank), F32)
    z_two = jnp.zeros((height + 2, width + 2, 2 * rank), F32)
    for t, (a, b) in enumerate(TAPS):
        z_one = z_one + y_one[1 + a : 1 + a + height, 1 + b : 1 + b + width, t]
        z_two = z_two + y_two[1 + a : 3 + a + height, 1 + b : 3 + b + width, t]
    z_one = (z_one[..., :rank] + z_one[..., rank:]).reshape(pixels, rank)
    z_two = (z_two[..., :rank] + z_two[..., rank:]).reshape(-1, rank)
    p_parts = []
    for left, right in ((z_one, pre_grad), (z_two, g_pad.reshape(-1, channels))):
        high, low = halves(left)
        p_parts.append(dot(high, right, ((0,), (0,))) + dot(low, right, ((0,), (0,))))
    p_t = jnp.concatenate(p_parts, axis=0)

    devices = images * plane
    if (2 * rank) % devices == 0:
        rows_each = 2 * rank // devices
        mine = exchange(p_t.reshape(devices, rows_each, channels), ALL).sum(0)
        p_t = exchange(jnp.broadcast_to(mine, (devices, rows_each, channels)), ALL)
        p_t = p_t.reshape(2 * rank, channels)
    else:
        p_t = lax.psum(p_t, ALL)

    p_hl = jnp.stack(halves(p_t))
    w_parts = []
    for layer, right in ((0, pre_grad), (1, g_tile.reshape(pixels, channels))):
        part = p_hl[:, layer * rank : (layer + 1) * rank]
        w_parts.append(dot(right, part[0], ((1,), (1,))) + dot(right, part[1], ((1,), (1,))))
    w_own = jnp.concatenate(halves(jnp.stack(w_parts)), axis=-1)
    w_all = exchange(
        jnp.broadcast_to(w_own[:, None], (2, cols, pixels, 2 * rank)).reshape(
            plane, pixels, 2 * rank
        ),
        PLANE,
    )

    p_layers = p_t.reshape(2, rank, channels)
    gram = jnp.einsum("lrm,lsm->lrs", p_layers, p_layers, precision=lax.Precision.HIGHEST)
    lower = jnp.linalg.cholesky(gram)
    eye = jnp.broadcast_to(jnp.eye(rank, dtype=F32), (2, rank, rank))
    inverse = lax.linalg.triangular_solve(lower, eye, left_side=True, lower=True)
    basis = jnp.einsum("lsr,lrm->lsm", inverse, p_layers, precision=lax.Precision.HIGHEST)
    count = channels // images
    basis_out = lax.dynamic_slice_in_dim(basis, z * count, count, 2).transpose(2, 0, 1)

    def image_of(tiles):
        return (
            tiles.reshape(rows, cols, height, width, -1)
            .transpose(0, 2, 1, 3, 4)
            .reshape(rows * height, cols * width, -1)
        )

    w_image = jnp.pad(image_of(w_all), ((1, 1), (1, 1), (0, 0)))
    x_image = image_of(slices.transpose(0, 2, 1)).reshape(-1, share)
    u_parts = []
    for a, b in TAPS:
        window = w_image[1 - a : 1 - a + rows * height, 1 - b : 1 - b + cols * width]
        u_parts.append(dot(window.reshape(-1, 2 * rank), x_image, ((0,), (0,))))
    u = jnp.stack(u_parts)
    u = u[:, :rank] + u[:, rank:]
    own_inverse = inverse[row]
    if images == 4 and cols == 4 and rows == 2:
        u = jnp.pad(u, ((0, 1), (0, 0), (0, 0)))
        parts = [
            lax.dynamic_slice_in_dim(u, (9 * k - col + 3) // 4, 3, 0) for k in range(images)
        ]
        got = exchange(jnp.stack(parts), ("dp",)).sum(0)
        mine = jnp.einsum(
            "sr,tri->tsi", own_inverse, got, precision=lax.Precision.HIGHEST
        ).astype(BF)
        every = exchange(jnp.broadcast_to(mine, (plane,) + mine.shape), PLANE)
        every = every.reshape(rows, cols, 3, rank, share)
        blocks = [
            lax.dynamic_index_in_dim(every, (z + j) % cols, 1, False)[:, j // 4] for j in range(9)
        ]
        q_out = jnp.concatenate(blocks, axis=-1).astype(F32).transpose(2, 0, 1)
    else:
        u = lax.psum(u, "dp")
        mine = jnp.einsum("sr,tri->tsi", own_inverse, u, precision=lax.Precision.HIGHEST)
        every = lax.all_gather(mine, PLANE).reshape(rows, cols, 9, rank, share)
        every = every.transpose(2, 1, 4, 0, 3).reshape(9 * channels, rows, rank)
        count = 9 * channels // images
        q_out = lax.dynamic_slice_in_dim(every, z * count, count, 0)
    return basis_out, q_out


def solution(mesh):
    tiles = P("dp", "row", "col", None)
    return jax.shard_map(
        on_device,
        mesh=mesh,
        in_specs=(tiles, tiles, tiles, P(), P()),
        out_specs=(P("dp", None, None), P("dp", None, None)),
        check_vma=False,
    )
```

```python
import jax
import jax.numpy as jnp
from jax import lax
from jax.experimental import pallas as pl
from jax.experimental.pallas import tpu as pltpu
from jax.sharding import PartitionSpec as P

PLANE = ("row", "col")
ALL = ("dp", "row", "col")
BF = jnp.bfloat16
F32 = jnp.float32
NN = ((1,), (0,))
NT = ((1,), (1,))
TN = ((0,), (0,))
VMEM_LIMIT = 40 * 1024 * 1024


def dot(left, right, dims, precision=None):
    return lax.dot_general(
        left, right, (dims, ((), ())), precision=precision, preferred_element_type=F32
    )


def call(body, out, flops, moved, **extra):
    return pl.pallas_call(
        body,
        out_shape=out,
        cost_estimate=pl.CostEstimate(flops=flops, bytes_accessed=moved, transcendentals=0),
        compiler_params=pltpu.CompilerParams(vmem_limit_bytes=VMEM_LIMIT),
        **extra,
    )


def exchange(chunks, axes):
    return lax.all_to_all(chunks, axes, 0, 0, tiled=True)


def stacked_halves(value):
    high = value.astype(BF)
    return jnp.concatenate([high, (value - high.astype(F32)).astype(BF)], axis=0)


def paired_halves(value):
    total = value + pltpu.roll(value, 64, 1)
    high = total.astype(BF).astype(F32)
    lane = lax.broadcasted_iota(jnp.int32, value.shape, 1)
    return jnp.where(lane < 64, high, total - high)


def rim_body(place, x_ref, g_ref, out_ref):
    row, col = place[1], place[2]
    rows, cols = 2, out_ref.shape[0] // 2
    for i, ref in enumerate((x_ref, g_ref)):
        tile = ref[...].astype(F32)
        first, last = tile[:, 0, :], tile[:, -1, :]
        edge = jnp.where(row == 0, tile[-1], tile[0])
        span = slice(16 * i, 16 * i + 16)
        for r in range(rows):
            for c in range(cols):
                along = jnp.where(c > col, last, first)
                out_ref[r * cols + c, span] = jnp.where(row == r, along, edge).astype(BF)


def rim_pick(row, col, cols):
    shape = (3, 18, 16)
    s, y, x = (lax.broadcasted_iota(jnp.int32, shape, i) for i in range(3))
    y, x = y - 1, x + s - 1
    up = jnp.where(y < 0, -1, jnp.where(y > 15, 1, 0))
    side = jnp.where(x < 0, -1, jnp.where(x > 15, 1, 0))
    there_r, there_c = row + up, col + side
    inside = (there_r >= 0) & (there_r < 2) & (there_c >= 0) & (there_c < cols)
    cell = jnp.where(up != 0, x - 16 * side, y)
    got = 256 + (there_r * cols + there_c) * 16 + cell
    index = jnp.where((up == 0) & (side == 0), 16 * y + x, got)
    index = jnp.where(inside, index, -1).reshape(3, 288, 1)
    width = 256 + 32 * cols
    return (index == lax.broadcasted_iota(jnp.int32, (3, 288, width), 2)).astype(BF)


def prepare_body(x_ref, act_ref, q_ref, slices_ref, q_one_ref, y_ref, hidden_ref):
    share = slices_ref.shape[1]

    @pl.when(pl.program_id(0) == 0)
    def _():
        act = act_ref[...].astype(F32)
        hidden_ref[...] = (act / (1.0 + jnp.exp(-act))).astype(BF)
        for layer, ref in enumerate((x_ref, hidden_ref)):
            turned = ref[...].astype(F32).T
            for k in range(4):
                pieces = [turned[160 * j + 40 * k : 160 * j + 40 * k + 40] for j in range(4)]
                slices_ref[4 * layer + k] = jnp.concatenate(pieces, axis=0).astype(BF)

    q = q_ref[...]
    q_one_ref[...] = stacked_halves(q[:64])
    y = dot(stacked_halves(q[64:]), hidden_ref[...], NT)
    y_ref[0] = stacked_halves(y[:64] + y[64:])


def power_body(
    x_ref, g_ref, got_ref, pick_ref, act_ref, q_ref, y_ref, w_ref,
    grad_ref, p_ref, x_win, g_win, back, z_sum, p_sum,
):
    t = pl.program_id(0)

    @pl.when(t == 0)
    def _():
        for i, (ref, win) in enumerate(((x_ref, x_win), (g_ref, g_win))):
            cells = got_ref[:, 16 * i : 16 * i + 16, :].reshape(-1, 640)
            cells = jnp.concatenate([ref[...], cells], axis=0)
            for s in range(3):
                win[s] = dot(pick_ref[s], cells, NN).astype(BF)
        back[...] = jnp.zeros_like(back)
        z_sum[...] = jnp.zeros_like(z_sum)
        p_sum[...] = jnp.zeros_like(p_sum)

    a, b = t // 3, t % 3
    grads = g_win[2 - b, pl.ds(pl.multiple_of(16 * (2 - a), 16), 256), :]
    inputs = x_win[b, pl.ds(pl.multiple_of(16 * a, 16), 256), :]
    back[...] += dot(grads, w_ref[0, 0], NT)
    z_sum[...] += dot(inputs, q_ref[...], NT)
    p_sum[...] += dot(y_ref[0], grads, NN)

    @pl.when(t == 8)
    def _():
        act = act_ref[...].astype(F32)
        sigma = 1.0 / (1.0 + jnp.exp(-act))
        grad = (back[...] * (sigma * (1.0 + act * (1.0 - sigma)))).astype(BF)
        grad_ref[...] = grad
        one = dot(paired_halves(z_sum[...]).astype(BF), grad, TN)
        two = p_sum[...]
        each = p_ref.shape[1]
        for layer, value in enumerate((one, two)):
            value = value[:64] + value[64:]
            for i in range(64 // each):
                p_ref[layer * (64 // each) + i] = value[i * each : (i + 1) * each]


def sum_body(got_ref, out_ref):
    total = jnp.sum(got_ref[...], axis=0)
    for i in range(out_ref.shape[0]):
        out_ref[i] = total


def project_body(got_ref, grad_ref, g_ref, w_ref, p_ref):
    each = got_ref.shape[1]
    for i in range(16):
        rows = [got_ref[i * (8 // each) + j] for j in range(8 // each)]
        p_ref[8 * i : 8 * i + 8, :] = jnp.concatenate(rows, axis=0)
    for layer, ref in enumerate((grad_ref, g_ref)):
        factor = stacked_halves(p_ref[64 * layer : 64 * layer + 64, :])
        out = paired_halves(dot(ref[...], factor, NT)).astype(BF)
        for k in range(4):
            w_ref[4 * layer + k] = out


def factor_body(p_ref, inverse_ref, basis_ref):
    high = lax.Precision.HIGHEST
    line = lax.broadcasted_iota(jnp.int32, (64, 128), 0)
    lane = lax.broadcasted_iota(jnp.int32, (64, 128), 1)
    unit = jnp.where(lane == line + 64, 1.0, 0.0)
    tables = []
    for layer in range(2):
        p = p_ref[64 * layer : 64 * layer + 64, :]
        gram = dot(p, p, NT, high)
        tables.append(jnp.concatenate([gram, unit[:, 64:]], axis=1))
    for k in range(64):
        for layer in range(2):
            table = tables[layer]
            pivot_row = table[k : k + 1, :]
            scaled = pivot_row / pivot_row[:, k : k + 1]
            column = jnp.where(line[:, :1] > k, table[:, k : k + 1], 0.0)
            tables[layer] = table - column * scaled
    for layer in range(2):
        table = tables[layer]
        pivots = jnp.sum(jnp.where(line == lane, table, 0.0), axis=1, keepdims=True)
        inverse = table[:, 64:] / jnp.sqrt(pivots)
        inverse_ref[layer] = inverse
        basis_ref[layer] = dot(inverse, p_ref[64 * layer : 64 * layer + 64, :], NN, high)


def taps_body(w_ref, x_ref, out_ref, image, sums):
    zero = jnp.zeros((1, 4, 16, 384), BF)
    image[0:1] = zero
    image[33:34] = zero
    at = lax.broadcasted_iota(jnp.int32, (1024, 128), 0) % 64
    for r in range(2):
        tiles = [w_ref[4 * r + c].astype(F32).reshape(16, 16, 128) for c in range(4)]
        flat = jnp.stack(tiles, axis=1).reshape(1024, 128)
        left = jnp.where(at == 63, 0.0, pltpu.roll(flat, 1023, 0))
        right = jnp.where(at == 0, 0.0, pltpu.roll(flat, 1, 0))
        for i, value in enumerate((left, flat, right)):
            image[1 + 16 * r : 17 + 16 * r, :, :, 128 * i : 128 * i + 128] = value.astype(BF).reshape(
                16, 4, 16, 128
            )
    for a in range(3):
        total = jnp.zeros((160, 384), F32)
        for r in range(2):
            for c in range(4):
                window = image[16 * r + 2 - a : 16 * r + 18 - a, c].reshape(256, 384)
                total = total + dot(x_ref[4 * r + c], window, NN)
        for b in range(3):
            t = 3 * a + b
            sums[160 * t : 160 * t + 160, :] = paired_halves(total[:, 128 * b : 128 * b + 128])
    sums[1440:1472, :] = jnp.zeros((32, 128), F32)
    for i in range(4):
        out_ref[i] = sums[360 * i : 360 * i + 384, :].astype(BF)


def rotate_body(place, got_ref, inverse_ref, out_ref):
    total = got_ref[0].astype(F32)
    for i in range(1, got_ref.shape[0]):
        total = total + got_ref[i].astype(F32)
    total = total + pltpu.roll(total, 64, 1)
    out = dot(inverse_ref[place[1]], total[:, :64], NT, lax.Precision.HIGHEST).astype(BF)
    for i in range(out_ref.shape[0]):
        out_ref[i] = out


def place_body(got_ref, out_ref):
    for layer in range(2):
        for k in range(4):
            value = got_ref[4 * layer + k].astype(F32)
            for j in range(9):
                start = 160 * j + 40 * k
                out_ref[layer, :, start : start + 40] = value[:, 40 * j : 40 * j + 40]


def on_device(x_input, pre_act, out_grad, conv_weight, q_prev):
    shape = jax.ShapeDtypeStruct
    whole = pl.BlockSpec(memory_space=pltpu.VMEM)
    small = pl.BlockSpec(memory_space=pltpu.SMEM)
    images, rows, cols = (lax.axis_size(a) for a in ALL)
    z, row, col = (lax.axis_index(a) for a in ALL)
    place = jnp.stack([z, row, col]).astype(jnp.int32)
    plane, devices = rows * cols, images * rows * cols
    x_tile, g_tile = x_input.reshape(16, 16, 640), out_grad.reshape(16, 16, 640)
    x, act, g = (v.reshape(256, 640) for v in (x_input, pre_act, out_grad))
    q_t = q_prev.transpose(1, 2, 0).reshape(128, 5760)

    rims = call(
        rim_body,
        shape((plane, 32, 640), BF),
        0,
        1 << 20,
        in_specs=[small, whole, whole],
    )(place, x_tile, g_tile)
    got = exchange(rims, PLANE)

    full = lambda *dims: pl.BlockSpec(dims, lambda t: (0,) * len(dims))
    slices, q_one, y_two = call(
        prepare_body,
        (shape((8, 160, 256), BF), shape((128, 5760), BF), shape((9, 128, 256), BF)),
        2 * 1152 * 640 * 256,
        8 << 20,
        grid=(9,),
        in_specs=[full(256, 640), full(256, 640), pl.BlockSpec((128, 640), lambda t: (0, t))],
        out_specs=(
            full(8, 160, 256),
            pl.BlockSpec((128, 640), lambda t: (0, t)),
            pl.BlockSpec((1, 128, 256), lambda t: (t, 0, 0)),
        ),
        scratch_shapes=[pltpu.VMEM((256, 640), BF)],
    )(x, act, q_t)
    slices = exchange(slices, PLANE)

    each = 2 * 64 // devices if 128 % devices == 0 and devices >= 16 else 8
    parts = 128 // each
    pre_grad, p_part = call(
        power_body,
        (shape((256, 640), BF), shape((parts, each, 640), F32)),
        2 * 256 * 5760 * 1100,
        12 << 20,
        grid=(9,),
        in_specs=[
            full(256, 640),
            full(256, 640),
            full(plane, 32, 640),
            full(3, 288, 256 + 32 * cols),
            full(256, 640),
            pl.BlockSpec((128, 640), lambda t: (0, t)),
            pl.BlockSpec((1, 128, 256), lambda t: (t, 0, 0)),
            pl.BlockSpec((1, 1, 640, 640), lambda t: (t // 3, t % 3, 0, 0)),
        ],
        out_specs=(full(256, 640), full(parts, each, 640)),
        scratch_shapes=[
            pltpu.VMEM((3, 288, 640), BF),
            pltpu.VMEM((3, 288, 640), BF),
            pltpu.VMEM((256, 640), F32),
            pltpu.VMEM((256, 128), F32),
            pltpu.VMEM((128, 640), F32),
        ],
    )(x, g, got, rim_pick(row, col, cols), act, q_one, y_two, conv_weight)

    if parts == devices:
        p_got = exchange(p_part, ALL)
        p_got = call(sum_body, shape((parts, each, 640), F32), 0, 1 << 20)(p_got)
        p_all = exchange(p_got, ALL)
    else:
        p_all = lax.psum(p_part, ALL)

    w_own, p_t = call(
        project_body,
        (shape((8, 256, 128), BF), shape((128, 640), F32)),
        2 * 512 * 640 * 128,
        2 << 20,
    )(p_all, pre_grad, g)
    w_all = exchange(w_own, PLANE)
    inverse, basis = call(
        factor_body,
        (shape((2, 64, 64), F32), shape((2, 64, 640), F32)),
        1 << 30,
        1 << 20,
    )(p_t)
    count = 640 // images
    basis_out = lax.dynamic_slice_in_dim(basis, z * count, count, 2).transpose(2, 0, 1)

    sums = call(
        taps_body,
        shape((4, 384, 128), BF),
        2 * 160 * 2048 * 1152,
        2 << 20,
        scratch_shapes=[pltpu.VMEM((34, 4, 16, 384), BF), pltpu.VMEM((1472, 128), F32)],
    )(w_all, slices)

    if images == 4:
        sums = exchange(sums, ("dp",))
        mine = call(
            rotate_body,
            shape((plane, 64, 384), BF),
            1 << 24,
            1 << 20,
            in_specs=[small, whole, whole],
        )(place, sums, inverse)
        every = exchange(mine, PLANE)
        q_out = call(place_body, shape((2, 64, 1440), F32), 0, 1 << 20)(every)
        q_out = q_out.transpose(2, 0, 1)
    else:
        sums = sums[:, :360, :64].astype(F32) + sums[:, :360, 64:].astype(F32)
        sums = lax.psum(sums, "dp")
        mine = jnp.einsum("sr,cir->csi", inverse[row], sums, precision=lax.Precision.HIGHEST)
        every = lax.all_gather(mine, PLANE).reshape(rows, cols, 4, 64, 9, 40)
        every = every.transpose(2, 4, 1, 5, 0, 3).reshape(5760, 2, 64)
        count = 5760 // images
        q_out = lax.dynamic_slice_in_dim(every, z * count, count, 0)
    return basis_out, q_out


def solution(mesh):
    tiles = P("dp", "row", "col", None)
    return jax.shard_map(
        on_device,
        mesh=mesh,
        in_specs=(tiles, tiles, tiles, P(), P()),
        out_specs=(P("dp", None, None), P("dp", None, None)),
        check_vma=False,
    )
```

```python
import jax
import jax.numpy as jnp
from jax import lax
from jax.experimental import pallas as pl
from jax.experimental.pallas import tpu as pltpu
from jax.sharding import PartitionSpec as P

PLANE = ("row", "col")
ALL = ("dp", "row", "col")
BF = jnp.bfloat16
F32 = jnp.float32
NN = ((1,), (0,))
NT = ((1,), (1,))
TN = ((0,), (0,))
MIB = 1024 * 1024


def dot(left, right, dims, precision=None):
    return lax.dot_general(
        left, right, (dims, ((), ())), precision=precision, preferred_element_type=F32
    )


def call(body, out, flops, moved, vmem=40, **extra):
    return pl.pallas_call(
        body,
        out_shape=out,
        cost_estimate=pl.CostEstimate(flops=flops, bytes_accessed=moved, transcendentals=0),
        compiler_params=pltpu.CompilerParams(vmem_limit_bytes=vmem * MIB),
        **extra,
    )


def exchange(chunks, axes):
    return lax.all_to_all(chunks, axes, 0, 0, tiled=True)


def stacked_halves(value):
    high = value.astype(BF)
    return jnp.concatenate([high, (value - high.astype(F32)).astype(BF)], axis=0)


def paired_halves(value):
    total = value + pltpu.roll(value, 64, 1)
    high = total.astype(BF).astype(F32)
    lane = lax.broadcasted_iota(jnp.int32, value.shape, 1)
    return jnp.where(lane < 64, high, total - high)


def rim_body(place, x_ref, g_ref, out_ref):
    row, col = place[1], place[2]
    cols = out_ref.shape[0] // 2
    line = lax.broadcasted_iota(jnp.int32, (48, 256), 0)
    lane = lax.broadcasted_iota(jnp.int32, (48, 256), 1)
    ends = jnp.where(line < 32, 16 * (line % 16) + 15 * (line // 16), 240 * (1 - row) + line - 32)
    pick = jnp.where(lane == ends, 1.0, 0.0).astype(BF)
    for i, ref in enumerate((x_ref, g_ref)):
        rims = dot(pick, ref[...], NN)
        first, last, edge = rims[:16], rims[16:32], rims[32:]
        span = slice(16 * i, 16 * i + 16)
        for r in range(2):
            for c in range(cols):
                along = jnp.where(c > col, last, first)
                out_ref[r * cols + c, span] = jnp.where(row == r, along, edge).astype(BF)


def rim_pick(row, col, cols):
    shape = (3, 18, 16)
    s, y, x = (lax.broadcasted_iota(jnp.int32, shape, i) for i in range(3))
    y, x = y - 1, x + s - 1
    up = jnp.where(y < 0, -1, jnp.where(y > 15, 1, 0))
    side = jnp.where(x < 0, -1, jnp.where(x > 15, 1, 0))
    there_r, there_c = row + up, col + side
    inside = (there_r >= 0) & (there_r < 2) & (there_c >= 0) & (there_c < cols)
    cell = jnp.where(up != 0, x - 16 * side, y)
    got = 256 + (there_r * cols + there_c) * 16 + cell
    index = jnp.where((up == 0) & (side == 0), 16 * y + x, got)
    index = jnp.where(inside, index, -1).reshape(3, 288, 1)
    width = 256 + 32 * cols
    return (index == lax.broadcasted_iota(jnp.int32, (3, 288, width), 2)).astype(BF)


def turn_body(x_ref, act_ref, slices_ref, hidden_ref):
    act = act_ref[...].astype(F32)
    hidden = (act / (1.0 + jnp.exp(-act))).astype(BF)
    hidden_ref[...] = hidden
    for layer, value in enumerate((x_ref[...], hidden)):
        turned = value.astype(F32).T
        for k in range(4):
            pieces = [turned[160 * j + 40 * k : 160 * j + 40 * k + 40] for j in range(4)]
            slices_ref[4 * layer + k] = jnp.concatenate(pieces, axis=0).astype(BF)


def prepare_body(hidden_ref, q_ref, q_one_ref, y_ref):
    q = q_ref[...]
    q_one_ref[...] = stacked_halves(q[:64])
    y = dot(stacked_halves(q[64:]), hidden_ref[...], NT)
    y_ref[0] = stacked_halves(y[:64] + y[64:])


def power_body(
    x_ref, g_ref, got_ref, pick_ref, act_ref, q_ref, y_ref, w_ref,
    grad_ref, p_ref, x_win, g_win, back, z_sum, p_sum,
):
    t = pl.program_id(0)

    @pl.when(t == 0)
    def _():
        for i, (ref, win) in enumerate(((x_ref, x_win), (g_ref, g_win))):
            cells = got_ref[:, 16 * i : 16 * i + 16, :].reshape(-1, 640)
            cells = jnp.concatenate([ref[...], cells], axis=0)
            for s in range(3):
                win[s] = dot(pick_ref[s], cells, NN).astype(BF)
        back[...] = jnp.zeros_like(back)
        z_sum[...] = jnp.zeros_like(z_sum)
        p_sum[...] = jnp.zeros_like(p_sum)

    a, b = t // 3, t % 3
    grads = g_win[2 - b, pl.ds(pl.multiple_of(16 * (2 - a), 16), 256), :]
    inputs = x_win[b, pl.ds(pl.multiple_of(16 * a, 16), 256), :]
    back[...] += dot(grads, w_ref[0, 0], NT)
    z_sum[...] += dot(inputs, q_ref[...], NT)
    p_sum[...] += dot(y_ref[0], grads, NN)

    @pl.when(t == 8)
    def _():
        act = act_ref[...].astype(F32)
        sigma = 1.0 / (1.0 + jnp.exp(-act))
        grad = (back[...] * (sigma * (1.0 + act * (1.0 - sigma)))).astype(BF)
        grad_ref[...] = grad
        one = dot(paired_halves(z_sum[...]).astype(BF), grad, TN)
        two = p_sum[...]
        each = p_ref.shape[1]
        for layer, value in enumerate((one, two)):
            value = value[:64] + value[64:]
            for i in range(64 // each):
                p_ref[layer * (64 // each) + i] = value[i * each : (i + 1) * each]


def sum_body(got_ref, out_ref):
    total = jnp.sum(got_ref[...], axis=0)
    for i in range(out_ref.shape[0]):
        out_ref[i] = total


def project_body(got_ref, grad_ref, g_ref, w_ref, p_ref):
    each = got_ref.shape[1]
    for i in range(16):
        rows = [got_ref[i * (8 // each) + j] for j in range(8 // each)]
        p_ref[8 * i : 8 * i + 8, :] = jnp.concatenate(rows, axis=0)
    for layer, ref in enumerate((grad_ref, g_ref)):
        factor = stacked_halves(p_ref[64 * layer : 64 * layer + 64, :])
        out = paired_halves(dot(ref[...], factor, NT)).astype(BF)
        for k in range(4):
            w_ref[4 * layer + k] = out


def factor_body(p_ref, inverse_ref, basis_ref):
    high = lax.Precision.HIGHEST
    line = lax.broadcasted_iota(jnp.int32, (64, 128), 0)
    lane = lax.broadcasted_iota(jnp.int32, (64, 128), 1)
    unit = jnp.where(lane == line + 64, 1.0, 0.0)
    tables = []
    for layer in range(2):
        p = p_ref[64 * layer : 64 * layer + 64, :]
        gram = dot(p, p, NT, high)
        tables.append(jnp.concatenate([gram, unit[:, 64:]], axis=1))
    for k in range(64):
        for layer in range(2):
            table = tables[layer]
            pivot_row = table[k : k + 1, :]
            scaled = pivot_row / pivot_row[:, k : k + 1]
            column = jnp.where(line[:, :1] > k, table[:, k : k + 1], 0.0)
            tables[layer] = table - column * scaled
    for layer in range(2):
        table = tables[layer]
        pivots = jnp.sum(jnp.where(line == lane, table, 0.0), axis=1, keepdims=True)
        inverse = table[:, 64:] / jnp.sqrt(pivots)
        inverse_ref[layer] = inverse
        basis_ref[layer] = dot(inverse, p_ref[64 * layer : 64 * layer + 64, :], NN, high)


def taps_body(place, w_ref, x_ref, inverse_ref, out_ref, image, sums):
    zero = jnp.zeros((1, 4, 16, 384), BF)
    image[0:1] = zero
    image[33:34] = zero
    at = lax.broadcasted_iota(jnp.int32, (1024, 128), 0) % 64
    for r in range(2):
        tiles = [w_ref[4 * r + c].astype(F32).reshape(16, 16, 128) for c in range(4)]
        flat = jnp.stack(tiles, axis=1).reshape(1024, 128)
        left = jnp.where(at == 63, 0.0, pltpu.roll(flat, 1023, 0))
        right = jnp.where(at == 0, 0.0, pltpu.roll(flat, 1, 0))
        for i, value in enumerate((left, flat, right)):
            image[1 + 16 * r : 17 + 16 * r, :, :, 128 * i : 128 * i + 128] = value.astype(BF).reshape(
                16, 4, 16, 128
            )
    for a in range(3):
        total = jnp.zeros((160, 384), F32)
        for r in range(2):
            for c in range(4):
                window = image[16 * r + 2 - a : 16 * r + 18 - a, c].reshape(256, 384)
                total = total + dot(x_ref[4 * r + c], window, NN)
        for b in range(3):
            t = 3 * a + b
            value = total[:, 128 * b : 128 * b + 128]
            sums[160 * t : 160 * t + 160, :] = value + pltpu.roll(value, 64, 1)
    sums[1440:1472, :] = jnp.zeros((32, 128), F32)
    inverse = inverse_ref[place[1]]
    for i in range(4):
        part = sums[360 * i : 360 * i + 384, :][:, :64]
        out_ref[i] = dot(inverse, part, NT, lax.Precision.HIGHEST).astype(BF)


def total_body(got_ref, out_ref):
    total = got_ref[0].astype(F32)
    for i in range(1, got_ref.shape[0]):
        total = total + got_ref[i].astype(F32)
    for i in range(out_ref.shape[0]):
        out_ref[i] = total.astype(BF)


def place_body(got_ref, out_ref):
    for layer in range(2):
        for k in range(4):
            value = got_ref[4 * layer + k].astype(F32)
            for j in range(9):
                start = 160 * j + 40 * k
                out_ref[layer, :, start : start + 40] = value[:, 40 * j : 40 * j + 40]


def on_device(x_input, pre_act, out_grad, conv_weight, q_prev):
    shape = jax.ShapeDtypeStruct
    whole = pl.BlockSpec(memory_space=pltpu.VMEM)
    small = pl.BlockSpec(memory_space=pltpu.SMEM)
    images, rows, cols = (lax.axis_size(a) for a in ALL)
    z, row, col = (lax.axis_index(a) for a in ALL)
    place = jnp.stack([z, row, col]).astype(jnp.int32)
    plane, devices = rows * cols, images * rows * cols
    x, act, g = (v.reshape(256, 640) for v in (x_input, pre_act, out_grad))
    q_t = q_prev.transpose(1, 2, 0).reshape(128, 5760)

    rims = call(
        rim_body,
        shape((plane, 32, 640), BF),
        0,
        1 << 20,
        vmem=62,
        in_specs=[small, whole, whole],
    )(place, x, g)
    got = exchange(rims, PLANE)

    full = lambda *dims: pl.BlockSpec(dims, lambda t: (0,) * len(dims))
    slices, hidden = call(
        turn_body, (shape((8, 160, 256), BF), shape((256, 640), BF)), 1 << 28, 2 << 20
    )(x, act)
    slices = exchange(slices, PLANE)
    q_one, y_two = call(
        prepare_body,
        (shape((128, 5760), BF), shape((9, 128, 256), BF)),
        2 * 1152 * 640 * 256,
        8 << 20,
        vmem=62,
        grid=(9,),
        in_specs=[full(256, 640), pl.BlockSpec((128, 640), lambda t: (0, t))],
        out_specs=(
            pl.BlockSpec((128, 640), lambda t: (0, t)),
            pl.BlockSpec((1, 128, 256), lambda t: (t, 0, 0)),
        ),
    )(hidden, q_t)

    each = 2 * 64 // devices if 128 % devices == 0 and devices >= 16 else 8
    parts = 128 // each
    pre_grad, p_part = call(
        power_body,
        (shape((256, 640), BF), shape((parts, each, 640), F32)),
        2 * 256 * 5760 * 1100,
        12 << 20,
        vmem=58,
        grid=(9,),
        in_specs=[
            full(256, 640),
            full(256, 640),
            full(plane, 32, 640),
            full(3, 288, 256 + 32 * cols),
            full(256, 640),
            pl.BlockSpec((128, 640), lambda t: (0, t)),
            pl.BlockSpec((1, 128, 256), lambda t: (t, 0, 0)),
            pl.BlockSpec((1, 1, 640, 640), lambda t: (t // 3, t % 3, 0, 0)),
        ],
        out_specs=(full(256, 640), full(parts, each, 640)),
        scratch_shapes=[
            pltpu.VMEM((3, 288, 640), BF),
            pltpu.VMEM((3, 288, 640), BF),
            pltpu.VMEM((256, 640), F32),
            pltpu.VMEM((256, 128), F32),
            pltpu.VMEM((128, 640), F32),
        ],
    )(x, g, got, rim_pick(row, col, cols), act, q_one, y_two, conv_weight)

    p_part, slices = lax.optimization_barrier((p_part, slices))
    if parts == devices:
        p_got = exchange(p_part, ALL)
        p_got = call(sum_body, shape((parts, each, 640), F32), 0, 1 << 20)(p_got)
        p_all = exchange(p_got, ALL)
    else:
        p_all = lax.psum(p_part, ALL)

    w_own, p_t = call(
        project_body,
        (shape((8, 256, 128), BF), shape((128, 640), F32)),
        2 * 512 * 640 * 128,
        2 << 20,
    )(p_all, pre_grad, g)
    w_all = exchange(w_own, PLANE)
    inverse, basis = call(
        factor_body,
        (shape((2, 64, 64), F32), shape((2, 64, 640), F32)),
        1 << 30,
        1 << 20,
    )(p_t)
    count = 640 // images
    basis_out = lax.dynamic_slice_in_dim(basis, z * count, count, 2).transpose(2, 0, 1)

    sums = call(
        taps_body,
        shape((4, 64, 384), BF),
        2 * 160 * 2048 * 1152,
        2 << 20,
        in_specs=[small, whole, whole, whole],
        scratch_shapes=[pltpu.VMEM((34, 4, 16, 384), BF), pltpu.VMEM((1472, 128), F32)],
    )(place, w_all, slices, inverse)

    if images == 4:
        sums = exchange(sums, ("dp",))
        mine = call(total_body, shape((plane, 64, 384), BF), 0, 1 << 20)(sums)
        every = exchange(mine, PLANE)
        q_out = call(place_body, shape((2, 64, 1440), F32), 0, 1 << 20)(every)
        q_out = q_out.transpose(2, 0, 1)
    else:
        sums = lax.psum(sums[:, :, :360].astype(F32), "dp")
        every = lax.all_gather(sums, PLANE).reshape(rows, cols, 4, 64, 9, 40)
        every = every.transpose(2, 4, 1, 5, 0, 3).reshape(5760, 2, 64)
        count = 5760 // images
        q_out = lax.dynamic_slice_in_dim(every, z * count, count, 0)
    return basis_out, q_out


def solution(mesh):
    tiles = P("dp", "row", "col", None)
    return jax.shard_map(
        on_device,
        mesh=mesh,
        in_specs=(tiles, tiles, tiles, P(), P()),
        out_specs=(P("dp", None, None), P("dp", None, None)),
        check_vma=False,
    )
```

```python
import jax
import jax.numpy as jnp
from jax import lax
from jax.experimental import pallas as pl
from jax.experimental.pallas import tpu as pltpu
from jax.sharding import PartitionSpec as P

PLANE = ("row", "col")
ALL = ("dp", "row", "col")
BF = jnp.bfloat16
F32 = jnp.float32
NN = ((1,), (0,))
NT = ((1,), (1,))
TN = ((0,), (0,))
MIB = 1024 * 1024


def dot(left, right, dims, precision=None):
    return lax.dot_general(
        left, right, (dims, ((), ())), precision=precision, preferred_element_type=F32
    )


def call(body, out, flops, moved, vmem=40, **extra):
    return pl.pallas_call(
        body,
        out_shape=out,
        cost_estimate=pl.CostEstimate(flops=flops, bytes_accessed=moved, transcendentals=0),
        compiler_params=pltpu.CompilerParams(vmem_limit_bytes=vmem * MIB),
        **extra,
    )


def exchange(chunks, axes):
    return lax.all_to_all(chunks, axes, 0, 0, tiled=True)


def stacked_halves(value):
    high = value.astype(BF)
    return jnp.concatenate([high, (value - high.astype(F32)).astype(BF)], axis=0)


def paired_halves(value):
    total = value + pltpu.roll(value, 64, 1)
    high = total.astype(BF).astype(F32)
    lane = lax.broadcasted_iota(jnp.int32, value.shape, 1)
    return jnp.where(lane < 64, high, total - high)


def fetch(pairs, sems):
    copies = [pltpu.make_async_copy(src, dst, sems.at[i]) for i, (src, dst) in enumerate(pairs)]
    for copy in copies:
        copy.start()
    return copies


def outgoing_body(x_hbm, g_hbm, act_hbm, out_ref, hidden_ref, x_ref, g_ref, act_ref, sems):
    copies = fetch(((x_hbm, x_ref), (g_hbm, g_ref), (act_hbm, act_ref)), sems)
    row, col = lax.axis_index("row"), lax.axis_index("col")
    cols = out_ref.shape[0] // 2
    line = lax.broadcasted_iota(jnp.int32, (48, 256), 0)
    lane = lax.broadcasted_iota(jnp.int32, (48, 256), 1)
    ends = jnp.where(line < 32, 16 * (line % 16) + 15 * (line // 16), 240 * (1 - row) + line - 32)
    pick = jnp.where(lane == ends, 1.0, 0.0).astype(BF)
    for i, ref in enumerate((x_ref, g_ref)):
        copies[i].wait()
        rims = dot(pick, ref[...], NN)
        first, last, edge = rims[:16], rims[16:32], rims[32:]
        span = slice(16 * i, 16 * i + 16)
        for r in range(2):
            for c in range(cols):
                along = jnp.where(c > col, last, first)
                out_ref[r * cols + c, span] = jnp.where(row == r, along, edge).astype(BF)
    copies[2].wait()
    act = act_ref[...].astype(F32)
    hidden = (act / (1.0 + jnp.exp(-act))).astype(BF)
    hidden_ref[...] = hidden
    for layer, value in enumerate((x_ref[...], hidden)):
        turned = value.astype(F32).T
        for k in range(4):
            pieces = [turned[160 * j + 40 * k : 160 * j + 40 * k + 40] for j in range(4)]
            part = jnp.concatenate(pieces, axis=0).astype(BF)
            part = jnp.concatenate([part[:, :128], part[:, 128:]], axis=0)
            for j in range(5):
                out_ref[4 * layer + k, 32:96, 128 * j : 128 * j + 128] = part[64 * j : 64 * j + 64]


def slice_of(got_ref, d):
    part = [got_ref[d, 32:96, 128 * j : 128 * j + 128] for j in range(5)]
    part = jnp.concatenate(part, axis=0)
    return jnp.concatenate([part[:160], part[160:]], axis=1)


def rim_pick(row, col, cols):
    shape = (3, 18, 16)
    s, y, x = (lax.broadcasted_iota(jnp.int32, shape, i) for i in range(3))
    y, x = y - 1, x + s - 1
    up = jnp.where(y < 0, -1, jnp.where(y > 15, 1, 0))
    side = jnp.where(x < 0, -1, jnp.where(x > 15, 1, 0))
    there_r, there_c = row + up, col + side
    inside = (there_r >= 0) & (there_r < 2) & (there_c >= 0) & (there_c < cols)
    cell = jnp.where(up != 0, x - 16 * side, y)
    got = 256 + (there_r * cols + there_c) * 16 + cell
    index = jnp.where((up == 0) & (side == 0), 16 * y + x, got)
    index = jnp.where(inside, index, -1).reshape(3, 288, 1)
    width = 256 + 32 * cols
    return (index == lax.broadcasted_iota(jnp.int32, (3, 288, width), 2)).astype(BF)


def prepare_body(hidden_ref, act_ref, q_hbm, q_one_ref, y_ref, slope_ref, q_all, sems):
    copies = fetch([(q_hbm.at[:, 640 * t : 640 * t + 640], q_all.at[t]) for t in range(9)], sems)
    act = act_ref[...].astype(F32)
    sigma = 1.0 / (1.0 + jnp.exp(-act))
    slope_ref[...] = sigma * (1.0 + act * (1.0 - sigma))
    for t in range(9):
        copies[t].wait()
        q = q_all[t]
        q_one_ref[t] = stacked_halves(q[:64])
        y = dot(stacked_halves(q[64:]), hidden_ref[...], NT)
        y_ref[t] = stacked_halves(y[:64] + y[64:])


def power_body(
    x_ref, g_ref, got_ref, pick_ref, slope_ref, q_ref, y_ref, w_hbm,
    grad_ref, p_ref, x_win, g_win, back, z_sum, p_sum, w_all, sems,
):
    copies = fetch([(w_hbm.at[t // 3, t % 3], w_all.at[t]) for t in range(9)], sems)
    for i, (ref, win) in enumerate(((g_ref, g_win), (x_ref, x_win))):
        cells = got_ref[:, 16 - 16 * i : 32 - 16 * i, :].reshape(-1, 640)
        cells = jnp.concatenate([ref[...], cells], axis=0)
        for s in range(3):
            win[s] = dot(pick_ref[s], cells, NN).astype(BF)
    for t in range(9):
        a, b = t // 3, t % 3
        grads = g_win[2 - b, 16 * (2 - a) : 16 * (2 - a) + 256, :]
        inputs = x_win[b, 16 * a : 16 * a + 256, :]
        copies[t].wait()
        terms = (
            (back, dot(grads, w_all[t], NT)),
            (z_sum, dot(inputs, q_ref[t], NT)),
            (p_sum, dot(y_ref[t], grads, NN)),
        )
        for ref, term in terms:
            ref[...] = term if t == 0 else ref[...] + term
    grad = (back[...] * slope_ref[...]).astype(BF)
    grad_ref[...] = grad
    one = dot(paired_halves(z_sum[...]).astype(BF), grad, TN)
    each = p_ref.shape[1]
    for layer, value in enumerate((one, p_sum[...])):
        value = value[:64] + value[64:]
        for i in range(64 // each):
            p_ref[layer * (64 // each) + i] = value[i * each : (i + 1) * each]


def sum_body(got_ref, out_ref):
    total = jnp.sum(got_ref[...], axis=0)
    for i in range(out_ref.shape[0]):
        out_ref[i] = total


def project_body(got_ref, grad_ref, g_ref, w_ref, p_ref):
    each = got_ref.shape[1]
    for i in range(16):
        rows = [got_ref[i * (8 // each) + j] for j in range(8 // each)]
        p_ref[8 * i : 8 * i + 8, :] = jnp.concatenate(rows, axis=0)
    for layer, ref in enumerate((grad_ref, g_ref)):
        factor = stacked_halves(p_ref[64 * layer : 64 * layer + 64, :])
        out = paired_halves(dot(ref[...], factor, NT)).astype(BF)
        for k in range(4):
            w_ref[4 * layer + k] = out


def factor_body(p_ref, inverse_ref, basis_ref):
    high = lax.Precision.HIGHEST
    line = lax.broadcasted_iota(jnp.int32, (64, 128), 0)
    lane = lax.broadcasted_iota(jnp.int32, (64, 128), 1)
    unit = jnp.where(lane == line + 64, 1.0, 0.0)
    tables = []
    for layer in range(2):
        p = p_ref[64 * layer : 64 * layer + 64, :]
        gram = dot(p, p, NT, high)
        tables.append(jnp.concatenate([gram, unit[:, 64:]], axis=1))
    for k in range(64):
        for layer in range(2):
            table = tables[layer]
            pivot_row = table[k : k + 1, :]
            scaled = pivot_row / pivot_row[:, k : k + 1]
            column = jnp.where(line[:, :1] > k, table[:, k : k + 1], 0.0)
            tables[layer] = table - column * scaled
    for layer in range(2):
        table = tables[layer]
        pivots = jnp.sum(jnp.where(line == lane, table, 0.0), axis=1, keepdims=True)
        inverse = table[:, 64:] / jnp.sqrt(pivots)
        inverse_ref[layer] = inverse
        basis_ref[layer] = dot(inverse, p_ref[64 * layer : 64 * layer + 64, :], NN, high)


def taps_body(w_ref, x_ref, inverse_ref, out_ref, image, sums):
    zero = jnp.zeros((1, 4, 16, 384), BF)
    image[0:1] = zero
    image[33:34] = zero
    at = lax.broadcasted_iota(jnp.int32, (1024, 128), 0) % 64
    for r in range(2):
        tiles = [w_ref[4 * r + c].astype(F32).reshape(16, 16, 128) for c in range(4)]
        flat = jnp.stack(tiles, axis=1).reshape(1024, 128)
        left = jnp.where(at == 63, 0.0, pltpu.roll(flat, 1023, 0))
        right = jnp.where(at == 0, 0.0, pltpu.roll(flat, 1, 0))
        for i, value in enumerate((left, flat, right)):
            image[1 + 16 * r : 17 + 16 * r, :, :, 128 * i : 128 * i + 128] = value.astype(BF).reshape(
                16, 4, 16, 128
            )
    slices = [slice_of(x_ref, d) for d in range(8)]
    for a in range(3):
        total = jnp.zeros((160, 384), F32)
        for r in range(2):
            for c in range(4):
                window = image[16 * r + 2 - a : 16 * r + 18 - a, c].reshape(256, 384)
                total = total + dot(slices[4 * r + c], window, NN)
        for b in range(3):
            t = 3 * a + b
            value = total[:, 128 * b : 128 * b + 128]
            sums[160 * t : 160 * t + 160, :] = value + pltpu.roll(value, 64, 1)
    sums[1440:1472, :] = jnp.zeros((32, 128), F32)
    inverse = inverse_ref[lax.axis_index("row")]
    for i in range(4):
        part = sums[360 * i : 360 * i + 384, :][:, :64]
        out_ref[i] = dot(inverse, part, NT, lax.Precision.HIGHEST).astype(BF)


def total_body(got_ref, out_ref):
    total = got_ref[0].astype(F32)
    for i in range(1, got_ref.shape[0]):
        total = total + got_ref[i].astype(F32)
    for i in range(out_ref.shape[0]):
        out_ref[i] = total.astype(BF)


def place_body(got_ref, out_ref):
    for layer in range(2):
        for k in range(4):
            value = got_ref[4 * layer + k].astype(F32)
            for j in range(9):
                start = 160 * j + 40 * k
                out_ref[layer, :, start : start + 40] = value[:, 40 * j : 40 * j + 40]


def on_device(x_input, pre_act, out_grad, conv_weight, q_prev):
    shape = jax.ShapeDtypeStruct
    whole = pl.BlockSpec(memory_space=pltpu.VMEM)
    far = pl.BlockSpec(memory_space=pltpu.HBM)
    images, rows, cols = (lax.axis_size(a) for a in ALL)
    z, row, col = (lax.axis_index(a) for a in ALL)
    plane, devices = rows * cols, images * rows * cols
    x, act, g = (v.reshape(256, 640) for v in (x_input, pre_act, out_grad))
    q_t = q_prev.transpose(1, 2, 0).reshape(128, 5760)

    sems = pltpu.SemaphoreType.DMA
    send, hidden = call(
        outgoing_body,
        (shape((plane, 96, 640), BF), shape((256, 640), BF)),
        1 << 28,
        3 << 20,
        in_specs=[far] * 3,
        scratch_shapes=[pltpu.VMEM((256, 640), BF)] * 3 + [sems((3,))],
    )(x, g, act)
    got = exchange(send, PLANE)
    q_one, y_two, slope = call(
        prepare_body,
        (shape((9, 128, 640), BF), shape((9, 128, 256), BF), shape((256, 640), F32)),
        2 * 1152 * 640 * 256,
        8 << 20,
        in_specs=[whole, whole, far],
        scratch_shapes=[pltpu.VMEM((9, 128, 640), F32), sems((9,))],
    )(hidden, act, q_t)

    each = 2 * 64 // devices if 128 % devices == 0 and devices >= 16 else 8
    parts = 128 // each
    pre_grad, p_part = call(
        power_body,
        (shape((256, 640), BF), shape((parts, each, 640), F32)),
        2 * 256 * 5760 * 1100,
        12 << 20,
        in_specs=[whole] * 7 + [far],
        scratch_shapes=[
            pltpu.VMEM((3, 288, 640), BF),
            pltpu.VMEM((3, 288, 640), BF),
            pltpu.VMEM((256, 640), F32),
            pltpu.VMEM((256, 128), F32),
            pltpu.VMEM((128, 640), F32),
            pltpu.VMEM((9, 640, 640), BF),
            sems((9,)),
        ],
    )(x, g, got, rim_pick(row, col, cols), slope, q_one, y_two, conv_weight)

    if parts == devices:
        p_got = exchange(p_part, ALL)
        p_got = call(sum_body, shape((parts, each, 640), F32), 0, 1 << 20)(p_got)
        p_all = exchange(p_got, ALL)
    else:
        p_all = lax.psum(p_part, ALL)

    w_own, p_t = call(
        project_body,
        (shape((8, 256, 128), BF), shape((128, 640), F32)),
        2 * 512 * 640 * 128,
        2 << 20,
    )(p_all, pre_grad, g)
    w_all = exchange(w_own, PLANE)
    inverse, basis = call(
        factor_body,
        (shape((2, 64, 64), F32), shape((2, 64, 640), F32)),
        1 << 30,
        1 << 20,
    )(p_t)
    count = 640 // images
    basis_out = lax.dynamic_slice_in_dim(basis, z * count, count, 2).transpose(2, 0, 1)

    sums = call(
        taps_body,
        shape((4, 64, 384), BF),
        2 * 160 * 2048 * 1152,
        2 << 20,
        scratch_shapes=[pltpu.VMEM((34, 4, 16, 384), BF), pltpu.VMEM((1472, 128), F32)],
    )(w_all, got, inverse)

    if images == 4:
        sums = exchange(sums, ("dp",))
        mine = call(total_body, shape((plane, 64, 384), BF), 0, 1 << 20)(sums)
        every = exchange(mine, PLANE)
        q_out = call(place_body, shape((2, 64, 1440), F32), 0, 1 << 20)(every)
        q_out = q_out.transpose(2, 0, 1)
    else:
        sums = lax.psum(sums[:, :, :360].astype(F32), "dp")
        every = lax.all_gather(sums, PLANE).reshape(rows, cols, 4, 64, 9, 40)
        every = every.transpose(2, 4, 1, 5, 0, 3).reshape(5760, 2, 64)
        count = 5760 // images
        q_out = lax.dynamic_slice_in_dim(every, z * count, count, 0)
    return basis_out, q_out


def solution(mesh):
    tiles = P("dp", "row", "col", None)
    return jax.shard_map(
        on_device,
        mesh=mesh,
        in_specs=(tiles, tiles, tiles, P(), P()),
        out_specs=(P("dp", None, None), P("dp", None, None)),
        check_vma=False,
    )
```

```python
import jax
import jax.numpy as jnp
from jax import lax
from jax.experimental import pallas as pl
from jax.experimental.pallas import tpu as pltpu
from jax.sharding import PartitionSpec as P

PLANE = ("row", "col")
ALL = ("dp", "row", "col")
BF = jnp.bfloat16
F32 = jnp.float32
NN = ((1,), (0,))
NT = ((1,), (1,))
TN = ((0,), (0,))
MIB = 1024 * 1024


def dot(left, right, dims, precision=None):
    return lax.dot_general(
        left, right, (dims, ((), ())), precision=precision, preferred_element_type=F32
    )


def call(body, out, flops, moved, vmem=40, **extra):
    return pl.pallas_call(
        body,
        out_shape=out,
        cost_estimate=pl.CostEstimate(flops=flops, bytes_accessed=moved, transcendentals=0),
        compiler_params=pltpu.CompilerParams(vmem_limit_bytes=vmem * MIB),
        **extra,
    )


def exchange(chunks, axes):
    return lax.all_to_all(chunks, axes, 0, 0, tiled=True)


def stacked_halves(value):
    high = value.astype(BF)
    return jnp.concatenate([high, (value - high.astype(F32)).astype(BF)], axis=0)


def paired_halves(value):
    total = value + pltpu.roll(value, 64, 1)
    high = total.astype(BF).astype(F32)
    lane = lax.broadcasted_iota(jnp.int32, value.shape, 1)
    return jnp.where(lane < 64, high, total - high)


def fetch(pairs, sems):
    copies = [pltpu.make_async_copy(src, dst, sems.at[i]) for i, (src, dst) in enumerate(pairs)]
    for copy in copies:
        copy.start()
    return copies


def rim_body(x_hbm, g_hbm, out_ref, x_ref, g_ref, sems):
    copies = fetch(((x_hbm, x_ref), (g_hbm, g_ref)), sems)
    row, col = lax.axis_index("row"), lax.axis_index("col")
    cols = out_ref.shape[0] // 2
    line = lax.broadcasted_iota(jnp.int32, (48, 256), 0)
    lane = lax.broadcasted_iota(jnp.int32, (48, 256), 1)
    ends = jnp.where(line < 32, 16 * (line % 16) + 15 * (line // 16), 240 * (1 - row) + line - 32)
    pick = jnp.where(lane == ends, 1.0, 0.0).astype(BF)
    for i, ref in enumerate((x_ref, g_ref)):
        copies[i].wait()
        rims = dot(pick, ref[...], NN)
        first, last, edge = rims[:16], rims[16:32], rims[32:]
        span = slice(16 * i, 16 * i + 16)
        for r in range(2):
            for c in range(cols):
                along = jnp.where(c > col, last, first)
                out_ref[r * cols + c, span] = jnp.where(row == r, along, edge).astype(BF)


def rim_pick(row, col, cols):
    shape = (3, 18, 16)
    s, y, x = (lax.broadcasted_iota(jnp.int32, shape, i) for i in range(3))
    y, x = y - 1, x + s - 1
    up = jnp.where(y < 0, -1, jnp.where(y > 15, 1, 0))
    side = jnp.where(x < 0, -1, jnp.where(x > 15, 1, 0))
    there_r, there_c = row + up, col + side
    inside = (there_r >= 0) & (there_r < 2) & (there_c >= 0) & (there_c < cols)
    cell = jnp.where(up != 0, x - 16 * side, y)
    got = 256 + (there_r * cols + there_c) * 16 + cell
    index = jnp.where((up == 0) & (side == 0), 16 * y + x, got)
    index = jnp.where(inside, index, -1).reshape(3, 288, 1)
    width = 256 + 32 * cols
    return (index == lax.broadcasted_iota(jnp.int32, (3, 288, width), 2)).astype(BF)


def prepare_body(
    x_hbm, act_hbm, q_hbm, slices_ref, q_one_ref, y_ref, slope_ref, x_ref, act_ref, q_all, sems
):
    pairs = [(x_hbm, x_ref), (act_hbm, act_ref)]
    pairs += [(q_hbm.at[:, 640 * t : 640 * t + 640], q_all.at[t]) for t in range(9)]
    copies = fetch(pairs, sems)
    copies[0].wait()
    copies[1].wait()
    act = act_ref[...].astype(F32)
    sigma = 1.0 / (1.0 + jnp.exp(-act))
    hidden = (act * sigma).astype(BF)
    slope_ref[...] = sigma * (1.0 + act * (1.0 - sigma))
    for layer, value in enumerate((x_ref[...], hidden)):
        turned = value.astype(F32).T
        for k in range(4):
            pieces = [turned[160 * j + 40 * k : 160 * j + 40 * k + 40] for j in range(4)]
            slices_ref[4 * layer + k] = jnp.concatenate(pieces, axis=0).astype(BF)
    for t in range(9):
        copies[2 + t].wait()
        q = q_all[t]
        q_one_ref[t] = stacked_halves(q[:64])
        y = dot(stacked_halves(q[64:]), hidden, NT)
        y_ref[t] = stacked_halves(y[:64] + y[64:])


def power_body(
    x_hbm, g_hbm, got_hbm, pick_hbm, slope_hbm, q_hbm, y_hbm, w_hbm,
    grad_ref, p_ref,
    x_ref, g_ref, got_ref, pick_ref, slope_ref, q_ref, y_ref, w_all,
    x_win, g_win, back, z_sum, p_sum, sems,
):
    pairs = [(got_hbm, got_ref), (g_hbm, g_ref), (pick_hbm, pick_ref), (x_hbm, x_ref)]
    pairs += [(q_hbm, q_ref), (y_hbm, y_ref), (slope_hbm, slope_ref)]
    pairs += [(w_hbm.at[t // 3, t % 3], w_all.at[t]) for t in range(9)]
    copies = fetch(pairs, sems)
    for i in range(4):
        copies[i].wait()
    for i, (ref, win) in enumerate(((g_ref, g_win), (x_ref, x_win))):
        cells = got_ref[:, 16 - 16 * i : 32 - 16 * i, :].reshape(-1, 640)
        cells = jnp.concatenate([ref[...], cells], axis=0)
        for s in range(3):
            win[s] = dot(pick_ref[s], cells, NN).astype(BF)
    copies[4].wait()
    copies[5].wait()
    for t in range(9):
        a, b = t // 3, t % 3
        grads = g_win[2 - b, 16 * (2 - a) : 16 * (2 - a) + 256, :]
        inputs = x_win[b, 16 * a : 16 * a + 256, :]
        copies[7 + t].wait()
        terms = (
            (back, dot(grads, w_all[t], NT)),
            (z_sum, dot(inputs, q_ref[t], NT)),
            (p_sum, dot(y_ref[t], grads, NN)),
        )
        for ref, term in terms:
            ref[...] = term if t == 0 else ref[...] + term
    copies[6].wait()
    grad = (back[...] * slope_ref[...]).astype(BF)
    grad_ref[...] = grad
    one = dot(paired_halves(z_sum[...]).astype(BF), grad, TN)
    each = p_ref.shape[1]
    for layer, value in enumerate((one, p_sum[...])):
        value = value[:64] + value[64:]
        for i in range(64 // each):
            p_ref[layer * (64 // each) + i] = value[i * each : (i + 1) * each]


def sum_body(got_ref, out_ref):
    total = jnp.sum(got_ref[...], axis=0)
    for i in range(out_ref.shape[0]):
        out_ref[i] = total


def project_body(got_ref, grad_ref, g_ref, w_ref, p_ref):
    each = got_ref.shape[1]
    for i in range(16):
        rows = [got_ref[i * (8 // each) + j] for j in range(8 // each)]
        p_ref[8 * i : 8 * i + 8, :] = jnp.concatenate(rows, axis=0)
    for layer, ref in enumerate((grad_ref, g_ref)):
        factor = stacked_halves(p_ref[64 * layer : 64 * layer + 64, :])
        out = paired_halves(dot(ref[...], factor, NT)).astype(BF)
        for k in range(4):
            w_ref[4 * layer + k] = out


def factor_body(p_ref, inverse_ref, basis_ref):
    high = lax.Precision.HIGHEST
    line = lax.broadcasted_iota(jnp.int32, (64, 128), 0)
    lane = lax.broadcasted_iota(jnp.int32, (64, 128), 1)
    unit = jnp.where(lane == line + 64, 1.0, 0.0)
    tables = []
    for layer in range(2):
        p = p_ref[64 * layer : 64 * layer + 64, :]
        gram = dot(p, p, NT, high)
        tables.append(jnp.concatenate([gram, unit[:, 64:]], axis=1))
    for k in range(64):
        for layer in range(2):
            table = tables[layer]
            pivot_row = table[k : k + 1, :]
            scaled = pivot_row / pivot_row[:, k : k + 1]
            column = jnp.where(line[:, :1] > k, table[:, k : k + 1], 0.0)
            tables[layer] = table - column * scaled
    for layer in range(2):
        table = tables[layer]
        pivots = jnp.sum(jnp.where(line == lane, table, 0.0), axis=1, keepdims=True)
        inverse = table[:, 64:] / jnp.sqrt(pivots)
        inverse_ref[layer] = inverse
        basis_ref[layer] = dot(inverse, p_ref[64 * layer : 64 * layer + 64, :], NN, high)


def taps_body(w_ref, x_ref, inverse_ref, out_ref, image, sums):
    zero = jnp.zeros((1, 4, 16, 384), BF)
    image[0:1] = zero
    image[33:34] = zero
    at = lax.broadcasted_iota(jnp.int32, (1024, 128), 0) % 64
    for r in range(2):
        tiles = [w_ref[4 * r + c].astype(F32).reshape(16, 16, 128) for c in range(4)]
        flat = jnp.stack(tiles, axis=1).reshape(1024, 128)
        left = jnp.where(at == 63, 0.0, pltpu.roll(flat, 1023, 0))
        right = jnp.where(at == 0, 0.0, pltpu.roll(flat, 1, 0))
        for i, value in enumerate((left, flat, right)):
            image[1 + 16 * r : 17 + 16 * r, :, :, 128 * i : 128 * i + 128] = value.astype(BF).reshape(
                16, 4, 16, 128
            )
    for a in range(3):
        total = jnp.zeros((160, 384), F32)
        for r in range(2):
            for c in range(4):
                window = image[16 * r + 2 - a : 16 * r + 18 - a, c].reshape(256, 384)
                total = total + dot(x_ref[4 * r + c], window, NN)
        for b in range(3):
            t = 3 * a + b
            value = total[:, 128 * b : 128 * b + 128]
            sums[160 * t : 160 * t + 160, :] = value + pltpu.roll(value, 64, 1)
    sums[1440:1472, :] = jnp.zeros((32, 128), F32)
    inverse = inverse_ref[lax.axis_index("row")]
    for i in range(4):
        part = sums[360 * i : 360 * i + 384, :][:, :64]
        out_ref[i] = dot(inverse, part, NT, lax.Precision.HIGHEST).astype(BF)


def total_body(got_ref, out_ref):
    total = got_ref[0].astype(F32)
    for i in range(1, got_ref.shape[0]):
        total = total + got_ref[i].astype(F32)
    for i in range(out_ref.shape[0]):
        out_ref[i] = total.astype(BF)


def place_body(got_ref, out_ref):
    for layer in range(2):
        for k in range(4):
            value = got_ref[4 * layer + k].astype(F32)
            for j in range(9):
                start = 160 * j + 40 * k
                out_ref[layer, :, start : start + 40] = value[:, 40 * j : 40 * j + 40]


def on_device(x_input, pre_act, out_grad, conv_weight, q_prev):
    shape = jax.ShapeDtypeStruct
    whole = pl.BlockSpec(memory_space=pltpu.VMEM)
    far = pl.BlockSpec(memory_space=pltpu.HBM)
    images, rows, cols = (lax.axis_size(a) for a in ALL)
    z, row, col = (lax.axis_index(a) for a in ALL)
    plane, devices = rows * cols, images * rows * cols
    x, act, g = (v.reshape(256, 640) for v in (x_input, pre_act, out_grad))
    q_t = q_prev.transpose(1, 2, 0).reshape(128, 5760)

    sems = pltpu.SemaphoreType.DMA
    rims = call(
        rim_body,
        shape((plane, 32, 640), BF),
        1 << 24,
        1 << 20,
        vmem=62,
        in_specs=[far] * 2,
        scratch_shapes=[pltpu.VMEM((256, 640), BF)] * 2 + [sems((2,))],
    )(x, g)
    got = exchange(rims, PLANE)
    slices, q_one, y_two, slope = call(
        prepare_body,
        (
            shape((8, 160, 256), BF),
            shape((9, 128, 640), BF),
            shape((9, 128, 256), BF),
            shape((256, 640), F32),
        ),
        2 * 1152 * 640 * 256,
        8 << 20,
        vmem=62,
        in_specs=[far] * 3,
        scratch_shapes=[pltpu.VMEM((256, 640), BF)] * 2
        + [pltpu.VMEM((9, 128, 640), F32), sems((11,))],
    )(x, act, q_t)
    slices = exchange(slices, PLANE)

    each = 2 * 64 // devices if 128 % devices == 0 and devices >= 16 else 8
    parts = 128 // each
    pre_grad, p_part = call(
        power_body,
        (shape((256, 640), BF), shape((parts, each, 640), F32)),
        2 * 256 * 5760 * 1100,
        12 << 20,
        vmem=62,
        in_specs=[far] * 8,
        scratch_shapes=[
            pltpu.VMEM((256, 640), BF),
            pltpu.VMEM((256, 640), BF),
            pltpu.VMEM((plane, 32, 640), BF),
            pltpu.VMEM((3, 288, 256 + 32 * cols), BF),
            pltpu.VMEM((256, 640), F32),
            pltpu.VMEM((9, 128, 640), BF),
            pltpu.VMEM((9, 128, 256), BF),
            pltpu.VMEM((9, 640, 640), BF),
            pltpu.VMEM((3, 288, 640), BF),
            pltpu.VMEM((3, 288, 640), BF),
            pltpu.VMEM((256, 640), F32),
            pltpu.VMEM((256, 128), F32),
            pltpu.VMEM((128, 640), F32),
            sems((16,)),
        ],
    )(x, g, got, rim_pick(row, col, cols), slope, q_one, y_two, conv_weight)

    p_part, slices = lax.optimization_barrier((p_part, slices))
    if parts == devices:
        p_got = exchange(p_part, ALL)
        p_got = call(sum_body, shape((parts, each, 640), F32), 0, 1 << 20)(p_got)
        p_all = exchange(p_got, ALL)
    else:
        p_all = lax.psum(p_part, ALL)

    w_own, p_t = call(
        project_body,
        (shape((8, 256, 128), BF), shape((128, 640), F32)),
        2 * 512 * 640 * 128,
        2 << 20,
    )(p_all, pre_grad, g)
    w_all = exchange(w_own, PLANE)
    inverse, basis = call(
        factor_body,
        (shape((2, 64, 64), F32), shape((2, 64, 640), F32)),
        1 << 30,
        1 << 20,
    )(p_t)
    count = 640 // images
    basis_out = lax.dynamic_slice_in_dim(basis, z * count, count, 2).transpose(2, 0, 1)

    sums = call(
        taps_body,
        shape((4, 64, 384), BF),
        2 * 160 * 2048 * 1152,
        2 << 20,
        scratch_shapes=[pltpu.VMEM((34, 4, 16, 384), BF), pltpu.VMEM((1472, 128), F32)],
    )(w_all, slices, inverse)

    if images == 4:
        sums = exchange(sums, ("dp",))
        mine = call(total_body, shape((plane, 64, 384), BF), 0, 1 << 20)(sums)
        every = exchange(mine, PLANE)
        q_out = call(place_body, shape((2, 64, 1440), F32), 0, 1 << 20)(every)
        q_out = q_out.transpose(2, 0, 1)
    else:
        sums = lax.psum(sums[:, :, :360].astype(F32), "dp")
        every = lax.all_gather(sums, PLANE).reshape(rows, cols, 4, 64, 9, 40)
        every = every.transpose(2, 4, 1, 5, 0, 3).reshape(5760, 2, 64)
        count = 5760 // images
        q_out = lax.dynamic_slice_in_dim(every, z * count, count, 0)
    return basis_out, q_out


def solution(mesh):
    tiles = P("dp", "row", "col", None)
    return jax.shard_map(
        on_device,
        mesh=mesh,
        in_specs=(tiles, tiles, tiles, P(), P()),
        out_specs=(P("dp", None, None), P("dp", None, None)),
        check_vma=False,
    )
```

```python
import jax
import jax.numpy as jnp
from jax import lax
from jax.experimental import pallas as pl
from jax.experimental.pallas import tpu as pltpu
from jax.sharding import PartitionSpec as P

PLANE = ("row", "col")
ALL = ("dp", "row", "col")
BF = jnp.bfloat16
F32 = jnp.float32
NN = ((1,), (0,))
NT = ((1,), (1,))
TN = ((0,), (0,))
MIB = 1024 * 1024


def dot(left, right, dims, precision=None):
    return lax.dot_general(
        left, right, (dims, ((), ())), precision=precision, preferred_element_type=F32
    )


def call(body, out, flops, moved, vmem=40, **extra):
    return pl.pallas_call(
        body,
        out_shape=out,
        cost_estimate=pl.CostEstimate(flops=flops, bytes_accessed=moved, transcendentals=0),
        compiler_params=pltpu.CompilerParams(vmem_limit_bytes=vmem * MIB),
        **extra,
    )


def exchange(chunks, axes):
    return lax.all_to_all(chunks, axes, 0, 0, tiled=True)


def stacked_halves(value):
    high = value.astype(BF)
    return jnp.concatenate([high, (value - high.astype(F32)).astype(BF)], axis=0)


def paired_halves(value):
    total = value + pltpu.roll(value, 64, 1)
    high = total.astype(BF).astype(F32)
    lane = lax.broadcasted_iota(jnp.int32, value.shape, 1)
    return jnp.where(lane < 64, high, total - high)


def fetch(pairs, sems):
    copies = [pltpu.make_async_copy(src, dst, sems.at[i]) for i, (src, dst) in enumerate(pairs)]
    for copy in copies:
        copy.start()
    return copies


def rim_body(x_hbm, g_hbm, out_ref, x_ref, g_ref, sems):
    copies = fetch(((x_hbm, x_ref), (g_hbm, g_ref)), sems)
    row, col = lax.axis_index("row"), lax.axis_index("col")
    cols = out_ref.shape[0] // 2
    line = lax.broadcasted_iota(jnp.int32, (48, 256), 0)
    lane = lax.broadcasted_iota(jnp.int32, (48, 256), 1)
    ends = jnp.where(line < 32, 16 * (line % 16) + 15 * (line // 16), 240 * (1 - row) + line - 32)
    pick = jnp.where(lane == ends, 1.0, 0.0).astype(BF)
    for i, ref in enumerate((x_ref, g_ref)):
        copies[i].wait()
        rims = dot(pick, ref[...], NN)
        first, last, edge = rims[:16], rims[16:32], rims[32:]
        span = slice(16 * i, 16 * i + 16)
        for r in range(2):
            for c in range(cols):
                along = jnp.where(c > col, last, first)
                out_ref[r * cols + c, span] = jnp.where(row == r, along, edge).astype(BF)


def rim_pick(row, col, cols, s, first, count, start, width):
    cell = first + lax.broadcasted_iota(jnp.int32, (count, width), 0)
    lane = start + lax.broadcasted_iota(jnp.int32, (count, width), 1)
    y, x = cell // 16 - 1, cell % 16 + s - 1
    up = jnp.where(y < 0, -1, jnp.where(y > 15, 1, 0))
    side = jnp.where(x < 0, -1, jnp.where(x > 15, 1, 0))
    there_r, there_c = row + up, col + side
    inside = (there_r >= 0) & (there_r < 2) & (there_c >= 0) & (there_c < cols)
    got = 256 + (there_r * cols + there_c) * 16 + jnp.where(up != 0, x - 16 * side, y)
    index = jnp.where((up == 0) & (side == 0), 16 * y + x, got)
    hit = inside & (index == lane)
    return jnp.where(hit, 1.0, 0.0).astype(BF)


def prepare_body(
    x_hbm, act_hbm, q_hbm, slices_ref, q_one_ref, y_ref, slope_ref, x_ref, act_ref, q_all, sems
):
    pairs = [(x_hbm, x_ref), (act_hbm, act_ref)]
    pairs += [(q_hbm.at[:, 640 * t : 640 * t + 640], q_all.at[t]) for t in range(9)]
    copies = fetch(pairs, sems)
    copies[0].wait()
    copies[1].wait()
    act = act_ref[...].astype(F32)
    sigma = 1.0 / (1.0 + jnp.exp(-act))
    hidden = (act * sigma).astype(BF)
    slope_ref[...] = sigma * (1.0 + act * (1.0 - sigma))
    for layer, value in enumerate((x_ref[...], hidden)):
        turned = value.astype(F32).T
        for k in range(4):
            pieces = [turned[160 * j + 40 * k : 160 * j + 40 * k + 40] for j in range(4)]
            slices_ref[4 * layer + k] = jnp.concatenate(pieces, axis=0).astype(BF)
    for b in range(3):
        shifted = jnp.zeros((64, 384), F32)
        for a in range(3):
            t = 3 * a + b
            copies[2 + t].wait()
            q = q_all[t]
            q_one_ref[b, 128 * a : 128 * a + 128] = stacked_halves(q[:64])
            y = dot(stacked_halves(q[64:]), hidden, NT)
            y = jnp.concatenate([y[:64] + y[64:], jnp.zeros((64, 128), F32)], axis=1)
            shifted = shifted + (pltpu.roll(y, 16 * (2 - a), 1) if a < 2 else y)
        y_ref[b] = stacked_halves(shifted)


def power_body(
    x_hbm, g_hbm, got_hbm, slope_hbm, q_hbm, y_hbm, w_hbm,
    grad_ref, p_ref,
    x_ref, g_ref, got_ref, slope_ref, q_ref, y_ref, w_all,
    x_win, g_win, back, sems,
):
    pairs = [(got_hbm, got_ref), (g_hbm, g_ref), (x_hbm, x_ref)]
    pairs += [(y_hbm, y_ref), (q_hbm, q_ref), (slope_hbm, slope_ref)]
    pairs += [(w_hbm.at[t // 3, t % 3], w_all.at[t]) for t in range(9)]
    copies = fetch(pairs, sems)
    row, col = lax.axis_index("row"), lax.axis_index("col")
    cols = got_ref.shape[0] // 2
    width = 256 + 32 * cols
    picks = [rim_pick(row, col, cols, s, 0, 288, 0, width) for s in (0, 2)]
    ends = [rim_pick(row, col, cols, 1, r, 16, 256, 32 * cols) for r in (0, 272)]
    picks = [picks[0], jnp.concatenate(ends, axis=0), picks[1]]
    copies[0].wait()
    for i, (ref, win) in enumerate(((g_ref, g_win), (x_ref, x_win))):
        copies[1 + i].wait()
        rims = got_ref[:, 16 - 16 * i : 32 - 16 * i, :].reshape(-1, 640)
        lines = dot(picks[1], rims, NN).astype(BF)
        win[1, 0:16] = lines[:16]
        win[1, 16:272] = ref[...]
        win[1, 272:288] = lines[16:]
        cells = jnp.concatenate([ref[...], rims], axis=0)
        for s in (0, 2):
            win[s] = dot(picks[s], cells, NN).astype(BF)
    copies[3].wait()
    copies[4].wait()
    two, z_sum = 0.0, 0.0
    for b in range(3):
        two = two + dot(y_ref[b][:, :288], g_win[2 - b], NN)
        wide = dot(x_win[b], q_ref[b], NT)
        for a in range(3):
            z_sum = z_sum + wide[16 * a : 16 * a + 256, 128 * a : 128 * a + 128]
    each = p_ref.shape[1]

    def put(layer, value):
        value = value[:64] + value[64:]
        for i in range(64 // each):
            p_ref[layer * (64 // each) + i] = value[i * each : (i + 1) * each]

    put(1, two)
    z_sum = paired_halves(z_sum).astype(BF)
    for t in range(9):
        a, b = t // 3, t % 3
        copies[6 + t].wait()
        term = dot(g_win[2 - b, 16 * (2 - a) : 16 * (2 - a) + 256, :], w_all[t], NT)
        back[...] = term if t == 0 else back[...] + term
    copies[5].wait()
    grad = (back[...] * slope_ref[...]).astype(BF)
    grad_ref[...] = grad
    put(0, dot(z_sum, grad, TN))


def sum_body(got_ref, out_ref):
    total = jnp.sum(got_ref[...], axis=0)
    for i in range(out_ref.shape[0]):
        out_ref[i] = total


def project_body(got_ref, grad_ref, g_ref, w_ref, p_ref):
    each = got_ref.shape[1]
    for i in range(16):
        rows = [got_ref[i * (8 // each) + j] for j in range(8 // each)]
        p_ref[8 * i : 8 * i + 8, :] = jnp.concatenate(rows, axis=0)
    for layer, ref in enumerate((grad_ref, g_ref)):
        factor = stacked_halves(p_ref[64 * layer : 64 * layer + 64, :])
        out = paired_halves(dot(ref[...], factor, NT)).astype(BF)
        for k in range(4):
            w_ref[4 * layer + k] = out


def factor_body(p_ref, inverse_ref, basis_ref):
    high = lax.Precision.HIGHEST
    line = lax.broadcasted_iota(jnp.int32, (64, 128), 0)
    lane = lax.broadcasted_iota(jnp.int32, (64, 128), 1)
    unit = jnp.where(lane == line + 64, 1.0, 0.0)
    tables = []
    for layer in range(2):
        p = p_ref[64 * layer : 64 * layer + 64, :]
        gram = dot(p, p, NT, high)
        tables.append(jnp.concatenate([gram, unit[:, 64:]], axis=1))
    for k in range(64):
        for layer in range(2):
            table = tables[layer]
            pivot_row = table[k : k + 1, :]
            scaled = pivot_row / pivot_row[:, k : k + 1]
            column = jnp.where(line[:, :1] > k, table[:, k : k + 1], 0.0)
            tables[layer] = table - column * scaled
    for layer in range(2):
        table = tables[layer]
        pivots = jnp.sum(jnp.where(line == lane, table, 0.0), axis=1, keepdims=True)
        inverse = table[:, 64:] / jnp.sqrt(pivots)
        inverse_ref[layer] = inverse
        basis_ref[layer] = dot(inverse, p_ref[64 * layer : 64 * layer + 64, :], NN, high)


def taps_body(w_ref, x_ref, inverse_ref, out_ref, image, sums):
    zero = jnp.zeros((1, 4, 16, 384), BF)
    image[0:1] = zero
    image[33:34] = zero
    at = lax.broadcasted_iota(jnp.int32, (1024, 128), 0) % 64
    for r in range(2):
        tiles = [w_ref[4 * r + c].astype(F32).reshape(16, 16, 128) for c in range(4)]
        flat = jnp.stack(tiles, axis=1).reshape(1024, 128)
        left = jnp.where(at == 63, 0.0, pltpu.roll(flat, 1023, 0))
        right = jnp.where(at == 0, 0.0, pltpu.roll(flat, 1, 0))
        for i, value in enumerate((left, flat, right)):
            image[1 + 16 * r : 17 + 16 * r, :, :, 128 * i : 128 * i + 128] = value.astype(BF).reshape(
                16, 4, 16, 128
            )
    for a in range(3):
        total = jnp.zeros((160, 384), F32)
        for r in range(2):
            for c in range(4):
                window = image[16 * r + 2 - a : 16 * r + 18 - a, c].reshape(256, 384)
                total = total + dot(x_ref[4 * r + c], window, NN)
        for b in range(3):
            t = 3 * a + b
            value = total[:, 128 * b : 128 * b + 128]
            sums[160 * t : 160 * t + 160, :] = value + pltpu.roll(value, 64, 1)
    sums[1440:1472, :] = jnp.zeros((32, 128), F32)
    inverse = inverse_ref[lax.axis_index("row")]
    for i in range(4):
        part = sums[360 * i : 360 * i + 384, :][:, :64]
        out_ref[i] = dot(inverse, part, NT, lax.Precision.HIGHEST).astype(BF)


def total_body(got_ref, out_ref):
    total = got_ref[0].astype(F32)
    for i in range(1, got_ref.shape[0]):
        total = total + got_ref[i].astype(F32)
    for i in range(out_ref.shape[0]):
        out_ref[i] = total.astype(BF)


def place_body(got_ref, out_ref):
    for layer in range(2):
        for k in range(4):
            value = got_ref[4 * layer + k].astype(F32)
            for j in range(9):
                start = 160 * j + 40 * k
                out_ref[layer, :, start : start + 40] = value[:, 40 * j : 40 * j + 40]


def on_device(x_input, pre_act, out_grad, conv_weight, q_prev):
    shape = jax.ShapeDtypeStruct
    whole = pl.BlockSpec(memory_space=pltpu.VMEM)
    far = pl.BlockSpec(memory_space=pltpu.HBM)
    images, rows, cols = (lax.axis_size(a) for a in ALL)
    z = lax.axis_index("dp")
    plane, devices = rows * cols, images * rows * cols
    x, act, g = (v.reshape(256, 640) for v in (x_input, pre_act, out_grad))
    q_t = q_prev.transpose(1, 2, 0).reshape(128, 5760)

    sems = pltpu.SemaphoreType.DMA
    rims = call(
        rim_body,
        shape((plane, 32, 640), BF),
        1 << 24,
        1 << 20,
        vmem=62,
        in_specs=[far] * 2,
        scratch_shapes=[pltpu.VMEM((256, 640), BF)] * 2 + [sems((2,))],
    )(x, g)
    got = exchange(rims, PLANE)
    slices, q_one, y_two, slope = call(
        prepare_body,
        (
            shape((8, 160, 256), BF),
            shape((3, 384, 640), BF),
            shape((3, 128, 384), BF),
            shape((256, 640), F32),
        ),
        2 * 1152 * 640 * 256,
        8 << 20,
        vmem=62,
        in_specs=[far] * 3,
        scratch_shapes=[pltpu.VMEM((256, 640), BF)] * 2
        + [pltpu.VMEM((9, 128, 640), F32), sems((11,))],
    )(x, act, q_t)
    slices = exchange(slices, PLANE)

    each = 2 * 64 // devices if 128 % devices == 0 and devices >= 16 else 8
    parts = 128 // each
    pre_grad, p_part = call(
        power_body,
        (shape((256, 640), BF), shape((parts, each, 640), F32)),
        2 * 256 * 5760 * 1100,
        12 << 20,
        vmem=62,
        in_specs=[far] * 7,
        scratch_shapes=[
            pltpu.VMEM((256, 640), BF),
            pltpu.VMEM((256, 640), BF),
            pltpu.VMEM((plane, 32, 640), BF),
            pltpu.VMEM((256, 640), F32),
            pltpu.VMEM((3, 384, 640), BF),
            pltpu.VMEM((3, 128, 384), BF),
            pltpu.VMEM((9, 640, 640), BF),
            pltpu.VMEM((3, 288, 640), BF),
            pltpu.VMEM((3, 288, 640), BF),
            pltpu.VMEM((256, 640), F32),
            sems((15,)),
        ],
    )(x, g, got, slope, q_one, y_two, conv_weight)

    p_part, slices = lax.optimization_barrier((p_part, slices))
    if parts == devices:
        p_got = exchange(p_part, ALL)
        p_got = call(sum_body, shape((parts, each, 640), F32), 0, 1 << 20)(p_got)
        p_all = exchange(p_got, ALL)
    else:
        p_all = lax.psum(p_part, ALL)

    w_own, p_t = call(
        project_body,
        (shape((8, 256, 128), BF), shape((128, 640), F32)),
        2 * 512 * 640 * 128,
        2 << 20,
    )(p_all, pre_grad, g)
    w_all = exchange(w_own, PLANE)
    inverse, basis = call(
        factor_body,
        (shape((2, 64, 64), F32), shape((2, 64, 640), F32)),
        1 << 30,
        1 << 20,
    )(p_t)
    count = 640 // images
    basis_out = lax.dynamic_slice_in_dim(basis, z * count, count, 2).transpose(2, 0, 1)

    sums = call(
        taps_body,
        shape((4, 64, 384), BF),
        2 * 160 * 2048 * 1152,
        2 << 20,
        scratch_shapes=[pltpu.VMEM((34, 4, 16, 384), BF), pltpu.VMEM((1472, 128), F32)],
    )(w_all, slices, inverse)

    if images == 4:
        sums = exchange(sums, ("dp",))
        mine = call(total_body, shape((plane, 64, 384), BF), 0, 1 << 20)(sums)
        every = exchange(mine, PLANE)
        q_out = call(place_body, shape((2, 64, 1440), F32), 0, 1 << 20)(every)
        q_out = q_out.transpose(2, 0, 1)
    else:
        sums = lax.psum(sums[:, :, :360].astype(F32), "dp")
        every = lax.all_gather(sums, PLANE).reshape(rows, cols, 4, 64, 9, 40)
        every = every.transpose(2, 4, 1, 5, 0, 3).reshape(5760, 2, 64)
        count = 5760 // images
        q_out = lax.dynamic_slice_in_dim(every, z * count, count, 0)
    return basis_out, q_out


def solution(mesh):
    tiles = P("dp", "row", "col", None)
    return jax.shard_map(
        on_device,
        mesh=mesh,
        in_specs=(tiles, tiles, tiles, P(), P()),
        out_specs=(P("dp", None, None), P("dp", None, None)),
        check_vma=False,
    )
```

```python
import jax
import jax.numpy as jnp
from jax import lax
from jax.experimental import pallas as pl
from jax.experimental.pallas import tpu as pltpu
from jax.sharding import PartitionSpec as P

PLANE = ("row", "col")
ALL = ("dp", "row", "col")
BF = jnp.bfloat16
F32 = jnp.float32
NN = ((1,), (0,))
NT = ((1,), (1,))
TN = ((0,), (0,))
MIB = 1024 * 1024


def dot(left, right, dims, precision=None):
    return lax.dot_general(
        left, right, (dims, ((), ())), precision=precision, preferred_element_type=F32
    )


def call(body, out, flops, moved, vmem=40, **extra):
    return pl.pallas_call(
        body,
        out_shape=out,
        cost_estimate=pl.CostEstimate(flops=flops, bytes_accessed=moved, transcendentals=0),
        compiler_params=pltpu.CompilerParams(vmem_limit_bytes=vmem * MIB),
        **extra,
    )


def exchange(chunks, axes):
    return lax.all_to_all(chunks, axes, 0, 0, tiled=True)


def stacked_halves(value):
    high = value.astype(BF)
    return jnp.concatenate([high, (value - high.astype(F32)).astype(BF)], axis=0)


def paired_halves(value):
    total = value + pltpu.roll(value, 64, 1)
    high = total.astype(BF).astype(F32)
    lane = lax.broadcasted_iota(jnp.int32, value.shape, 1)
    return jnp.where(lane < 64, high, total - high)


def fetch(pairs, sems):
    copies = [pltpu.make_async_copy(src, dst, sems.at[i]) for i, (src, dst) in enumerate(pairs)]
    for copy in copies:
        copy.start()
    return copies


def rim_body(x_hbm, g_hbm, out_ref, x_ref, g_ref, sems):
    copies = fetch(((x_hbm, x_ref), (g_hbm, g_ref)), sems)
    row, col = lax.axis_index("row"), lax.axis_index("col")
    cols = out_ref.shape[0] // 2
    line = lax.broadcasted_iota(jnp.int32, (48, 256), 0)
    lane = lax.broadcasted_iota(jnp.int32, (48, 256), 1)
    ends = jnp.where(line < 32, 16 * (line % 16) + 15 * (line // 16), 240 * (1 - row) + line - 32)
    pick = jnp.where(lane == ends, 1.0, 0.0).astype(BF)
    for i, ref in enumerate((x_ref, g_ref)):
        copies[i].wait()
        rims = dot(pick, ref[...], NN)
        first, last, edge = rims[:16], rims[16:32], rims[32:]
        span = slice(16 * i, 16 * i + 16)
        for r in range(2):
            for c in range(cols):
                along = jnp.where(c > col, last, first)
                out_ref[r * cols + c, span] = jnp.where(row == r, along, edge).astype(BF)


def rim_pick(row, col, cols, s, first, count, start, width):
    cell = first + lax.broadcasted_iota(jnp.int32, (count, width), 0)
    lane = start + lax.broadcasted_iota(jnp.int32, (count, width), 1)
    y, x = cell // 16 - 1, cell % 16 + s - 1
    up = jnp.where(y < 0, -1, jnp.where(y > 15, 1, 0))
    side = jnp.where(x < 0, -1, jnp.where(x > 15, 1, 0))
    there_r, there_c = row + up, col + side
    inside = (there_r >= 0) & (there_r < 2) & (there_c >= 0) & (there_c < cols)
    got = 256 + (there_r * cols + there_c) * 16 + jnp.where(up != 0, x - 16 * side, y)
    index = jnp.where((up == 0) & (side == 0), 16 * y + x, got)
    hit = inside & (index == lane)
    return jnp.where(hit, 1.0, 0.0).astype(BF)


def prepare_body(
    x_hbm, act_hbm, q_hbm, slices_ref, q_one_ref, y_ref, slope_ref, x_ref, act_ref, q_all, sems
):
    pairs = [(x_hbm, x_ref), (act_hbm, act_ref)]
    pairs += [(q_hbm.at[:, 640 * t : 640 * t + 640], q_all.at[t]) for t in range(9)]
    copies = fetch(pairs, sems)
    copies[0].wait()
    copies[1].wait()
    act = act_ref[...].astype(F32)
    sigma = 1.0 / (1.0 + jnp.exp(-act))
    hidden = (act * sigma).astype(BF)
    slope_ref[...] = sigma * (1.0 + act * (1.0 - sigma))
    for layer, value in enumerate((x_ref[...], hidden)):
        turned = value.astype(F32).T
        for k in range(4):
            pieces = [turned[160 * j + 40 * k : 160 * j + 40 * k + 40] for j in range(4)]
            slices_ref[4 * layer + k] = jnp.concatenate(pieces, axis=0).astype(BF)
    for b in range(3):
        shifted = jnp.zeros((64, 384), F32)
        for a in range(3):
            t = 3 * a + b
            copies[2 + t].wait()
            q = q_all[t]
            q_one_ref[b, 128 * a : 128 * a + 128] = stacked_halves(q[:64])
            y = dot(stacked_halves(q[64:]), hidden, NT)
            y = jnp.concatenate([y[:64] + y[64:], jnp.zeros((64, 128), F32)], axis=1)
            shifted = shifted + (pltpu.roll(y, 16 * (2 - a), 1) if a < 2 else y)
        y_ref[b] = stacked_halves(shifted)


def power_body(
    x_hbm, g_hbm, got_hbm, slope_hbm, q_hbm, y_hbm, w_hbm,
    grad_ref, p_ref,
    x_ref, g_ref, got_ref, slope_ref, q_ref, y_ref, w_all,
    x_win, g_win, back, sems,
):
    pairs = [(got_hbm, got_ref), (g_hbm, g_ref), (x_hbm, x_ref)]
    pairs += [(y_hbm, y_ref), (q_hbm, q_ref), (slope_hbm, slope_ref)]
    pairs += [(w_hbm.at[t // 3, t % 3], w_all.at[t]) for t in range(9)]
    copies = fetch(pairs, sems)
    row, col = lax.axis_index("row"), lax.axis_index("col")
    cols = got_ref.shape[0] // 2
    width = 256 + 32 * cols
    picks = [rim_pick(row, col, cols, s, 0, 288, 0, width) for s in (0, 2)]
    ends = [rim_pick(row, col, cols, 1, r, 16, 256, 32 * cols) for r in (0, 272)]
    picks = [picks[0], jnp.concatenate(ends, axis=0), picks[1]]
    copies[0].wait()
    for i, (ref, win) in enumerate(((g_ref, g_win), (x_ref, x_win))):
        copies[1 + i].wait()
        rims = got_ref[:, 16 - 16 * i : 32 - 16 * i, :].reshape(-1, 640)
        lines = dot(picks[1], rims, NN).astype(BF)
        win[1, 0:16] = lines[:16]
        win[1, 16:272] = ref[...]
        win[1, 272:288] = lines[16:]
        cells = jnp.concatenate([ref[...], rims], axis=0)
        for s in (0, 2):
            win[s] = dot(picks[s], cells, NN).astype(BF)
    copies[3].wait()
    copies[4].wait()
    two, z_sum = 0.0, 0.0
    for b in range(3):
        two = two + dot(y_ref[b][:, :288], g_win[2 - b], NN)
        wide = dot(x_win[b], q_ref[b], NT)
        for a in range(3):
            z_sum = z_sum + wide[16 * a : 16 * a + 256, 128 * a : 128 * a + 128]
    each = p_ref.shape[1]

    def put(layer, value):
        value = value[:64] + value[64:]
        for i in range(64 // each):
            p_ref[layer * (64 // each) + i] = value[i * each : (i + 1) * each]

    put(1, two)
    z_sum = paired_halves(z_sum).astype(BF)
    for a in range(3):
        windows = [g_win[2 - b, 16 * (2 - a) : 16 * (2 - a) + 256, :] for b in range(3)]
        for b in range(3):
            copies[6 + 3 * a + b].wait()
        taps = jnp.concatenate([w_all[3 * a + b] for b in range(3)], axis=1)
        term = dot(jnp.concatenate(windows, axis=1), taps, NT)
        back[...] = term if a == 0 else back[...] + term
    copies[5].wait()
    grad = (back[...] * slope_ref[...]).astype(BF)
    grad_ref[...] = grad
    put(0, dot(z_sum, grad, TN))


def sum_body(got_ref, out_ref):
    total = jnp.sum(got_ref[...], axis=0)
    for i in range(out_ref.shape[0]):
        out_ref[i] = total


def project_body(got_ref, grad_hbm, g_hbm, w_ref, p_ref, grad_ref, g_ref, sems):
    copies = fetch(((grad_hbm, grad_ref), (g_hbm, g_ref)), sems)
    each = got_ref.shape[1]
    for i in range(16):
        rows = [got_ref[i * (8 // each) + j] for j in range(8 // each)]
        p_ref[8 * i : 8 * i + 8, :] = jnp.concatenate(rows, axis=0)
    for layer, ref in enumerate((grad_ref, g_ref)):
        factor = stacked_halves(p_ref[64 * layer : 64 * layer + 64, :])
        copies[layer].wait()
        out = paired_halves(dot(ref[...], factor, NT)).astype(BF)
        for k in range(4):
            w_ref[4 * layer + k] = out


def factor_body(p_ref, inverse_ref, basis_ref):
    high = lax.Precision.HIGHEST
    line = lax.broadcasted_iota(jnp.int32, (64, 128), 0)
    lane = lax.broadcasted_iota(jnp.int32, (64, 128), 1)
    unit = jnp.where(lane == line + 64, 1.0, 0.0)
    tables = []
    for layer in range(2):
        p = p_ref[64 * layer : 64 * layer + 64, :]
        gram = dot(p, p, NT, high)
        tables.append(jnp.concatenate([gram, unit[:, 64:]], axis=1))
    for k in range(64):
        for layer in range(2):
            table = tables[layer]
            pivot_row = table[k : k + 1, :]
            scaled = pivot_row / pivot_row[:, k : k + 1]
            column = jnp.where(line[:, :1] > k, table[:, k : k + 1], 0.0)
            tables[layer] = table - column * scaled
    for layer in range(2):
        table = tables[layer]
        pivots = jnp.sum(jnp.where(line == lane, table, 0.0), axis=1, keepdims=True)
        inverse = table[:, 64:] / jnp.sqrt(pivots)
        inverse_ref[layer] = inverse
        basis_ref[layer] = dot(inverse, p_ref[64 * layer : 64 * layer + 64, :], NN, high)


def taps_body(w_ref, x_ref, inverse_ref, out_ref, image, sums):
    zero = jnp.zeros((1, 4, 16, 384), BF)
    image[0:1] = zero
    image[33:34] = zero
    at = lax.broadcasted_iota(jnp.int32, (1024, 128), 0) % 64
    for r in range(2):
        tiles = [w_ref[4 * r + c].astype(F32).reshape(16, 16, 128) for c in range(4)]
        flat = jnp.stack(tiles, axis=1).reshape(1024, 128)
        left = jnp.where(at == 63, 0.0, pltpu.roll(flat, 1023, 0))
        right = jnp.where(at == 0, 0.0, pltpu.roll(flat, 1, 0))
        for i, value in enumerate((left, flat, right)):
            image[1 + 16 * r : 17 + 16 * r, :, :, 128 * i : 128 * i + 128] = value.astype(BF).reshape(
                16, 4, 16, 128
            )
    slices = jnp.concatenate([x_ref[4 * r + c] for c in range(4) for r in range(2)], axis=1)
    for a in range(3):
        windows = [image[2 - a : 34 - a, c].reshape(512, 384) for c in range(4)]
        total = dot(slices, jnp.concatenate(windows, axis=0), NN)
        for b in range(3):
            t = 3 * a + b
            value = total[:, 128 * b : 128 * b + 128]
            sums[160 * t : 160 * t + 160, :] = value + pltpu.roll(value, 64, 1)
    sums[1440:1472, :] = jnp.zeros((32, 128), F32)
    inverse = inverse_ref[lax.axis_index("row")]
    for i in range(4):
        part = sums[360 * i : 360 * i + 384, :][:, :64]
        out_ref[i] = dot(inverse, part, NT, lax.Precision.HIGHEST).astype(BF)


def total_body(got_ref, out_ref):
    total = got_ref[0].astype(F32)
    for i in range(1, got_ref.shape[0]):
        total = total + got_ref[i].astype(F32)
    for i in range(out_ref.shape[0]):
        out_ref[i] = total.astype(BF)


def place_body(got_ref, out_ref):
    for layer in range(2):
        for k in range(4):
            value = got_ref[4 * layer + k].astype(F32)
            for j in range(9):
                start = 160 * j + 40 * k
                out_ref[layer, :, start : start + 40] = value[:, 40 * j : 40 * j + 40]


def on_device(x_input, pre_act, out_grad, conv_weight, q_prev):
    shape = jax.ShapeDtypeStruct
    whole = pl.BlockSpec(memory_space=pltpu.VMEM)
    far = pl.BlockSpec(memory_space=pltpu.HBM)
    images, rows, cols = (lax.axis_size(a) for a in ALL)
    z = lax.axis_index("dp")
    plane, devices = rows * cols, images * rows * cols
    x, act, g = (v.reshape(256, 640) for v in (x_input, pre_act, out_grad))
    q_t = q_prev.transpose(1, 2, 0).reshape(128, 5760)

    sems = pltpu.SemaphoreType.DMA
    rims = call(
        rim_body,
        shape((plane, 32, 640), BF),
        1 << 24,
        1 << 20,
        vmem=62,
        in_specs=[far] * 2,
        scratch_shapes=[pltpu.VMEM((256, 640), BF)] * 2 + [sems((2,))],
    )(x, g)
    got = exchange(rims, PLANE)
    slices, q_one, y_two, slope = call(
        prepare_body,
        (
            shape((8, 160, 256), BF),
            shape((3, 384, 640), BF),
            shape((3, 128, 384), BF),
            shape((256, 640), F32),
        ),
        2 * 1152 * 640 * 256,
        8 << 20,
        vmem=62,
        in_specs=[far] * 3,
        scratch_shapes=[pltpu.VMEM((256, 640), BF)] * 2
        + [pltpu.VMEM((9, 128, 640), F32), sems((11,))],
    )(x, act, q_t)
    slices = exchange(slices, PLANE)

    each = 2 * 64 // devices if 128 % devices == 0 and devices >= 16 else 8
    parts = 128 // each
    pre_grad, p_part = call(
        power_body,
        (shape((256, 640), BF), shape((parts, each, 640), F32)),
        2 * 256 * 5760 * 1100,
        12 << 20,
        vmem=62,
        in_specs=[far] * 7,
        scratch_shapes=[
            pltpu.VMEM((256, 640), BF),
            pltpu.VMEM((256, 640), BF),
            pltpu.VMEM((plane, 32, 640), BF),
            pltpu.VMEM((256, 640), F32),
            pltpu.VMEM((3, 384, 640), BF),
            pltpu.VMEM((3, 128, 384), BF),
            pltpu.VMEM((9, 640, 640), BF),
            pltpu.VMEM((3, 288, 640), BF),
            pltpu.VMEM((3, 288, 640), BF),
            pltpu.VMEM((256, 640), F32),
            sems((15,)),
        ],
    )(x, g, got, slope, q_one, y_two, conv_weight)

    p_part, slices = lax.optimization_barrier((p_part, slices))
    if parts == devices:
        p_got = exchange(p_part, ALL)
        p_got = call(sum_body, shape((parts, each, 640), F32), 0, 1 << 20)(p_got)
        p_all = exchange(p_got, ALL)
    else:
        p_all = lax.psum(p_part, ALL)

    w_own, p_t = call(
        project_body,
        (shape((8, 256, 128), BF), shape((128, 640), F32)),
        2 * 512 * 640 * 128,
        2 << 20,
        vmem=62,
        in_specs=[whole, far, far],
        scratch_shapes=[pltpu.VMEM((256, 640), BF)] * 2 + [sems((2,))],
    )(p_all, pre_grad, g)
    w_all = exchange(w_own, PLANE)
    inverse, basis = call(
        factor_body,
        (shape((2, 64, 64), F32), shape((2, 64, 640), F32)),
        1 << 30,
        1 << 20,
    )(p_t)
    count = 640 // images
    basis_out = lax.dynamic_slice_in_dim(basis, z * count, count, 2).transpose(2, 0, 1)

    sums = call(
        taps_body,
        shape((4, 64, 384), BF),
        2 * 160 * 2048 * 1152,
        2 << 20,
        scratch_shapes=[pltpu.VMEM((34, 4, 16, 384), BF), pltpu.VMEM((1472, 128), F32)],
    )(w_all, slices, inverse)

    if images == 4:
        sums = exchange(sums, ("dp",))
        mine = call(total_body, shape((plane, 64, 384), BF), 0, 1 << 20)(sums)
        every = exchange(mine, PLANE)
        q_out = call(place_body, shape((2, 64, 1440), F32), 0, 1 << 20)(every)
        q_out = q_out.transpose(2, 0, 1)
    else:
        sums = lax.psum(sums[:, :, :360].astype(F32), "dp")
        every = lax.all_gather(sums, PLANE).reshape(rows, cols, 4, 64, 9, 40)
        every = every.transpose(2, 4, 1, 5, 0, 3).reshape(5760, 2, 64)
        count = 5760 // images
        q_out = lax.dynamic_slice_in_dim(every, z * count, count, 0)
    return basis_out, q_out


def solution(mesh):
    tiles = P("dp", "row", "col", None)
    return jax.shard_map(
        on_device,
        mesh=mesh,
        in_specs=(tiles, tiles, tiles, P(), P()),
        out_specs=(P("dp", None, None), P("dp", None, None)),
        check_vma=False,
    )
```

```python
import jax
import jax.numpy as jnp
from jax import lax
from jax.experimental import pallas as pl
from jax.experimental.pallas import tpu as pltpu
from jax.sharding import PartitionSpec as P

PLANE = ("row", "col")
ALL = ("dp", "row", "col")
BF = jnp.bfloat16
F32 = jnp.float32
NN = ((1,), (0,))
NT = ((1,), (1,))
TN = ((0,), (0,))
MIB = 1024 * 1024


def dot(left, right, dims, precision=None):
    return lax.dot_general(
        left, right, (dims, ((), ())), precision=precision, preferred_element_type=F32
    )


def call(body, out, flops, moved, vmem=40, **extra):
    return pl.pallas_call(
        body,
        out_shape=out,
        cost_estimate=pl.CostEstimate(flops=flops, bytes_accessed=moved, transcendentals=0),
        compiler_params=pltpu.CompilerParams(vmem_limit_bytes=vmem * MIB),
        **extra,
    )


def exchange(chunks, axes):
    return lax.all_to_all(chunks, axes, 0, 0, tiled=True)


def stacked_halves(value):
    high = value.astype(BF)
    return jnp.concatenate([high, (value - high.astype(F32)).astype(BF)], axis=0)


def paired_halves(value):
    total = value + pltpu.roll(value, 64, 1)
    high = total.astype(BF).astype(F32)
    lane = lax.broadcasted_iota(jnp.int32, value.shape, 1)
    return jnp.where(lane < 64, high, total - high)


def fetch(pairs, sems):
    copies = [pltpu.make_async_copy(src, dst, sems.at[i]) for i, (src, dst) in enumerate(pairs)]
    for copy in copies:
        copy.start()
    return copies


def rim_body(x_hbm, g_hbm, out_ref, x_ref, g_ref, sems):
    copies = fetch(((x_hbm, x_ref), (g_hbm, g_ref)), sems)
    row, col = lax.axis_index("row"), lax.axis_index("col")
    cols = out_ref.shape[0] // 2
    line = lax.broadcasted_iota(jnp.int32, (48, 256), 0)
    lane = lax.broadcasted_iota(jnp.int32, (48, 256), 1)
    ends = jnp.where(line < 32, 16 * (line % 16) + 15 * (line // 16), 240 * (1 - row) + line - 32)
    pick = jnp.where(lane == ends, 1.0, 0.0).astype(BF)
    for i, ref in enumerate((x_ref, g_ref)):
        copies[i].wait()
        rims = dot(pick, ref[...], NN)
        first, last, edge = rims[:16], rims[16:32], rims[32:]
        span = slice(16 * i, 16 * i + 16)
        for r in range(2):
            for c in range(cols):
                along = jnp.where(c > col, last, first)
                out_ref[r * cols + c, span] = jnp.where(row == r, along, edge).astype(BF)


def rim_pick(row, col, cols, s, first, count, start, width):
    cell = first + lax.broadcasted_iota(jnp.int32, (count, width), 0)
    lane = start + lax.broadcasted_iota(jnp.int32, (count, width), 1)
    y, x = cell // 16 - 1, cell % 16 + s - 1
    up = jnp.where(y < 0, -1, jnp.where(y > 15, 1, 0))
    side = jnp.where(x < 0, -1, jnp.where(x > 15, 1, 0))
    there_r, there_c = row + up, col + side
    inside = (there_r >= 0) & (there_r < 2) & (there_c >= 0) & (there_c < cols)
    got = 256 + (there_r * cols + there_c) * 16 + jnp.where(up != 0, x - 16 * side, y)
    index = jnp.where((up == 0) & (side == 0), 16 * y + x, got)
    hit = inside & (index == lane)
    return jnp.where(hit, 1.0, 0.0).astype(BF)


def prepare_body(
    x_hbm, act_hbm, q_hbm, slices_ref, q_one_ref, y_ref, slope_ref, x_ref, act_ref, q_all, sems
):
    pairs = [(x_hbm, x_ref), (act_hbm, act_ref)]
    pairs += [(q_hbm.at[:, 640 * t : 640 * t + 640], q_all.at[t]) for t in range(9)]
    copies = fetch(pairs, sems)
    copies[0].wait()
    copies[1].wait()
    act = act_ref[...].astype(F32)
    sigma = 1.0 / (1.0 + jnp.exp(-act))
    hidden = (act * sigma).astype(BF)
    slope_ref[...] = sigma * (1.0 + act * (1.0 - sigma))
    for layer, value in enumerate((x_ref[...], hidden)):
        turned = value.astype(F32).T
        for k in range(4):
            pieces = [turned[160 * j + 40 * k : 160 * j + 40 * k + 40] for j in range(4)]
            slices_ref[4 * layer + k] = jnp.concatenate(pieces, axis=0).astype(BF)
    for b in range(3):
        shifted = jnp.zeros((64, 384), F32)
        for a in range(3):
            t = 3 * a + b
            copies[2 + t].wait()
            q = q_all[t]
            q_one_ref[b, 128 * a : 128 * a + 128] = stacked_halves(q[:64])
            y = dot(stacked_halves(q[64:]), hidden, NT)
            y = jnp.concatenate([y[:64] + y[64:], jnp.zeros((64, 128), F32)], axis=1)
            shifted = shifted + (pltpu.roll(y, 16 * (2 - a), 1) if a < 2 else y)
        y_ref[b] = stacked_halves(shifted)


def power_body(
    x_hbm, g_hbm, got_hbm, slope_hbm, q_hbm, y_hbm, w_hbm,
    keep_ref, swap_ref, p_ref,
    x_ref, g_ref, got_ref, slope_ref, q_ref, y_ref, w_all,
    x_win, g_win, back, sems,
):
    pairs = [(got_hbm, got_ref), (g_hbm, g_ref), (x_hbm, x_ref)]
    pairs += [(y_hbm, y_ref), (q_hbm, q_ref), (slope_hbm, slope_ref)]
    pairs += [(w_hbm.at[t // 3, t % 3], w_all.at[t]) for t in range(9)]
    copies = fetch(pairs, sems)
    row, col = lax.axis_index("row"), lax.axis_index("col")
    cols = got_ref.shape[0] // 2
    width = 256 + 32 * cols
    picks = [rim_pick(row, col, cols, s, 0, 288, 0, width) for s in (0, 2)]
    ends = [rim_pick(row, col, cols, 1, r, 16, 256, 32 * cols) for r in (0, 272)]
    picks = [picks[0], jnp.concatenate(ends, axis=0), picks[1]]
    copies[0].wait()
    for i, (ref, win) in enumerate(((g_ref, g_win), (x_ref, x_win))):
        copies[1 + i].wait()
        rims = got_ref[:, 16 - 16 * i : 32 - 16 * i, :].reshape(-1, 640)
        lines = dot(picks[1], rims, NN).astype(BF)
        win[1, 0:16] = lines[:16]
        win[1, 16:272] = ref[...]
        win[1, 272:288] = lines[16:]
        cells = jnp.concatenate([ref[...], rims], axis=0)
        for s in (0, 2):
            win[s] = dot(picks[s], cells, NN).astype(BF)
    copies[3].wait()
    copies[4].wait()
    two, z_sum = 0.0, 0.0
    for b in range(3):
        two = two + dot(y_ref[b][:, :288], g_win[2 - b], NN)
        wide = dot(x_win[b], q_ref[b], NT)
        for a in range(3):
            z_sum = z_sum + wide[16 * a : 16 * a + 256, 128 * a : 128 * a + 128]
    each = p_ref.shape[1]

    def put(layer, value):
        value = value[:64] + value[64:]
        for i in range(64 // each):
            owner = i // cols * 2 * cols + layer * cols + i % cols
            p_ref[owner] = value[i * each : (i + 1) * each]

    put(1, two)
    z_sum = paired_halves(z_sum).astype(BF)
    for a in range(3):
        windows = [g_win[2 - b, 16 * (2 - a) : 16 * (2 - a) + 256, :] for b in range(3)]
        for b in range(3):
            copies[6 + 3 * a + b].wait()
        taps = jnp.concatenate([w_all[3 * a + b] for b in range(3)], axis=1)
        term = dot(jnp.concatenate(windows, axis=1), taps, NT)
        back[...] = term if a == 0 else back[...] + term
    copies[5].wait()
    grad = (back[...] * slope_ref[...]).astype(BF)
    keep_ref[...] = jnp.where(row == 0, grad, g_ref[...])
    swap_ref[...] = jnp.where(row == 0, g_ref[...], grad)
    put(0, dot(z_sum, grad, TN))


def sum_body(got_ref, out_ref):
    total = jnp.sum(got_ref[...], axis=0)
    for i in range(out_ref.shape[0]):
        out_ref[i] = total


def project_body(got_ref, keep_ref, swap_ref, w_ref, p_ref):
    row = lax.axis_index("row")
    each = got_ref.shape[1]
    for i in range(8):
        rows = [got_ref[i * (8 // each) + j] for j in range(8 // each)]
        p_ref[8 * i : 8 * i + 8, :] = jnp.concatenate(rows, axis=0)
    factor = stacked_halves(p_ref[...])
    for start, ref in ((row, keep_ref), (1 - row, swap_ref)):
        out = paired_halves(dot(ref[...], factor, NT)).astype(BF)
        for k in range(4):
            w_ref[k, pl.ds(pl.multiple_of(256 * start, 256), 256), :] = out


def factor_body(p_ref, inverse_ref, basis_ref, share_ref, slot):
    high = lax.Precision.HIGHEST
    line = lax.broadcasted_iota(jnp.int32, (64, 128), 0)
    lane = lax.broadcasted_iota(jnp.int32, (64, 128), 1)
    p = p_ref[...]
    unit = jnp.where(lane == line + 64, 1.0, 0.0)
    table = jnp.concatenate([dot(p, p, NT, high), unit[:, 64:]], axis=1)
    for k in range(64):
        pivot_row = table[k : k + 1, :]
        scaled = pivot_row / pivot_row[:, k : k + 1]
        column = jnp.where(line[:, :1] > k, table[:, k : k + 1], 0.0)
        table = table - column * scaled
    pivots = jnp.sum(jnp.where(line == lane, table, 0.0), axis=1, keepdims=True)
    inverse = table[:, 64:] / jnp.sqrt(pivots)
    inverse_ref[...] = inverse
    basis = dot(inverse, p, NN, high)
    basis_ref[...] = basis
    slot[...] = basis
    z, col = lax.axis_index("dp"), lax.axis_index("col")
    rows = slot[pl.ds(pl.multiple_of(16 * col, 16), 16), :]
    part = jnp.zeros((16, 160), F32)
    for i in range(4):
        part = jnp.where(z == i, rows[:, 160 * i : 160 * i + 160], part)
    top = part.astype(BF).astype(F32)
    part = jnp.concatenate([top, part - top, jnp.zeros((16, 64), F32)], axis=1)
    share_ref[...] = part.astype(BF)


def taps_body(w_ref, x_ref, inverse_ref, out_ref, image, sums):
    zero = jnp.zeros((1, 4, 16, 384), BF)
    image[0:1] = zero
    image[33:34] = zero
    at = lax.broadcasted_iota(jnp.int32, (2048, 128), 0) % 64
    strips = [w_ref[c].astype(F32).reshape(32, 16, 128) for c in range(4)]
    flat = jnp.stack(strips, axis=1).reshape(2048, 128)
    left = jnp.where(at == 63, 0.0, pltpu.roll(flat, 2047, 0))
    right = jnp.where(at == 0, 0.0, pltpu.roll(flat, 1, 0))
    for i, value in enumerate((left, flat, right)):
        value = value.astype(BF).reshape(32, 4, 16, 128)
        image[1:33, :, :, 128 * i : 128 * i + 128] = value
    slices = jnp.concatenate([x_ref[4 * r + c] for c in range(4) for r in range(2)], axis=1)
    for a in range(3):
        windows = [image[2 - a : 34 - a, c].reshape(512, 384) for c in range(4)]
        total = dot(slices, jnp.concatenate(windows, axis=0), NN)
        for b in range(3):
            t = 3 * a + b
            value = total[:, 128 * b : 128 * b + 128]
            sums[160 * t : 160 * t + 160, :] = value + pltpu.roll(value, 64, 1)
    sums[1440:1472, :] = jnp.zeros((32, 128), F32)
    inverse = inverse_ref[...]
    for i in range(4):
        part = sums[360 * i : 360 * i + 384, :][:, :64]
        out_ref[i] = dot(inverse, part, NT, lax.Precision.HIGHEST).astype(BF)


def total_body(got_ref, share_ref, out_ref):
    total = got_ref[0].astype(F32)
    for i in range(1, got_ref.shape[0]):
        total = total + got_ref[i].astype(F32)
    for i in range(out_ref.shape[0]):
        out_ref[i, 0:64] = total.astype(BF)
        out_ref[i, 64:80] = share_ref[...]


def place_body(got_ref, basis_ref, out_ref):
    for layer in range(2):
        for k in range(4):
            value = got_ref[4 * layer + k].astype(F32)
            for j in range(9):
                start = 160 * j + 40 * k
                out_ref[layer, :, start : start + 40] = value[:64, 40 * j : 40 * j + 40]
            basis = value[64:, :160] + value[64:, 160:320]
            basis_ref[layer, 16 * k : 16 * k + 16, :] = basis


def on_device(x_input, pre_act, out_grad, conv_weight, q_prev):
    shape = jax.ShapeDtypeStruct
    whole = pl.BlockSpec(memory_space=pltpu.VMEM)
    far = pl.BlockSpec(memory_space=pltpu.HBM)
    images, rows, cols = (lax.axis_size(a) for a in ALL)
    z, row = lax.axis_index("dp"), lax.axis_index("row")
    plane, devices = rows * cols, images * rows * cols
    x, act, g = (v.reshape(256, 640) for v in (x_input, pre_act, out_grad))
    q_t = q_prev.transpose(1, 2, 0).reshape(128, 5760)

    sems = pltpu.SemaphoreType.DMA
    rims = call(
        rim_body,
        shape((plane, 32, 640), BF),
        1 << 24,
        1 << 20,
        vmem=62,
        in_specs=[far] * 2,
        scratch_shapes=[pltpu.VMEM((256, 640), BF)] * 2 + [sems((2,))],
    )(x, g)
    got = exchange(rims, PLANE)
    slices, q_one, y_two, slope = call(
        prepare_body,
        (
            shape((8, 160, 256), BF),
            shape((3, 384, 640), BF),
            shape((3, 128, 384), BF),
            shape((256, 640), F32),
        ),
        2 * 1152 * 640 * 256,
        8 << 20,
        vmem=62,
        in_specs=[far] * 3,
        scratch_shapes=[pltpu.VMEM((256, 640), BF)] * 2
        + [pltpu.VMEM((9, 128, 640), F32), sems((11,))],
    )(x, act, q_t)
    slices = exchange(slices, PLANE)

    each = 2 * 64 // devices if 128 % devices == 0 and devices >= 16 else 8
    parts = 128 // each
    keep, swap, p_part = call(
        power_body,
        (shape((256, 640), BF), shape((256, 640), BF), shape((parts, each, 640), F32)),
        2 * 256 * 5760 * 1100,
        12 << 20,
        vmem=62,
        in_specs=[far] * 7,
        scratch_shapes=[
            pltpu.VMEM((256, 640), BF),
            pltpu.VMEM((256, 640), BF),
            pltpu.VMEM((plane, 32, 640), BF),
            pltpu.VMEM((256, 640), F32),
            pltpu.VMEM((3, 384, 640), BF),
            pltpu.VMEM((3, 128, 384), BF),
            pltpu.VMEM((9, 640, 640), BF),
            pltpu.VMEM((3, 288, 640), BF),
            pltpu.VMEM((3, 288, 640), BF),
            pltpu.VMEM((256, 640), F32),
            sems((15,)),
        ],
    )(x, g, got, slope, q_one, y_two, conv_weight)

    swap = lax.ppermute(swap, "row", [(0, 1), (1, 0)])
    p_part, slices = lax.optimization_barrier((p_part, slices))
    if parts == devices:
        p_got = exchange(p_part, ALL)
        p_got = call(sum_body, shape((parts // 2, each, 640), F32), 0, 1 << 20)(p_got)
        p_own = exchange(p_got, ("dp", "col"))
    else:
        p_part = p_part.reshape(-1, 2, cols, each, 640).transpose(1, 0, 2, 3, 4)
        p_part = lax.psum(p_part.reshape(2, parts // 2, each, 640), ALL)
        p_own = lax.dynamic_index_in_dim(p_part, row, 0, False)

    w_own, p_t = call(
        project_body,
        (shape((4, 512, 128), BF), shape((64, 640), F32)),
        2 * 512 * 640 * 128,
        2 << 20,
    )(p_own, keep, swap)
    w_all = exchange(w_own, ("col",))
    inverse, basis, share = call(
        factor_body,
        (shape((64, 64), F32), shape((64, 640), F32), shape((16, 384), BF)),
        1 << 30,
        1 << 20,
        scratch_shapes=[pltpu.VMEM((64, 640), F32)],
    )(p_t)

    sums = call(
        taps_body,
        shape((4, 64, 384), BF),
        2 * 160 * 2048 * 1152,
        2 << 20,
        scratch_shapes=[pltpu.VMEM((34, 4, 16, 384), BF), pltpu.VMEM((1472, 128), F32)],
    )(w_all, slices, inverse)

    if images == 4:
        sums = exchange(sums, ("dp",))
        mine = call(total_body, shape((plane, 80, 384), BF), 0, 1 << 20)(sums, share)
        every = exchange(mine, PLANE)
        basis_out, q_out = call(
            place_body, (shape((2, 64, 160), F32), shape((2, 64, 1440), F32)), 0, 1 << 20
        )(every)
        return basis_out.transpose(2, 0, 1), q_out.transpose(2, 0, 1)
    sums = lax.psum(sums[:, :, :360].astype(F32), "dp")
    every = lax.all_gather(sums, PLANE).reshape(rows, cols, 4, 64, 9, 40)
    every = every.transpose(2, 4, 1, 5, 0, 3).reshape(5760, 2, 64)
    q_out = lax.dynamic_slice_in_dim(every, z * (5760 // images), 5760 // images, 0)
    bases = lax.all_gather(basis, "row").transpose(2, 0, 1)
    return lax.dynamic_slice_in_dim(bases, z * (640 // images), 640 // images, 0), q_out


def solution(mesh):
    tiles = P("dp", "row", "col", None)
    return jax.shard_map(
        on_device,
        mesh=mesh,
        in_specs=(tiles, tiles, tiles, P(), P()),
        out_specs=(P("dp", None, None), P("dp", None, None)),
        check_vma=False,
    )
```

```python
import jax
import jax.numpy as jnp
from jax import lax
from jax.experimental import pallas as pl
from jax.experimental.pallas import tpu as pltpu
from jax.sharding import PartitionSpec as P

PLANE = ("row", "col")
ALL = ("dp", "row", "col")
BF = jnp.bfloat16
F32 = jnp.float32
NN = ((1,), (0,))
NT = ((1,), (1,))
TN = ((0,), (0,))
MIB = 1024 * 1024


def dot(left, right, dims, precision=None):
    return lax.dot_general(
        left, right, (dims, ((), ())), precision=precision, preferred_element_type=F32
    )


def call(body, out, flops, moved, vmem=40, **extra):
    return pl.pallas_call(
        body,
        out_shape=out,
        cost_estimate=pl.CostEstimate(flops=flops, bytes_accessed=moved, transcendentals=0),
        compiler_params=pltpu.CompilerParams(vmem_limit_bytes=vmem * MIB),
        **extra,
    )


def exchange(chunks, axes):
    return lax.all_to_all(chunks, axes, 0, 0, tiled=True)


def stacked_halves(value):
    high = value.astype(BF)
    return jnp.concatenate([high, (value - high.astype(F32)).astype(BF)], axis=0)


def paired_halves(value):
    total = value + pltpu.roll(value, 64, 1)
    high = total.astype(BF).astype(F32)
    lane = lax.broadcasted_iota(jnp.int32, value.shape, 1)
    return jnp.where(lane < 64, high, total - high)


def fetch(pairs, sems):
    copies = [pltpu.make_async_copy(src, dst, sems.at[i]) for i, (src, dst) in enumerate(pairs)]
    for copy in copies:
        copy.start()
    return copies


def rim_body(x_hbm, g_hbm, out_ref, x_ref, g_ref, sems):
    copies = fetch(((x_hbm, x_ref), (g_hbm, g_ref)), sems)
    row, col = lax.axis_index("row"), lax.axis_index("col")
    cols = out_ref.shape[0] // 2
    line = lax.broadcasted_iota(jnp.int32, (48, 256), 0)
    lane = lax.broadcasted_iota(jnp.int32, (48, 256), 1)
    ends = jnp.where(line < 32, 16 * (line % 16) + 15 * (line // 16), 240 * (1 - row) + line - 32)
    pick = jnp.where(lane == ends, 1.0, 0.0).astype(BF)
    for i, ref in enumerate((x_ref, g_ref)):
        copies[i].wait()
        rims = dot(pick, ref[...], NN)
        first, last, edge = rims[:16], rims[16:32], rims[32:]
        span = slice(16 * i, 16 * i + 16)
        for r in range(2):
            for c in range(cols):
                along = jnp.where(c > col, last, first)
                out_ref[r * cols + c, span] = jnp.where(row == r, along, edge).astype(BF)


def rim_pick(row, col, cols, s, first, count, start, width):
    cell = first + lax.broadcasted_iota(jnp.int32, (count, width), 0)
    lane = start + lax.broadcasted_iota(jnp.int32, (count, width), 1)
    y, x = cell // 16 - 1, cell % 16 + s - 1
    up = jnp.where(y < 0, -1, jnp.where(y > 15, 1, 0))
    side = jnp.where(x < 0, -1, jnp.where(x > 15, 1, 0))
    there_r, there_c = row + up, col + side
    inside = (there_r >= 0) & (there_r < 2) & (there_c >= 0) & (there_c < cols)
    got = 256 + (there_r * cols + there_c) * 16 + jnp.where(up != 0, x - 16 * side, y)
    index = jnp.where((up == 0) & (side == 0), 16 * y + x, got)
    hit = inside & (index == lane)
    return jnp.where(hit, 1.0, 0.0).astype(BF)


def prepare_body(
    x_hbm, act_hbm, q_hbm, slices_ref, q_one_ref, y_ref, slope_ref, x_ref, act_ref, q_all, sems
):
    pairs = [(x_hbm, x_ref), (act_hbm, act_ref)]
    pairs += [(q_hbm.at[:, 640 * t : 640 * t + 640], q_all.at[t]) for t in range(9)]
    copies = fetch(pairs, sems)
    copies[0].wait()
    copies[1].wait()
    act = act_ref[...].astype(F32)
    sigma = 1.0 / (1.0 + jnp.exp(-act))
    hidden = (act * sigma).astype(BF)
    slope_ref[...] = sigma * (1.0 + act * (1.0 - sigma))
    for layer, value in enumerate((x_ref[...], hidden)):
        turned = value.astype(F32).T
        for k in range(4):
            pieces = [turned[160 * j + 40 * k : 160 * j + 40 * k + 40] for j in range(4)]
            slices_ref[4 * layer + k] = jnp.concatenate(pieces, axis=0).astype(BF)
    for b in range(3):
        shifted = jnp.zeros((64, 384), F32)
        for a in range(3):
            t = 3 * a + b
            copies[2 + t].wait()
            q = q_all[t]
            q_one_ref[b, 128 * a : 128 * a + 128] = stacked_halves(q[:64])
            y = dot(stacked_halves(q[64:]), hidden, NT)
            y = jnp.concatenate([y[:64] + y[64:], jnp.zeros((64, 128), F32)], axis=1)
            shifted = shifted + (pltpu.roll(y, 16 * (2 - a), 1) if a < 2 else y)
        y_ref[b] = stacked_halves(shifted)


def power_body(
    x_hbm, g_hbm, got_hbm, slope_hbm, q_hbm, y_hbm, w_hbm,
    keep_ref, swap_ref, p_keep_ref, p_swap_ref,
    x_ref, g_ref, got_ref, slope_ref, q_ref, y_ref, w_all,
    x_win, g_win, back, sems,
):
    pairs = [(got_hbm, got_ref), (g_hbm, g_ref), (x_hbm, x_ref)]
    pairs += [(y_hbm, y_ref), (q_hbm, q_ref), (slope_hbm, slope_ref)]
    pairs += [(w_hbm.at[t // 3, t % 3], w_all.at[t]) for t in range(9)]
    copies = fetch(pairs, sems)
    row, col = lax.axis_index("row"), lax.axis_index("col")
    cols = got_ref.shape[0] // 2
    width = 256 + 32 * cols
    picks = [rim_pick(row, col, cols, s, 0, 288, 0, width) for s in (0, 2)]
    ends = [rim_pick(row, col, cols, 1, r, 16, 256, 32 * cols) for r in (0, 272)]
    picks = [picks[0], jnp.concatenate(ends, axis=0), picks[1]]
    copies[0].wait()
    for i, (ref, win) in enumerate(((g_ref, g_win), (x_ref, x_win))):
        copies[1 + i].wait()
        rims = got_ref[:, 16 - 16 * i : 32 - 16 * i, :].reshape(-1, 640)
        lines = dot(picks[1], rims, NN).astype(BF)
        win[1, 0:16] = lines[:16]
        win[1, 16:272] = ref[...]
        win[1, 272:288] = lines[16:]
        cells = jnp.concatenate([ref[...], rims], axis=0)
        for s in (0, 2):
            win[s] = dot(picks[s], cells, NN).astype(BF)
    copies[3].wait()
    copies[4].wait()
    two, z_sum = 0.0, 0.0
    for b in range(3):
        two = two + dot(y_ref[b][:, :288], g_win[2 - b], NN)
        wide = dot(x_win[b], q_ref[b], NT)
        for a in range(3):
            z_sum = z_sum + wide[16 * a : 16 * a + 256, 128 * a : 128 * a + 128]
    z_sum = paired_halves(z_sum).astype(BF)
    for a in range(3):
        windows = [g_win[2 - b, 16 * (2 - a) : 16 * (2 - a) + 256, :] for b in range(3)]
        for b in range(3):
            copies[6 + 3 * a + b].wait()
        taps = jnp.concatenate([w_all[3 * a + b] for b in range(3)], axis=1)
        term = dot(jnp.concatenate(windows, axis=1), taps, NT)
        back[...] = term if a == 0 else back[...] + term
    copies[5].wait()
    grad = (back[...] * slope_ref[...]).astype(BF)
    keep_ref[...] = jnp.where(row == 0, grad, g_ref[...])
    swap_ref[...] = jnp.where(row == 0, g_ref[...], grad)
    one = dot(z_sum, grad, TN)
    one, two = one[:64] + one[64:], two[:64] + two[64:]
    each = p_keep_ref.shape[1]
    for ref, value in (
        (p_keep_ref, jnp.where(row == 0, one, two)),
        (p_swap_ref, jnp.where(row == 0, two, one)),
    ):
        for i in range(64 // each):
            ref[i] = value[i * each : (i + 1) * each]


def add_body(left_ref, right_ref, out_ref):
    out_ref[...] = left_ref[...] + right_ref[...]


def sum_body(got_ref, keep_ref, swap_ref, out_ref):
    total = jnp.sum(got_ref[...], axis=0)
    for i in range(out_ref.shape[0]):
        out_ref[i] = total


def project_body(got_ref, keep_ref, swap_ref, w_ref, p_ref):
    row = lax.axis_index("row")
    each = got_ref.shape[1]
    for i in range(8):
        rows = [got_ref[i * (8 // each) + j] for j in range(8 // each)]
        p_ref[8 * i : 8 * i + 8, :] = jnp.concatenate(rows, axis=0)
    factor = stacked_halves(p_ref[...])
    for start, ref in ((row, keep_ref), (1 - row, swap_ref)):
        out = paired_halves(dot(ref[...], factor, NT)).astype(BF)
        for k in range(4):
            w_ref[k, pl.ds(pl.multiple_of(256 * start, 256), 256), :] = out


def factor_body(p_ref, inverse_ref, basis_ref, share_ref):
    high = lax.Precision.HIGHEST
    line = lax.broadcasted_iota(jnp.int32, (64, 128), 0)
    lane = lax.broadcasted_iota(jnp.int32, (64, 128), 1)
    p = p_ref[...]
    unit = jnp.where(lane == line + 64, 1.0, 0.0)
    table = jnp.concatenate([dot(p, p, NT, high), unit[:, 64:]], axis=1)
    for k in range(64):
        pivot_row = table[k : k + 1, :]
        scaled = pivot_row / pivot_row[:, k : k + 1]
        column = jnp.where(line[:, :1] > k, table[:, k : k + 1], 0.0)
        table = table - column * scaled
    pivots = jnp.sum(jnp.where(line == lane, table, 0.0), axis=1, keepdims=True)
    inverse = table[:, 64:] / jnp.sqrt(pivots)
    inverse_ref[...] = inverse
    basis = dot(inverse, p, NN, high)
    basis_ref[...] = basis
    z = lax.axis_index("dp")
    part = basis[:, :160]
    for i in range(1, 4):
        part = jnp.where(z == i, basis[:, 160 * i : 160 * i + 160], part)
    share_ref[...] = part


def taps_body(w_ref, x_ref, inverse_ref, out_ref, image, sums):
    zero = jnp.zeros((1, 4, 16, 384), BF)
    image[0:1] = zero
    image[33:34] = zero
    at = lax.broadcasted_iota(jnp.int32, (2048, 128), 0) % 64
    strips = [w_ref[c].astype(F32).reshape(32, 16, 128) for c in range(4)]
    flat = jnp.stack(strips, axis=1).reshape(2048, 128)
    left = jnp.where(at == 63, 0.0, pltpu.roll(flat, 2047, 0))
    right = jnp.where(at == 0, 0.0, pltpu.roll(flat, 1, 0))
    for i, value in enumerate((left, flat, right)):
        value = value.astype(BF).reshape(32, 4, 16, 128)
        image[1:33, :, :, 128 * i : 128 * i + 128] = value
    slices = jnp.concatenate([x_ref[4 * r + c] for c in range(4) for r in range(2)], axis=1)
    for a in range(3):
        windows = [image[2 - a : 34 - a, c].reshape(512, 384) for c in range(4)]
        total = dot(slices, jnp.concatenate(windows, axis=0), NN)
        for b in range(3):
            t = 3 * a + b
            value = total[:, 128 * b : 128 * b + 128]
            sums[160 * t : 160 * t + 160, :] = value + pltpu.roll(value, 64, 1)
    sums[1440:1472, :] = jnp.zeros((32, 128), F32)
    inverse = inverse_ref[...]
    for i in range(4):
        part = sums[360 * i : 360 * i + 384, :][:, :64]
        out_ref[i] = dot(inverse, part, NT, lax.Precision.HIGHEST).astype(BF)


def total_body(got_ref, out_ref):
    total = got_ref[0].astype(F32)
    for i in range(1, got_ref.shape[0]):
        total = total + got_ref[i].astype(F32)
    for i in range(out_ref.shape[0]):
        out_ref[i] = total.astype(BF)


def place_body(got_ref, other_ref, share_ref, other_share_ref, basis_ref, out_ref):
    row = lax.axis_index("row")
    for layer, ref, share in ((row, got_ref, share_ref), (1 - row, other_ref, other_share_ref)):
        basis_ref[layer] = share[...]
        out = out_ref.at[layer]
        for k in range(4):
            value = ref[k].astype(F32)
            for j in range(9):
                start = 160 * j + 40 * k
                out[:, start : start + 40] = value[:, 40 * j : 40 * j + 40]


def on_device(x_input, pre_act, out_grad, conv_weight, q_prev):
    shape = jax.ShapeDtypeStruct
    whole = pl.BlockSpec(memory_space=pltpu.VMEM)
    far = pl.BlockSpec(memory_space=pltpu.HBM)
    images, rows, cols = (lax.axis_size(a) for a in ALL)
    z, row = lax.axis_index("dp"), lax.axis_index("row")
    plane = rows * cols
    x, act, g = (v.reshape(256, 640) for v in (x_input, pre_act, out_grad))
    q_t = q_prev.transpose(1, 2, 0).reshape(128, 5760)

    sems = pltpu.SemaphoreType.DMA
    rims = call(
        rim_body,
        shape((plane, 32, 640), BF),
        1 << 24,
        1 << 20,
        vmem=62,
        in_specs=[far] * 2,
        scratch_shapes=[pltpu.VMEM((256, 640), BF)] * 2 + [sems((2,))],
    )(x, g)
    got = exchange(rims, PLANE)
    slices, q_one, y_two, slope = call(
        prepare_body,
        (
            shape((8, 160, 256), BF),
            shape((3, 384, 640), BF),
            shape((3, 128, 384), BF),
            shape((256, 640), F32),
        ),
        2 * 1152 * 640 * 256,
        8 << 20,
        vmem=62,
        in_specs=[far] * 3,
        scratch_shapes=[pltpu.VMEM((256, 640), BF)] * 2
        + [pltpu.VMEM((9, 128, 640), F32), sems((11,))],
    )(x, act, q_t)
    slices = exchange(slices, PLANE)

    strip = images * cols
    each = 64 // strip if 64 % strip == 0 and strip >= 8 else 8
    parts = 64 // each
    p_shape = shape((parts, each, 640), F32)
    keep, swap, p_keep, p_swap = call(
        power_body,
        (shape((256, 640), BF), shape((256, 640), BF), p_shape, p_shape),
        2 * 256 * 5760 * 1100,
        12 << 20,
        vmem=62,
        in_specs=[far] * 7,
        scratch_shapes=[
            pltpu.VMEM((256, 640), BF),
            pltpu.VMEM((256, 640), BF),
            pltpu.VMEM((plane, 32, 640), BF),
            pltpu.VMEM((256, 640), F32),
            pltpu.VMEM((3, 384, 640), BF),
            pltpu.VMEM((3, 128, 384), BF),
            pltpu.VMEM((9, 640, 640), BF),
            pltpu.VMEM((3, 288, 640), BF),
            pltpu.VMEM((3, 288, 640), BF),
            pltpu.VMEM((256, 640), F32),
            sems((15,)),
        ],
    )(x, g, got, slope, q_one, y_two, conv_weight)

    across = [(0, 1), (1, 0)]
    p_part = call(add_body, p_shape, 0, 1 << 20)(p_keep, lax.ppermute(p_swap, "row", across))
    swap = lax.ppermute(swap, "row", across)
    p_part, slices = lax.optimization_barrier((p_part, slices))
    if parts == strip:
        p_got = exchange(p_part, ("dp", "col"))
        p_got = call(sum_body, p_shape, 0, 1 << 20)(p_got, keep, swap)
        p_own = exchange(p_got, ("dp", "col"))
    else:
        p_own = lax.psum(p_part, ("dp", "col"))

    w_own, p_t = call(
        project_body,
        (shape((4, 512, 128), BF), shape((64, 640), F32)),
        2 * 512 * 640 * 128,
        2 << 20,
    )(p_own, keep, swap)
    w_all = exchange(w_own, ("col",))
    inverse, basis, share = call(
        factor_body,
        (shape((64, 64), F32), shape((64, 640), F32), shape((64, 160), F32)),
        1 << 30,
        1 << 20,
    )(p_t)

    sums = call(
        taps_body,
        shape((4, 64, 384), BF),
        2 * 160 * 2048 * 1152,
        2 << 20,
        scratch_shapes=[pltpu.VMEM((34, 4, 16, 384), BF), pltpu.VMEM((1472, 128), F32)],
    )(w_all, slices, inverse)

    if images == 4:
        other_share = lax.ppermute(share, "row", across)
        sums = exchange(sums, ("dp",))
        mine = call(total_body, shape((cols, 64, 384), BF), 0, 1 << 20)(sums)
        every = exchange(mine, ("col",))
        other = lax.ppermute(every, "row", across)
        basis_out, q_out = call(
            place_body, (shape((2, 64, 160), F32), shape((2, 64, 1440), F32)), 0, 1 << 20
        )(every, other, share, other_share)
        return basis_out.transpose(2, 0, 1), q_out.transpose(2, 0, 1)
    sums = lax.psum(sums[:, :, :360].astype(F32), "dp")
    every = lax.all_gather(sums, PLANE).reshape(rows, cols, 4, 64, 9, 40)
    every = every.transpose(2, 4, 1, 5, 0, 3).reshape(5760, 2, 64)
    q_out = lax.dynamic_slice_in_dim(every, z * (5760 // images), 5760 // images, 0)
    bases = lax.all_gather(basis, "row").transpose(2, 0, 1)
    return lax.dynamic_slice_in_dim(bases, z * (640 // images), 640 // images, 0), q_out


def solution(mesh):
    tiles = P("dp", "row", "col", None)
    return jax.shard_map(
        on_device,
        mesh=mesh,
        in_specs=(tiles, tiles, tiles, P(), P()),
        out_specs=(P("dp", None, None), P("dp", None, None)),
        check_vma=False,
    )
```

```python
import functools

import jax
import jax.numpy as jnp
from jax import lax
from jax.experimental import pallas as pl
from jax.experimental.pallas import tpu as pltpu
from jax.sharding import PartitionSpec as P

PLANE = ("row", "col")
ALL = ("dp", "row", "col")
BF = jnp.bfloat16
F32 = jnp.float32
NN = ((1,), (0,))
NT = ((1,), (1,))
TN = ((0,), (0,))
MIB = 1024 * 1024


def dot(left, right, dims, precision=None):
    return lax.dot_general(
        left, right, (dims, ((), ())), precision=precision, preferred_element_type=F32
    )


def call(body, out, flops, moved, vmem=40, **extra):
    return pl.pallas_call(
        body,
        out_shape=out,
        cost_estimate=pl.CostEstimate(flops=flops, bytes_accessed=moved, transcendentals=0),
        compiler_params=pltpu.CompilerParams(vmem_limit_bytes=vmem * MIB),
        **extra,
    )


def exchange(chunks, axes):
    return lax.all_to_all(chunks, axes, 0, 0, tiled=True)


def shifts(values, axis):
    size = lax.axis_size(axis)
    moved = [values[0]]
    for s in range(1, len(values)):
        moved.append(lax.ppermute(values[s], axis, [(i, (i + s) % size) for i in range(size)]))
    return moved


def stacked_halves(value):
    high = value.astype(BF)
    return jnp.concatenate([high, (value - high.astype(F32)).astype(BF)], axis=0)


def paired_halves(value):
    total = value + pltpu.roll(value, 64, 1)
    high = total.astype(BF).astype(F32)
    lane = lax.broadcasted_iota(jnp.int32, value.shape, 1)
    return jnp.where(lane < 64, high, total - high)


def fetch(pairs, sems):
    copies = [pltpu.make_async_copy(src, dst, sems.at[i]) for i, (src, dst) in enumerate(pairs)]
    for copy in copies:
        copy.start()
    return copies


def rim_body(x_hbm, g_hbm, out_ref, x_ref, g_ref, sems):
    copies = fetch(((x_hbm, x_ref), (g_hbm, g_ref)), sems)
    row, col = lax.axis_index("row"), lax.axis_index("col")
    cols = out_ref.shape[0] // 2
    line = lax.broadcasted_iota(jnp.int32, (48, 256), 0)
    lane = lax.broadcasted_iota(jnp.int32, (48, 256), 1)
    ends = jnp.where(line < 32, 16 * (line % 16) + 15 * (line // 16), 240 * (1 - row) + line - 32)
    pick = jnp.where(lane == ends, 1.0, 0.0).astype(BF)
    for i, ref in enumerate((x_ref, g_ref)):
        copies[i].wait()
        rims = dot(pick, ref[...], NN)
        first, last, edge = rims[:16], rims[16:32], rims[32:]
        span = slice(16 * i, 16 * i + 16)
        for r in range(2):
            for c in range(cols):
                along = jnp.where(c > col, last, first)
                out_ref[r * cols + c, span] = jnp.where(row == r, along, edge).astype(BF)


def rim_pick(row, col, cols, s, first, count, start, width):
    cell = first + lax.broadcasted_iota(jnp.int32, (count, width), 0)
    lane = start + lax.broadcasted_iota(jnp.int32, (count, width), 1)
    y, x = cell // 16 - 1, cell % 16 + s - 1
    up = jnp.where(y < 0, -1, jnp.where(y > 15, 1, 0))
    side = jnp.where(x < 0, -1, jnp.where(x > 15, 1, 0))
    there_r, there_c = row + up, col + side
    inside = (there_r >= 0) & (there_r < 2) & (there_c >= 0) & (there_c < cols)
    got = 256 + (there_r * cols + there_c) * 16 + jnp.where(up != 0, x - 16 * side, y)
    index = jnp.where((up == 0) & (side == 0), 16 * y + x, got)
    hit = inside & (index == lane)
    return jnp.where(hit, 1.0, 0.0).astype(BF)


def prepare_body(
    x_hbm, act_hbm, q_hbm, slices_ref, q_one_ref, y_ref, slope_ref, x_ref, act_ref, q_all, sems
):
    pairs = [(x_hbm, x_ref), (act_hbm, act_ref)]
    pairs += [(q_hbm.at[:, 640 * t : 640 * t + 640], q_all.at[t]) for t in range(9)]
    copies = fetch(pairs, sems)
    copies[0].wait()
    copies[1].wait()
    act = act_ref[...].astype(F32)
    sigma = 1.0 / (1.0 + jnp.exp(-act))
    hidden = (act * sigma).astype(BF)
    slope_ref[...] = sigma * (1.0 + act * (1.0 - sigma))
    for layer, value in enumerate((x_ref[...], hidden)):
        turned = value.astype(F32).T
        for k in range(4):
            pieces = [turned[160 * j + 40 * k : 160 * j + 40 * k + 40] for j in range(4)]
            slices_ref[4 * layer + k] = jnp.concatenate(pieces, axis=0).astype(BF)
    for b in range(3):
        shifted = jnp.zeros((64, 384), F32)
        for a in range(3):
            t = 3 * a + b
            copies[2 + t].wait()
            q = q_all[t]
            q_one_ref[b, 128 * a : 128 * a + 128] = stacked_halves(q[:64])
            y = dot(stacked_halves(q[64:]), hidden, NT)
            y = jnp.concatenate([y[:64] + y[64:], jnp.zeros((64, 128), F32)], axis=1)
            shifted = shifted + (pltpu.roll(y, 16 * (2 - a), 1) if a < 2 else y)
        y_ref[b] = stacked_halves(shifted)


def power_body(
    x_hbm, g_hbm, got_hbm, slope_hbm, q_hbm, y_hbm, w_hbm,
    keep_ref, swap_ref, p_keep_ref, p_swap_ref,
    x_ref, g_ref, got_ref, slope_ref, q_ref, y_ref, w_all,
    x_win, g_win, back, sems,
):
    pairs = [(got_hbm, got_ref), (g_hbm, g_ref), (x_hbm, x_ref)]
    pairs += [(y_hbm, y_ref), (q_hbm, q_ref), (slope_hbm, slope_ref)]
    pairs += [(w_hbm.at[t // 3, t % 3], w_all.at[t]) for t in range(9)]
    copies = fetch(pairs, sems)
    row, col = lax.axis_index("row"), lax.axis_index("col")
    cols = got_ref.shape[0] // 2
    width = 256 + 32 * cols
    picks = [rim_pick(row, col, cols, s, 0, 288, 0, width) for s in (0, 2)]
    ends = [rim_pick(row, col, cols, 1, r, 16, 256, 32 * cols) for r in (0, 272)]
    picks = [picks[0], jnp.concatenate(ends, axis=0), picks[1]]
    copies[0].wait()
    for i, (ref, win) in enumerate(((g_ref, g_win), (x_ref, x_win))):
        copies[1 + i].wait()
        rims = got_ref[:, 16 - 16 * i : 32 - 16 * i, :].reshape(-1, 640)
        lines = dot(picks[1], rims, NN).astype(BF)
        win[1, 0:16] = lines[:16]
        win[1, 16:272] = ref[...]
        win[1, 272:288] = lines[16:]
        cells = jnp.concatenate([ref[...], rims], axis=0)
        for s in (0, 2):
            win[s] = dot(picks[s], cells, NN).astype(BF)
    copies[3].wait()
    copies[4].wait()
    two, z_sum = 0.0, 0.0
    for b in range(3):
        two = two + dot(y_ref[b][:, :288], g_win[2 - b], NN)
        wide = dot(x_win[b], q_ref[b], NT)
        for a in range(3):
            z_sum = z_sum + wide[16 * a : 16 * a + 256, 128 * a : 128 * a + 128]
    z_sum = paired_halves(z_sum).astype(BF)
    for a in range(3):
        windows = [g_win[2 - b, 16 * (2 - a) : 16 * (2 - a) + 256, :] for b in range(3)]
        for b in range(3):
            copies[6 + 3 * a + b].wait()
        taps = jnp.concatenate([w_all[3 * a + b] for b in range(3)], axis=1)
        term = dot(jnp.concatenate(windows, axis=1), taps, NT)
        back[...] = term if a == 0 else back[...] + term
    copies[5].wait()
    grad = (back[...] * slope_ref[...]).astype(BF)
    keep_ref[...] = jnp.where(row == 0, grad, g_ref[...])
    swap_ref[...] = jnp.where(row == 0, g_ref[...], grad)
    one = dot(z_sum, grad, TN)
    one, two = one[:64] + one[64:], two[:64] + two[64:]
    each = p_keep_ref.shape[1]
    for ref, value in (
        (p_keep_ref, jnp.where(row == 0, one, two)),
        (p_swap_ref, jnp.where(row == 0, two, one)),
    ):
        for i in range(64 // each):
            ref[i] = value[i * each : (i + 1) * each]


def add_body(left_ref, right_ref, out_ref):
    out_ref[...] = left_ref[...] + right_ref[...]


def sum_body(got_ref, keep_ref, swap_ref, out_ref):
    total = jnp.sum(got_ref[...], axis=0)
    for i in range(out_ref.shape[0]):
        out_ref[i] = total


def project_body(got_ref, keep_ref, swap_ref, w_ref, p_ref):
    row = lax.axis_index("row")
    each = got_ref.shape[1]
    for i in range(8):
        rows = [got_ref[i * (8 // each) + j] for j in range(8 // each)]
        p_ref[8 * i : 8 * i + 8, :] = jnp.concatenate(rows, axis=0)
    factor = stacked_halves(p_ref[...])
    for start, ref in ((row, keep_ref), (1 - row, swap_ref)):
        out = paired_halves(dot(ref[...], factor, NT)).astype(BF)
        w_ref[pl.ds(pl.multiple_of(256 * start, 256), 256), :] = out


def factor_body(p_ref, inverse_ref, basis_ref, share_ref):
    high = lax.Precision.HIGHEST
    line = lax.broadcasted_iota(jnp.int32, (64, 128), 0)
    lane = lax.broadcasted_iota(jnp.int32, (64, 128), 1)
    p = p_ref[...]
    unit = jnp.where(lane == line + 64, 1.0, 0.0)
    table = jnp.concatenate([dot(p, p, NT, high), unit[:, 64:]], axis=1)
    for k in range(64):
        pivot_row = table[k : k + 1, :]
        scaled = pivot_row / pivot_row[:, k : k + 1]
        column = jnp.where(line[:, :1] > k, table[:, k : k + 1], 0.0)
        table = table - column * scaled
    pivots = jnp.sum(jnp.where(line == lane, table, 0.0), axis=1, keepdims=True)
    inverse = table[:, 64:] / jnp.sqrt(pivots)
    inverse_ref[...] = inverse
    basis = dot(inverse, p, NN, high)
    basis_ref[...] = basis
    z = lax.axis_index("dp")
    part = basis[:, :160]
    for i in range(1, 4):
        part = jnp.where(z == i, basis[:, 160 * i : 160 * i + 160], part)
    share_ref[...] = part


def taps_body(own_order, *refs):
    w_refs, (x_ref, inverse_ref) = refs[:4], refs[4:6]
    out_refs, (w_ref, image, sums) = refs[6:10], refs[10:]
    col = lax.axis_index("col")
    for s in range(4):
        w_ref[lax.rem(col + 4 - s, 4)] = w_refs[s][...]
    zero = jnp.zeros((1, 4, 16, 384), BF)
    image[0:1] = zero
    image[33:34] = zero
    at = lax.broadcasted_iota(jnp.int32, (2048, 128), 0) % 64
    strips = [w_ref[c].astype(F32).reshape(32, 16, 128) for c in range(4)]
    flat = jnp.stack(strips, axis=1).reshape(2048, 128)
    left = jnp.where(at == 63, 0.0, pltpu.roll(flat, 2047, 0))
    right = jnp.where(at == 0, 0.0, pltpu.roll(flat, 1, 0))
    for i, value in enumerate((left, flat, right)):
        value = value.astype(BF).reshape(32, 4, 16, 128)
        image[1:33, :, :, 128 * i : 128 * i + 128] = value
    slices = jnp.concatenate([x_ref[4 * r + c] for c in range(4) for r in range(2)], axis=1)
    for a in range(3):
        windows = [image[2 - a : 34 - a, c].reshape(512, 384) for c in range(4)]
        total = dot(slices, jnp.concatenate(windows, axis=0), NN)
        for b in range(3):
            t = 3 * a + b
            value = total[:, 128 * b : 128 * b + 128]
            sums[160 * t : 160 * t + 160, :] = value + pltpu.roll(value, 64, 1)
    sums[1440:1472, :] = jnp.zeros((32, 128), F32)
    inverse = inverse_ref[...]
    for s in range(4):
        i = lax.rem(lax.axis_index("dp") + s, 4) if own_order else s
        part = sums[pl.ds(pl.multiple_of(360 * i, 8), 384), :][:, :64]
        out_refs[s][...] = dot(inverse, part, NT, lax.Precision.HIGHEST).astype(BF)


def total_body(a_ref, b_ref, c_ref, d_ref, out_ref):
    total = a_ref[...].astype(F32) + b_ref[...].astype(F32)
    total = total + (c_ref[...].astype(F32) + d_ref[...].astype(F32))
    out_ref[...] = total.astype(BF)


def place_body(*refs):
    own, other, shares = refs[:4], refs[4:8], refs[8:10]
    basis_ref, out_ref, held = refs[10:]
    row, col = lax.axis_index("row"), lax.axis_index("col")
    for layer, parts, share in ((row, own, shares[0]), (1 - row, other, shares[1])):
        basis_ref[layer] = share[...]
        for s in range(4):
            held[layer, lax.rem(col + 4 - s, 4)] = parts[s][...]
    for layer in range(2):
        for k in range(4):
            value = held[layer, k].astype(F32)
            for j in range(9):
                start = 160 * j + 40 * k
                out_ref[layer, :, start : start + 40] = value[:, 40 * j : 40 * j + 40]


def on_device(x_input, pre_act, out_grad, conv_weight, q_prev):
    shape = jax.ShapeDtypeStruct
    whole = pl.BlockSpec(memory_space=pltpu.VMEM)
    far = pl.BlockSpec(memory_space=pltpu.HBM)
    images, rows, cols = (lax.axis_size(a) for a in ALL)
    z, row = lax.axis_index("dp"), lax.axis_index("row")
    plane = rows * cols
    x, act, g = (v.reshape(256, 640) for v in (x_input, pre_act, out_grad))
    q_t = q_prev.transpose(1, 2, 0).reshape(128, 5760)

    sems = pltpu.SemaphoreType.DMA
    rims = call(
        rim_body,
        shape((plane, 32, 640), BF),
        1 << 24,
        1 << 20,
        vmem=62,
        in_specs=[far] * 2,
        scratch_shapes=[pltpu.VMEM((256, 640), BF)] * 2 + [sems((2,))],
    )(x, g)
    got = exchange(rims, PLANE)
    slices, q_one, y_two, slope = call(
        prepare_body,
        (
            shape((8, 160, 256), BF),
            shape((3, 384, 640), BF),
            shape((3, 128, 384), BF),
            shape((256, 640), F32),
        ),
        2 * 1152 * 640 * 256,
        8 << 20,
        vmem=62,
        in_specs=[far] * 3,
        scratch_shapes=[pltpu.VMEM((256, 640), BF)] * 2
        + [pltpu.VMEM((9, 128, 640), F32), sems((11,))],
    )(x, act, q_t)
    slices = exchange(slices, PLANE)

    strip = images * cols
    each = 64 // strip if 64 % strip == 0 and strip >= 8 else 8
    parts = 64 // each
    p_shape = shape((parts, each, 640), F32)
    keep, swap, p_keep, p_swap = call(
        power_body,
        (shape((256, 640), BF), shape((256, 640), BF), p_shape, p_shape),
        2 * 256 * 5760 * 1100,
        12 << 20,
        vmem=62,
        in_specs=[far] * 7,
        scratch_shapes=[
            pltpu.VMEM((256, 640), BF),
            pltpu.VMEM((256, 640), BF),
            pltpu.VMEM((plane, 32, 640), BF),
            pltpu.VMEM((256, 640), F32),
            pltpu.VMEM((3, 384, 640), BF),
            pltpu.VMEM((3, 128, 384), BF),
            pltpu.VMEM((9, 640, 640), BF),
            pltpu.VMEM((3, 288, 640), BF),
            pltpu.VMEM((3, 288, 640), BF),
            pltpu.VMEM((256, 640), F32),
            sems((15,)),
        ],
    )(x, g, got, slope, q_one, y_two, conv_weight)

    across = [(0, 1), (1, 0)]
    p_part = call(add_body, p_shape, 0, 1 << 20)(p_keep, lax.ppermute(p_swap, "row", across))
    swap = lax.ppermute(swap, "row", across)
    p_part, slices = lax.optimization_barrier((p_part, slices))
    if parts == strip:
        p_got = exchange(p_part, ("dp", "col"))
        p_got = call(sum_body, p_shape, 0, 1 << 20)(p_got, keep, swap)
        p_own = exchange(p_got, ("dp", "col"))
    else:
        p_own = lax.psum(p_part, ("dp", "col"))

    w_own, p_t = call(
        project_body,
        (shape((512, 128), BF), shape((64, 640), F32)),
        2 * 512 * 640 * 128,
        2 << 20,
    )(p_own, keep, swap)
    w_all = shifts([w_own] * 4, "col")
    inverse, basis, share = call(
        factor_body,
        (shape((64, 64), F32), shape((64, 640), F32), shape((64, 160), F32)),
        1 << 30,
        1 << 20,
    )(p_t)

    sums = call(
        functools.partial(taps_body, images == 4),
        (shape((64, 384), BF),) * 4,
        2 * 160 * 2048 * 1152,
        2 << 20,
        scratch_shapes=[
            pltpu.VMEM((4, 512, 128), BF),
            pltpu.VMEM((34, 4, 16, 384), BF),
            pltpu.VMEM((1472, 128), F32),
        ],
    )(*w_all, slices, inverse)

    if images == 4:
        other_share = lax.ppermute(share, "row", across)
        mine = call(total_body, shape((64, 384), BF), 0, 1 << 20)(*shifts(sums, "dp"))
        every = shifts([mine] * 4, "col")
        other = [lax.ppermute(part, "row", across) for part in every]
        basis_out, q_out = call(
            place_body,
            (shape((2, 64, 160), F32), shape((2, 64, 1440), F32)),
            0,
            1 << 20,
            scratch_shapes=[pltpu.VMEM((2, 4, 64, 384), BF)],
        )(*every, *other, share, other_share)
        return basis_out.transpose(2, 0, 1), q_out.transpose(2, 0, 1)
    sums = jnp.stack(sums)
    sums = lax.psum(sums[:, :, :360].astype(F32), "dp")
    every = lax.all_gather(sums, PLANE).reshape(rows, cols, 4, 64, 9, 40)
    every = every.transpose(2, 4, 1, 5, 0, 3).reshape(5760, 2, 64)
    q_out = lax.dynamic_slice_in_dim(every, z * (5760 // images), 5760 // images, 0)
    bases = lax.all_gather(basis, "row").transpose(2, 0, 1)
    return lax.dynamic_slice_in_dim(bases, z * (640 // images), 640 // images, 0), q_out


def solution(mesh):
    tiles = P("dp", "row", "col", None)
    return jax.shard_map(
        on_device,
        mesh=mesh,
        in_specs=(tiles, tiles, tiles, P(), P()),
        out_specs=(P("dp", None, None), P("dp", None, None)),
        check_vma=False,
    )
```

```python
import functools

import jax
import jax.numpy as jnp
from jax import lax
from jax.experimental import pallas as pl
from jax.experimental.pallas import tpu as pltpu
from jax.sharding import PartitionSpec as P

PLANE = ("row", "col")
ALL = ("dp", "row", "col")
BF = jnp.bfloat16
F32 = jnp.float32
NN = ((1,), (0,))
NT = ((1,), (1,))
TN = ((0,), (0,))
MIB = 1024 * 1024


def dot(left, right, dims, precision=None):
    return lax.dot_general(
        left, right, (dims, ((), ())), precision=precision, preferred_element_type=F32
    )


def call(body, out, flops, moved, vmem=40, **extra):
    return pl.pallas_call(
        body,
        out_shape=out,
        cost_estimate=pl.CostEstimate(flops=flops, bytes_accessed=moved, transcendentals=0),
        compiler_params=pltpu.CompilerParams(vmem_limit_bytes=vmem * MIB),
        **extra,
    )


def exchange(chunks, axes):
    return lax.all_to_all(chunks, axes, 0, 0, tiled=True)


def shifts(values, axis):
    size = lax.axis_size(axis)
    moved = [values[0]]
    for s in range(1, len(values)):
        moved.append(lax.ppermute(values[s], axis, [(i, (i + s) % size) for i in range(size)]))
    return moved


def stacked_halves(value):
    high = value.astype(BF)
    return jnp.concatenate([high, (value - high.astype(F32)).astype(BF)], axis=0)


def paired_halves(value):
    total = value + pltpu.roll(value, 64, 1)
    high = total.astype(BF).astype(F32)
    lane = lax.broadcasted_iota(jnp.int32, value.shape, 1)
    return jnp.where(lane < 64, high, total - high)


def fetch(pairs, sems):
    copies = [pltpu.make_async_copy(src, dst, sems.at[i]) for i, (src, dst) in enumerate(pairs)]
    for copy in copies:
        copy.start()
    return copies


def rim_body(x_hbm, g_hbm, out_ref, x_ref, g_ref, sems):
    copies = fetch(((x_hbm, x_ref), (g_hbm, g_ref)), sems)
    row, col = lax.axis_index("row"), lax.axis_index("col")
    cols = out_ref.shape[0] // 2
    line = lax.broadcasted_iota(jnp.int32, (48, 256), 0)
    lane = lax.broadcasted_iota(jnp.int32, (48, 256), 1)
    ends = jnp.where(line < 32, 16 * (line % 16) + 15 * (line // 16), 240 * (1 - row) + line - 32)
    pick = jnp.where(lane == ends, 1.0, 0.0).astype(BF)
    for i, ref in enumerate((x_ref, g_ref)):
        copies[i].wait()
        rims = dot(pick, ref[...], NN)
        first, last, edge = rims[:16], rims[16:32], rims[32:]
        span = slice(16 * i, 16 * i + 16)
        for r in range(2):
            for c in range(cols):
                along = jnp.where(c > col, last, first)
                out_ref[r * cols + c, span] = jnp.where(row == r, along, edge).astype(BF)


def rim_pick(row, col, cols, s, first, count, start, width):
    cell = first + lax.broadcasted_iota(jnp.int32, (count, width), 0)
    lane = start + lax.broadcasted_iota(jnp.int32, (count, width), 1)
    y, x = cell // 16 - 1, cell % 16 + s - 1
    up = jnp.where(y < 0, -1, jnp.where(y > 15, 1, 0))
    side = jnp.where(x < 0, -1, jnp.where(x > 15, 1, 0))
    there_r, there_c = row + up, col + side
    inside = (there_r >= 0) & (there_r < 2) & (there_c >= 0) & (there_c < cols)
    got = 256 + (there_r * cols + there_c) * 16 + jnp.where(up != 0, x - 16 * side, y)
    index = jnp.where((up == 0) & (side == 0), 16 * y + x, got)
    hit = inside & (index == lane)
    return jnp.where(hit, 1.0, 0.0).astype(BF)


def prepare_body(
    x_hbm, act_hbm, q_hbm, slices_ref, q_one_ref, y_ref, slope_ref, x_ref, act_ref, q_all, sems
):
    pairs = [(x_hbm, x_ref), (act_hbm, act_ref)]
    pairs += [(q_hbm.at[:, 640 * t : 640 * t + 640], q_all.at[t]) for t in range(9)]
    copies = fetch(pairs, sems)
    copies[0].wait()
    copies[1].wait()
    act = act_ref[...].astype(F32)
    sigma = 1.0 / (1.0 + jnp.exp(-act))
    hidden = (act * sigma).astype(BF)
    slope_ref[...] = sigma * (1.0 + act * (1.0 - sigma))
    for layer, value in enumerate((x_ref[...], hidden)):
        turned = value.astype(F32).T
        for k in range(4):
            pieces = [turned[160 * j + 40 * k : 160 * j + 40 * k + 40] for j in range(4)]
            slices_ref[4 * layer + k] = jnp.concatenate(pieces, axis=0).astype(BF)
    for b in range(3):
        shifted = jnp.zeros((64, 384), F32)
        for a in range(3):
            t = 3 * a + b
            copies[2 + t].wait()
            q = q_all[t]
            q_one_ref[b, 128 * a : 128 * a + 128] = stacked_halves(q[:64])
            y = dot(stacked_halves(q[64:]), hidden, NT)
            y = jnp.concatenate([y[:64] + y[64:], jnp.zeros((64, 128), F32)], axis=1)
            shifted = shifted + (pltpu.roll(y, 16 * (2 - a), 1) if a < 2 else y)
        y_ref[b] = stacked_halves(shifted)


def power_body(
    x_hbm, g_hbm, got_hbm, slope_hbm, q_hbm, y_hbm, w_hbm,
    keep_ref, swap_ref, p_keep_ref, p_swap_ref,
    x_ref, g_ref, got_ref, slope_ref, q_ref, y_ref, w_all,
    x_win, g_win, back, sems,
):
    pairs = [(got_hbm, got_ref), (g_hbm, g_ref), (x_hbm, x_ref)]
    pairs += [(y_hbm, y_ref), (q_hbm, q_ref), (slope_hbm, slope_ref)]
    pairs += [(w_hbm.at[t // 3, t % 3], w_all.at[t]) for t in range(9)]
    copies = fetch(pairs, sems)
    row, col = lax.axis_index("row"), lax.axis_index("col")
    cols = got_ref.shape[0] // 2
    width = 256 + 32 * cols
    picks = [rim_pick(row, col, cols, s, 0, 288, 0, width) for s in (0, 2)]
    ends = [rim_pick(row, col, cols, 1, r, 16, 256, 32 * cols) for r in (0, 272)]
    picks = [picks[0], jnp.concatenate(ends, axis=0), picks[1]]
    copies[0].wait()
    for i, (ref, win) in enumerate(((g_ref, g_win), (x_ref, x_win))):
        copies[1 + i].wait()
        rims = got_ref[:, 16 - 16 * i : 32 - 16 * i, :].reshape(-1, 640)
        lines = dot(picks[1], rims, NN).astype(BF)
        win[1, 0:16] = lines[:16]
        win[1, 16:272] = ref[...]
        win[1, 272:288] = lines[16:]
        cells = jnp.concatenate([ref[...], rims], axis=0)
        for s in (0, 2):
            win[s] = dot(picks[s], cells, NN).astype(BF)
    copies[3].wait()
    copies[4].wait()
    two, z_sum = 0.0, 0.0
    for b in range(3):
        two = two + dot(y_ref[b][:, :288], g_win[2 - b], NN)
        wide = dot(x_win[b], q_ref[b], NT)
        for a in range(3):
            z_sum = z_sum + wide[16 * a : 16 * a + 256, 128 * a : 128 * a + 128]
    z_sum = paired_halves(z_sum).astype(BF)
    for a in range(3):
        windows = [g_win[2 - b, 16 * (2 - a) : 16 * (2 - a) + 256, :] for b in range(3)]
        for b in range(3):
            copies[6 + 3 * a + b].wait()
        taps = jnp.concatenate([w_all[3 * a + b] for b in range(3)], axis=1)
        term = dot(jnp.concatenate(windows, axis=1), taps, NT)
        back[...] = term if a == 0 else back[...] + term
    copies[5].wait()
    grad = (back[...] * slope_ref[...]).astype(BF)
    keep_ref[...] = jnp.where(row == 0, grad, g_ref[...])
    swap_ref[...] = jnp.where(row == 0, g_ref[...], grad)
    one = dot(z_sum, grad, TN)
    one, two = one[:64] + one[64:], two[:64] + two[64:]
    each = p_keep_ref.shape[1]
    for ref, value in (
        (p_keep_ref, jnp.where(row == 0, one, two)),
        (p_swap_ref, jnp.where(row == 0, two, one)),
    ):
        for i in range(64 // each):
            ref[i] = value[i * each : (i + 1) * each]


def add_body(left_ref, right_ref, out_ref):
    out_ref[...] = left_ref[...] + right_ref[...]


def stage_body(keep_ref, out_ref):
    out_ref[...] = keep_ref[...]


def sum_body(got_ref, out_ref):
    total = jnp.sum(got_ref[...], axis=0)
    for i in range(out_ref.shape[0]):
        out_ref[i] = total


def project_body(got_ref, keep_ref, swap_ref, w_ref, p_ref):
    row = lax.axis_index("row")
    each = got_ref.shape[1]
    for i in range(8):
        rows = [got_ref[i * (8 // each) + j] for j in range(8 // each)]
        p_ref[8 * i : 8 * i + 8, :] = jnp.concatenate(rows, axis=0)
    factor = stacked_halves(p_ref[...])
    for start, ref in ((row, keep_ref), (1 - row, swap_ref)):
        out = paired_halves(dot(ref[...], factor, NT)).astype(BF)
        w_ref[pl.ds(pl.multiple_of(256 * start, 256), 256), :] = out


def factor_body(p_ref, inverse_ref, basis_ref, share_ref):
    high = lax.Precision.HIGHEST
    line = lax.broadcasted_iota(jnp.int32, (64, 128), 0)
    lane = lax.broadcasted_iota(jnp.int32, (64, 128), 1)
    p = p_ref[...]
    unit = jnp.where(lane == line + 64, 1.0, 0.0)
    table = jnp.concatenate([dot(p, p, NT, high), unit[:, 64:]], axis=1)
    for k in range(0, 64, 2):
        row_a, row_b = table[k : k + 1, :], table[k + 1 : k + 2, :]
        col_a = jnp.broadcast_to(table[:, k : k + 1], (64, 128))
        col_b = jnp.broadcast_to(table[:, k + 1 : k + 2], (64, 128))
        over = 1.0 / col_a[k : k + 1, :]
        first = col_a * over
        cross = col_b[k : k + 1, :]
        row_b = row_b - first[k + 1 : k + 2, :] * row_a
        col_b = col_b - first * cross
        second = col_b * (1.0 / col_b[k + 1 : k + 2, :])
        first = jnp.where(line > k, first, 0.0)
        second = jnp.where(line > k + 1, second, 0.0)
        table = table - first * row_a - second * row_b
    pivots = jnp.sum(jnp.where(line == lane, table, 0.0), axis=1, keepdims=True)
    inverse = table[:, 64:] / jnp.sqrt(pivots)
    inverse_ref[...] = inverse
    basis = dot(inverse, p, NN, high)
    basis_ref[...] = basis
    z = lax.axis_index("dp")
    part = basis[:, :160]
    for i in range(1, 4):
        part = jnp.where(z == i, basis[:, 160 * i : 160 * i + 160], part)
    share_ref[...] = part


def taps_body(own_order, *refs):
    w_refs, (x_ref, inverse_ref) = refs[:4], refs[4:6]
    out_refs, (w_ref, image, sums) = refs[6:10], refs[10:]
    col = lax.axis_index("col")
    for s in range(4):
        w_ref[lax.rem(col + 4 - s, 4)] = w_refs[s][...]
    zero = jnp.zeros((1, 4, 16, 384), BF)
    image[0:1] = zero
    image[33:34] = zero
    at = lax.broadcasted_iota(jnp.int32, (2048, 128), 0) % 64
    strips = [w_ref[c].astype(F32).reshape(32, 16, 128) for c in range(4)]
    flat = jnp.stack(strips, axis=1).reshape(2048, 128)
    left = jnp.where(at == 63, 0.0, pltpu.roll(flat, 2047, 0))
    right = jnp.where(at == 0, 0.0, pltpu.roll(flat, 1, 0))
    for i, value in enumerate((left, flat, right)):
        value = value.astype(BF).reshape(32, 4, 16, 128)
        image[1:33, :, :, 128 * i : 128 * i + 128] = value
    slices = jnp.concatenate([x_ref[4 * r + c] for c in range(4) for r in range(2)], axis=1)
    for a in range(3):
        windows = [image[2 - a : 34 - a, c].reshape(512, 384) for c in range(4)]
        total = dot(slices, jnp.concatenate(windows, axis=0), NN)
        for b in range(3):
            t = 3 * a + b
            value = total[:, 128 * b : 128 * b + 128]
            sums[160 * t : 160 * t + 160, :] = value + pltpu.roll(value, 64, 1)
    sums[1440:1472, :] = jnp.zeros((32, 128), F32)
    inverse = inverse_ref[...]
    for s in range(4):
        i = lax.rem(lax.axis_index("dp") + s, 4) if own_order else s
        part = sums[pl.ds(pl.multiple_of(360 * i, 8), 384), :][:, :64]
        out_refs[s][...] = dot(inverse, part, NT, lax.Precision.HIGHEST).astype(BF)


def total_body(a_ref, b_ref, c_ref, d_ref, out_ref):
    total = a_ref[...].astype(F32) + b_ref[...].astype(F32)
    total = total + (c_ref[...].astype(F32) + d_ref[...].astype(F32))
    out_ref[...] = total.astype(BF)


def place_body(*refs):
    own, other, shares = refs[:4], refs[4:8], refs[8:10]
    basis_ref, out_ref, held = refs[10:]
    row, col = lax.axis_index("row"), lax.axis_index("col")
    for layer, parts, share in ((row, own, shares[0]), (1 - row, other, shares[1])):
        basis_ref[layer] = share[...]
        for s in range(4):
            held[layer, lax.rem(col + 4 - s, 4)] = parts[s][...]
    for layer in range(2):
        for k in range(4):
            value = held[layer, k].astype(F32)
            for j in range(9):
                start = 160 * j + 40 * k
                out_ref[layer, :, start : start + 40] = value[:, 40 * j : 40 * j + 40]


def on_device(x_input, pre_act, out_grad, conv_weight, q_prev):
    shape = jax.ShapeDtypeStruct
    whole = pl.BlockSpec(memory_space=pltpu.VMEM)
    far = pl.BlockSpec(memory_space=pltpu.HBM)
    images, rows, cols = (lax.axis_size(a) for a in ALL)
    z, row = lax.axis_index("dp"), lax.axis_index("row")
    plane = rows * cols
    x, act, g = (v.reshape(256, 640) for v in (x_input, pre_act, out_grad))
    q_t = q_prev.transpose(1, 2, 0).reshape(128, 5760)

    sems = pltpu.SemaphoreType.DMA
    rims = call(
        rim_body,
        shape((plane, 32, 640), BF),
        1 << 24,
        1 << 20,
        vmem=62,
        in_specs=[far] * 2,
        scratch_shapes=[pltpu.VMEM((256, 640), BF)] * 2 + [sems((2,))],
    )(x, g)
    got = exchange(rims, PLANE)
    slices, q_one, y_two, slope = call(
        prepare_body,
        (
            shape((8, 160, 256), BF),
            shape((3, 384, 640), BF),
            shape((3, 128, 384), BF),
            shape((256, 640), F32),
        ),
        2 * 1152 * 640 * 256,
        8 << 20,
        vmem=62,
        in_specs=[far] * 3,
        scratch_shapes=[pltpu.VMEM((256, 640), BF)] * 2
        + [pltpu.VMEM((9, 128, 640), F32), sems((11,))],
    )(x, act, q_t)
    slices = exchange(slices, PLANE)

    strip = images * cols
    each = 64 // strip if 64 % strip == 0 and strip >= 8 else 8
    parts = 64 // each
    p_shape = shape((parts, each, 640), F32)
    keep, swap, p_keep, p_swap = call(
        power_body,
        (shape((256, 640), BF), shape((256, 640), BF), p_shape, p_shape),
        2 * 256 * 5760 * 1100,
        12 << 20,
        vmem=62,
        in_specs=[far] * 7,
        scratch_shapes=[
            pltpu.VMEM((256, 640), BF),
            pltpu.VMEM((256, 640), BF),
            pltpu.VMEM((plane, 32, 640), BF),
            pltpu.VMEM((256, 640), F32),
            pltpu.VMEM((3, 384, 640), BF),
            pltpu.VMEM((3, 128, 384), BF),
            pltpu.VMEM((9, 640, 640), BF),
            pltpu.VMEM((3, 288, 640), BF),
            pltpu.VMEM((3, 288, 640), BF),
            pltpu.VMEM((256, 640), F32),
            sems((15,)),
        ],
    )(x, g, got, slope, q_one, y_two, conv_weight)

    across = [(0, 1), (1, 0)]
    p_part = call(add_body, p_shape, 0, 1 << 20)(p_keep, lax.ppermute(p_swap, "row", across))
    swap = lax.ppermute(swap, "row", across)
    keep = call(stage_body, shape((256, 640), BF), 0, 8 << 20)(keep)
    p_part, slices = lax.optimization_barrier((p_part, slices))
    if parts == strip:
        p_got = exchange(p_part, ("dp", "col"))
        p_got = call(sum_body, p_shape, 0, 1 << 20)(p_got)
        p_own = exchange(p_got, ("dp", "col"))
    else:
        p_own = lax.psum(p_part, ("dp", "col"))

    w_own, p_t = call(
        project_body,
        (shape((512, 128), BF), shape((64, 640), F32)),
        2 * 512 * 640 * 128,
        2 << 20,
    )(p_own, keep, swap)
    w_all = shifts([w_own] * 4, "col")
    inverse, basis, share = call(
        factor_body,
        (shape((64, 64), F32), shape((64, 640), F32), shape((64, 160), F32)),
        1 << 30,
        1 << 20,
    )(p_t)

    sums = call(
        functools.partial(taps_body, images == 4),
        (shape((64, 384), BF),) * 4,
        2 * 160 * 2048 * 1152,
        2 << 20,
        scratch_shapes=[
            pltpu.VMEM((4, 512, 128), BF),
            pltpu.VMEM((34, 4, 16, 384), BF),
            pltpu.VMEM((1472, 128), F32),
        ],
    )(*w_all, slices, inverse)

    if images == 4:
        other_share = lax.ppermute(share, "row", across)
        mine = call(total_body, shape((64, 384), BF), 0, 1 << 20)(*shifts(sums, "dp"))
        every = shifts([mine] * 4, "col")
        other = [lax.ppermute(part, "row", across) for part in every]
        basis_out, q_out = call(
            place_body,
            (shape((2, 64, 160), F32), shape((2, 64, 1440), F32)),
            0,
            1 << 20,
            scratch_shapes=[pltpu.VMEM((2, 4, 64, 384), BF)],
        )(*every, *other, share, other_share)
        return basis_out.transpose(2, 0, 1), q_out.transpose(2, 0, 1)
    sums = jnp.stack(sums)
    sums = lax.psum(sums[:, :, :360].astype(F32), "dp")
    every = lax.all_gather(sums, PLANE).reshape(rows, cols, 4, 64, 9, 40)
    every = every.transpose(2, 4, 1, 5, 0, 3).reshape(5760, 2, 64)
    q_out = lax.dynamic_slice_in_dim(every, z * (5760 // images), 5760 // images, 0)
    bases = lax.all_gather(basis, "row").transpose(2, 0, 1)
    return lax.dynamic_slice_in_dim(bases, z * (640 // images), 640 // images, 0), q_out


def solution(mesh):
    tiles = P("dp", "row", "col", None)
    return jax.shard_map(
        on_device,
        mesh=mesh,
        in_specs=(tiles, tiles, tiles, P(), P()),
        out_specs=(P("dp", None, None), P("dp", None, None)),
        check_vma=False,
    )
```

```python
import functools

import jax
import jax.numpy as jnp
from jax import lax
from jax.experimental import pallas as pl
from jax.experimental.pallas import tpu as pltpu
from jax.sharding import PartitionSpec as P

PLANE = ("row", "col")
ALL = ("dp", "row", "col")
BF = jnp.bfloat16
F32 = jnp.float32
NN = ((1,), (0,))
NT = ((1,), (1,))
TN = ((0,), (0,))
MIB = 1024 * 1024


def dot(left, right, dims, precision=None):
    return lax.dot_general(
        left, right, (dims, ((), ())), precision=precision, preferred_element_type=F32
    )


def call(body, out, flops, moved, vmem=40, **extra):
    return pl.pallas_call(
        body,
        out_shape=out,
        cost_estimate=pl.CostEstimate(flops=flops, bytes_accessed=moved, transcendentals=0),
        compiler_params=pltpu.CompilerParams(vmem_limit_bytes=vmem * MIB),
        **extra,
    )


def exchange(chunks, axes):
    return lax.all_to_all(chunks, axes, 0, 0, tiled=True)


def shifts(values, axis):
    size = lax.axis_size(axis)
    moved = [values[0]]
    for s in range(1, len(values)):
        moved.append(lax.ppermute(values[s], axis, [(i, (i + s) % size) for i in range(size)]))
    return moved


def stacked_halves(value):
    high = value.astype(BF)
    return jnp.concatenate([high, (value - high.astype(F32)).astype(BF)], axis=0)


def paired_halves(value):
    total = value + pltpu.roll(value, 64, 1)
    high = total.astype(BF).astype(F32)
    lane = lax.broadcasted_iota(jnp.int32, value.shape, 1)
    return jnp.where(lane < 64, high, total - high)


def fetch(pairs, sems):
    copies = [pltpu.make_async_copy(src, dst, sems.at[i]) for i, (src, dst) in enumerate(pairs)]
    for copy in copies:
        copy.start()
    return copies


def rim_body(x_hbm, g_hbm, out_ref, x_ref, g_ref, sems):
    copies = fetch(((x_hbm, x_ref), (g_hbm, g_ref)), sems)
    row, col = lax.axis_index("row"), lax.axis_index("col")
    cols = out_ref.shape[0] // 2
    line = lax.broadcasted_iota(jnp.int32, (48, 256), 0)
    lane = lax.broadcasted_iota(jnp.int32, (48, 256), 1)
    ends = jnp.where(line < 32, 16 * (line % 16) + 15 * (line // 16), 240 * (1 - row) + line - 32)
    pick = jnp.where(lane == ends, 1.0, 0.0).astype(BF)
    for i, ref in enumerate((x_ref, g_ref)):
        copies[i].wait()
        rims = dot(pick, ref[...], NN)
        first, last, edge = rims[:16], rims[16:32], rims[32:]
        span = slice(16 * i, 16 * i + 16)
        for r in range(2):
            for c in range(cols):
                along = jnp.where(c > col, last, first)
                out_ref[r * cols + c, span] = jnp.where(row == r, along, edge).astype(BF)


def rim_pick(row, col, cols, s, first, count, start, width):
    cell = first + lax.broadcasted_iota(jnp.int32, (count, width), 0)
    lane = start + lax.broadcasted_iota(jnp.int32, (count, width), 1)
    y, x = cell // 16 - 1, cell % 16 + s - 1
    up = jnp.where(y < 0, -1, jnp.where(y > 15, 1, 0))
    side = jnp.where(x < 0, -1, jnp.where(x > 15, 1, 0))
    there_r, there_c = row + up, col + side
    inside = (there_r >= 0) & (there_r < 2) & (there_c >= 0) & (there_c < cols)
    got = 256 + (there_r * cols + there_c) * 16 + jnp.where(up != 0, x - 16 * side, y)
    index = jnp.where((up == 0) & (side == 0), 16 * y + x, got)
    hit = inside & (index == lane)
    return jnp.where(hit, 1.0, 0.0).astype(BF)


def prepare_body(
    x_hbm, act_hbm, q_hbm, slices_ref, q_one_ref, y_ref, slope_ref, x_ref, act_ref, q_all, sems
):
    pairs = [(x_hbm, x_ref), (act_hbm, act_ref)]
    pairs += [(q_hbm.at[:, 640 * t : 640 * t + 640], q_all.at[t]) for t in range(9)]
    copies = fetch(pairs, sems)
    copies[0].wait()
    copies[1].wait()
    act = act_ref[...].astype(F32)
    sigma = 1.0 / (1.0 + jnp.exp(-act))
    hidden = (act * sigma).astype(BF)
    slope_ref[...] = sigma * (1.0 + act * (1.0 - sigma))
    for layer, value in enumerate((x_ref[...], hidden)):
        turned = value.astype(F32).T
        for k in range(4):
            pieces = [turned[160 * j + 40 * k : 160 * j + 40 * k + 40] for j in range(4)]
            slices_ref[4 * layer + k] = jnp.concatenate(pieces, axis=0).astype(BF)
    for b in range(3):
        shifted = jnp.zeros((64, 384), F32)
        for a in range(3):
            t = 3 * a + b
            copies[2 + t].wait()
            q = q_all[t]
            q_one_ref[b, 128 * a : 128 * a + 128] = stacked_halves(q[:64])
            y = dot(stacked_halves(q[64:]), hidden, NT)
            y = jnp.concatenate([y[:64] + y[64:], jnp.zeros((64, 128), F32)], axis=1)
            shifted = shifted + (pltpu.roll(y, 16 * (2 - a), 1) if a < 2 else y)
        y_ref[b] = stacked_halves(shifted)


def power_body(
    x_hbm, g_hbm, got_hbm, slope_hbm, q_hbm, y_hbm, w_hbm,
    keep_ref, swap_ref, p_keep_ref, p_swap_ref,
    x_ref, g_ref, got_ref, slope_ref, q_ref, y_ref, w_all,
    x_win, g_win, back, sems,
):
    pairs = [(got_hbm, got_ref), (g_hbm, g_ref), (x_hbm, x_ref)]
    pairs += [(y_hbm, y_ref), (q_hbm, q_ref), (slope_hbm, slope_ref)]
    pairs += [(w_hbm.at[t // 3, t % 3], w_all.at[t]) for t in range(9)]
    copies = fetch(pairs, sems)
    row, col = lax.axis_index("row"), lax.axis_index("col")
    cols = got_ref.shape[0] // 2
    width = 256 + 32 * cols
    picks = [rim_pick(row, col, cols, s, 0, 288, 0, width) for s in (0, 2)]
    ends = [rim_pick(row, col, cols, 1, r, 16, 256, 32 * cols) for r in (0, 272)]
    picks = [picks[0], jnp.concatenate(ends, axis=0), picks[1]]
    copies[0].wait()
    for i, (ref, win) in enumerate(((g_ref, g_win), (x_ref, x_win))):
        copies[1 + i].wait()
        rims = got_ref[:, 16 - 16 * i : 32 - 16 * i, :].reshape(-1, 640)
        lines = dot(picks[1], rims, NN).astype(BF)
        win[1, 0:16] = lines[:16]
        win[1, 16:272] = ref[...]
        win[1, 272:288] = lines[16:]
        cells = jnp.concatenate([ref[...], rims], axis=0)
        for s in (0, 2):
            win[s] = dot(picks[s], cells, NN).astype(BF)
    copies[3].wait()
    copies[4].wait()
    two, z_sum = 0.0, 0.0
    for b in range(3):
        two = two + dot(y_ref[b][:, :288], g_win[2 - b], NN)
        wide = dot(x_win[b], q_ref[b], NT)
        for a in range(3):
            z_sum = z_sum + wide[16 * a : 16 * a + 256, 128 * a : 128 * a + 128]
    z_sum = paired_halves(z_sum).astype(BF)
    for a in range(3):
        windows = [g_win[2 - b, 16 * (2 - a) : 16 * (2 - a) + 256, :] for b in range(3)]
        for b in range(3):
            copies[6 + 3 * a + b].wait()
        taps = jnp.concatenate([w_all[3 * a + b] for b in range(3)], axis=1)
        term = dot(jnp.concatenate(windows, axis=1), taps, NT)
        back[...] = term if a == 0 else back[...] + term
    copies[5].wait()
    grad = (back[...] * slope_ref[...]).astype(BF)
    keep_ref[...] = jnp.where(row == 0, grad, g_ref[...])
    swap_ref[...] = jnp.where(row == 0, g_ref[...], grad)
    one = dot(z_sum, grad, TN)
    one, two = one[:64] + one[64:], two[:64] + two[64:]
    each = p_keep_ref.shape[1]
    for ref, value in (
        (p_keep_ref, jnp.where(row == 0, one, two)),
        (p_swap_ref, jnp.where(row == 0, two, one)),
    ):
        for i in range(64 // each):
            ref[i] = value[i * each : (i + 1) * each]


def stage_body(keep_ref, out_ref):
    out_ref[...] = keep_ref[...]


def sum_body(got_ref, out_ref):
    total = jnp.sum(got_ref[...], axis=0)
    for i in range(out_ref.shape[0]):
        out_ref[i] = total


def project_body(got_ref, keep_ref, swap_ref, w_ref, p_ref):
    row = lax.axis_index("row")
    each = got_ref.shape[1]
    for i in range(8):
        rows = [got_ref[i * (8 // each) + j] for j in range(8 // each)]
        p_ref[8 * i : 8 * i + 8, :] = jnp.concatenate(rows, axis=0)
    factor = stacked_halves(p_ref[...])
    for start, ref in ((row, keep_ref), (1 - row, swap_ref)):
        out = paired_halves(dot(ref[...], factor, NT)).astype(BF)
        w_ref[pl.ds(pl.multiple_of(256 * start, 256), 256), :] = out


def factor_body(p_ref, inverse_ref, basis_ref, share_ref):
    high = lax.Precision.HIGHEST
    line = lax.broadcasted_iota(jnp.int32, (64, 128), 0)
    lane = lax.broadcasted_iota(jnp.int32, (64, 128), 1)
    p = p_ref[...]
    unit = jnp.where(lane == line + 64, 1.0, 0.0)
    table = jnp.concatenate([dot(p, p, NT, high), unit[:, 64:]], axis=1)
    for k in range(0, 64, 2):
        row_a, row_b = table[k : k + 1, :], table[k + 1 : k + 2, :]
        col_a = jnp.broadcast_to(table[:, k : k + 1], (64, 128))
        col_b = jnp.broadcast_to(table[:, k + 1 : k + 2], (64, 128))
        over = 1.0 / col_a[k : k + 1, :]
        first = col_a * over
        cross = col_b[k : k + 1, :]
        row_b = row_b - first[k + 1 : k + 2, :] * row_a
        col_b = col_b - first * cross
        second = col_b * (1.0 / col_b[k + 1 : k + 2, :])
        first = jnp.where(line > k, first, 0.0)
        second = jnp.where(line > k + 1, second, 0.0)
        table = table - first * row_a - second * row_b
    pivots = jnp.sum(jnp.where(line == lane, table, 0.0), axis=1, keepdims=True)
    inverse = table[:, 64:] / jnp.sqrt(pivots)
    inverse_ref[...] = inverse
    basis = dot(inverse, p, NN, high)
    basis_ref[...] = basis
    z = lax.axis_index("dp")
    part = basis[:, :160]
    for i in range(1, 4):
        part = jnp.where(z == i, basis[:, 160 * i : 160 * i + 160], part)
    share_ref[...] = part


def taps_body(own_order, *refs):
    w_refs, (x_ref, inverse_ref) = refs[:4], refs[4:6]
    out_refs, (w_ref, image, sums) = refs[6:10], refs[10:]
    col = lax.axis_index("col")
    for s in range(4):
        w_ref[lax.rem(col + 4 - s, 4)] = w_refs[s][...]
    zero = jnp.zeros((1, 4, 16, 384), BF)
    image[0:1] = zero
    image[33:34] = zero
    at = lax.broadcasted_iota(jnp.int32, (2048, 128), 0) % 64
    strips = [w_ref[c].astype(F32).reshape(32, 16, 128) for c in range(4)]
    flat = jnp.stack(strips, axis=1).reshape(2048, 128)
    left = jnp.where(at == 63, 0.0, pltpu.roll(flat, 2047, 0))
    right = jnp.where(at == 0, 0.0, pltpu.roll(flat, 1, 0))
    for i, value in enumerate((left, flat, right)):
        value = value.astype(BF).reshape(32, 4, 16, 128)
        image[1:33, :, :, 128 * i : 128 * i + 128] = value
    slices = jnp.concatenate([x_ref[4 * r + c] for c in range(4) for r in range(2)], axis=1)
    for a in range(3):
        windows = [image[2 - a : 34 - a, c].reshape(512, 384) for c in range(4)]
        total = dot(slices, jnp.concatenate(windows, axis=0), NN)
        for b in range(3):
            t = 3 * a + b
            value = total[:, 128 * b : 128 * b + 128]
            sums[160 * t : 160 * t + 160, :] = value + pltpu.roll(value, 64, 1)
    sums[1440:1472, :] = jnp.zeros((32, 128), F32)
    inverse = inverse_ref[...]
    for s in range(4):
        i = lax.rem(lax.axis_index("dp") + s, 4) if own_order else s
        part = sums[pl.ds(pl.multiple_of(360 * i, 8), 384), :][:, :64]
        out_refs[s][...] = dot(inverse, part, NT, lax.Precision.HIGHEST).astype(BF)


def total_body(a_ref, b_ref, c_ref, d_ref, out_ref):
    total = a_ref[...].astype(F32) + b_ref[...].astype(F32)
    total = total + (c_ref[...].astype(F32) + d_ref[...].astype(F32))
    out_ref[...] = total.astype(BF)


def place_body(*refs):
    own, other, shares = refs[:4], refs[4:8], refs[8:10]
    basis_ref, out_ref, held = refs[10:]
    row, col = lax.axis_index("row"), lax.axis_index("col")
    for layer, parts, share in ((row, own, shares[0]), (1 - row, other, shares[1])):
        basis_ref[layer] = share[...]
        for s in range(4):
            held[layer, lax.rem(col + 4 - s, 4)] = parts[s][...]
    for layer in range(2):
        for k in range(4):
            value = held[layer, k].astype(F32)
            for j in range(9):
                start = 160 * j + 40 * k
                out_ref[layer, :, start : start + 40] = value[:, 40 * j : 40 * j + 40]


def on_device(x_input, pre_act, out_grad, conv_weight, q_prev):
    shape = jax.ShapeDtypeStruct
    whole = pl.BlockSpec(memory_space=pltpu.VMEM)
    far = pl.BlockSpec(memory_space=pltpu.HBM)
    images, rows, cols = (lax.axis_size(a) for a in ALL)
    z, row = lax.axis_index("dp"), lax.axis_index("row")
    plane = rows * cols
    x, act, g = (v.reshape(256, 640) for v in (x_input, pre_act, out_grad))
    q_t = q_prev.transpose(1, 2, 0).reshape(128, 5760)

    sems = pltpu.SemaphoreType.DMA
    rims = call(
        rim_body,
        shape((plane, 32, 640), BF),
        1 << 24,
        1 << 20,
        vmem=62,
        in_specs=[far] * 2,
        scratch_shapes=[pltpu.VMEM((256, 640), BF)] * 2 + [sems((2,))],
    )(x, g)
    got = exchange(rims, PLANE)
    slices, q_one, y_two, slope = call(
        prepare_body,
        (
            shape((8, 160, 256), BF),
            shape((3, 384, 640), BF),
            shape((3, 128, 384), BF),
            shape((256, 640), F32),
        ),
        2 * 1152 * 640 * 256,
        8 << 20,
        vmem=62,
        in_specs=[far] * 3,
        scratch_shapes=[pltpu.VMEM((256, 640), BF)] * 2
        + [pltpu.VMEM((9, 128, 640), F32), sems((11,))],
    )(x, act, q_t)
    slices = exchange(slices, PLANE)

    strip = images * cols
    each = 64 // strip if 64 % strip == 0 and strip >= 8 else 8
    parts = 64 // each
    p_shape = shape((parts, each, 640), F32)
    keep, swap, p_keep, p_swap = call(
        power_body,
        (shape((256, 640), BF), shape((256, 640), BF), p_shape, p_shape),
        2 * 256 * 5760 * 1100,
        12 << 20,
        vmem=62,
        in_specs=[far] * 7,
        scratch_shapes=[
            pltpu.VMEM((256, 640), BF),
            pltpu.VMEM((256, 640), BF),
            pltpu.VMEM((plane, 32, 640), BF),
            pltpu.VMEM((256, 640), F32),
            pltpu.VMEM((3, 384, 640), BF),
            pltpu.VMEM((3, 128, 384), BF),
            pltpu.VMEM((9, 640, 640), BF),
            pltpu.VMEM((3, 288, 640), BF),
            pltpu.VMEM((3, 288, 640), BF),
            pltpu.VMEM((256, 640), F32),
            sems((15,)),
        ],
    )(x, g, got, slope, q_one, y_two, conv_weight)

    across = [(0, 1), (1, 0)]
    p_part = p_keep + lax.ppermute(p_swap, "row", across)
    swap = lax.ppermute(swap, "row", across)
    keep = call(stage_body, shape((256, 640), BF), 0, 8 << 20)(keep)
    p_part, slices = lax.optimization_barrier((p_part, slices))
    if parts == strip:
        p_got = exchange(p_part, ("dp", "col"))
        p_got = call(sum_body, p_shape, 0, 1 << 20)(p_got)
        p_own = exchange(p_got, ("dp", "col"))
    else:
        p_own = lax.psum(p_part, ("dp", "col"))

    w_own, p_t = call(
        project_body,
        (shape((512, 128), BF), shape((64, 640), F32)),
        2 * 512 * 640 * 128,
        2 << 20,
    )(p_own, keep, swap)
    w_all = shifts([w_own] * 4, "col")
    inverse, basis, share = call(
        factor_body,
        (shape((64, 64), F32), shape((64, 640), F32), shape((64, 160), F32)),
        1 << 30,
        1 << 20,
    )(p_t)

    sums = call(
        functools.partial(taps_body, images == 4),
        (shape((64, 384), BF),) * 4,
        2 * 160 * 2048 * 1152,
        2 << 20,
        scratch_shapes=[
            pltpu.VMEM((4, 512, 128), BF),
            pltpu.VMEM((34, 4, 16, 384), BF),
            pltpu.VMEM((1472, 128), F32),
        ],
    )(*w_all, slices, inverse)

    if images == 4:
        other_share = lax.ppermute(share, "row", across)
        mine = call(total_body, shape((64, 384), BF), 0, 1 << 20)(*shifts(sums, "dp"))
        every = shifts([mine] * 4, "col")
        other = [lax.ppermute(part, "row", across) for part in every]
        basis_out, q_out = call(
            place_body,
            (shape((2, 64, 160), F32), shape((2, 64, 1440), F32)),
            0,
            1 << 20,
            scratch_shapes=[pltpu.VMEM((2, 4, 64, 384), BF)],
        )(*every, *other, share, other_share)
        return basis_out.transpose(2, 0, 1), q_out.transpose(2, 0, 1)
    sums = jnp.stack(sums)
    sums = lax.psum(sums[:, :, :360].astype(F32), "dp")
    every = lax.all_gather(sums, PLANE).reshape(rows, cols, 4, 64, 9, 40)
    every = every.transpose(2, 4, 1, 5, 0, 3).reshape(5760, 2, 64)
    q_out = lax.dynamic_slice_in_dim(every, z * (5760 // images), 5760 // images, 0)
    bases = lax.all_gather(basis, "row").transpose(2, 0, 1)
    return lax.dynamic_slice_in_dim(bases, z * (640 // images), 640 // images, 0), q_out


def solution(mesh):
    tiles = P("dp", "row", "col", None)
    return jax.shard_map(
        on_device,
        mesh=mesh,
        in_specs=(tiles, tiles, tiles, P(), P()),
        out_specs=(P("dp", None, None), P("dp", None, None)),
        check_vma=False,
    )
```

```python
import functools

import jax
import jax.numpy as jnp
from jax import lax
from jax.experimental import pallas as pl
from jax.experimental.pallas import tpu as pltpu
from jax.sharding import PartitionSpec as P

PLANE = ("row", "col")
ALL = ("dp", "row", "col")
BF = jnp.bfloat16
F32 = jnp.float32
NN = ((1,), (0,))
NT = ((1,), (1,))
TN = ((0,), (0,))
MIB = 1024 * 1024


def dot(left, right, dims, precision=None):
    return lax.dot_general(
        left, right, (dims, ((), ())), precision=precision, preferred_element_type=F32
    )


def call(body, out, flops, moved, vmem=40, **extra):
    return pl.pallas_call(
        body,
        out_shape=out,
        cost_estimate=pl.CostEstimate(flops=flops, bytes_accessed=moved, transcendentals=0),
        compiler_params=pltpu.CompilerParams(vmem_limit_bytes=vmem * MIB),
        **extra,
    )


def exchange(chunks, axes):
    return lax.all_to_all(chunks, axes, 0, 0, tiled=True)


def shifts(values, axis):
    size = lax.axis_size(axis)
    moved = [values[0]]
    for s in range(1, len(values)):
        moved.append(lax.ppermute(values[s], axis, [(i, (i + s) % size) for i in range(size)]))
    return moved


def stacked_halves(value):
    high = value.astype(BF)
    return jnp.concatenate([high, (value - high.astype(F32)).astype(BF)], axis=0)


def paired_halves(value):
    total = value + pltpu.roll(value, 64, 1)
    high = total.astype(BF).astype(F32)
    lane = lax.broadcasted_iota(jnp.int32, value.shape, 1)
    return jnp.where(lane < 64, high, total - high)


def fetch(pairs, sems):
    copies = [pltpu.make_async_copy(src, dst, sems.at[i]) for i, (src, dst) in enumerate(pairs)]
    for copy in copies:
        copy.start()
    return copies


def rim_body(x_hbm, g_hbm, out_ref, x_ref, g_ref, sems):
    copies = fetch(((x_hbm, x_ref), (g_hbm, g_ref)), sems)
    row, col = lax.axis_index("row"), lax.axis_index("col")
    cols = out_ref.shape[0] // 2
    line = lax.broadcasted_iota(jnp.int32, (48, 256), 0)
    lane = lax.broadcasted_iota(jnp.int32, (48, 256), 1)
    ends = jnp.where(line < 32, 16 * (line % 16) + 15 * (line // 16), 240 * (1 - row) + line - 32)
    pick = jnp.where(lane == ends, 1.0, 0.0).astype(BF)
    for i, ref in enumerate((x_ref, g_ref)):
        copies[i].wait()
        rims = dot(pick, ref[...], NN)
        first, last, edge = rims[:16], rims[16:32], rims[32:]
        span = slice(16 * i, 16 * i + 16)
        for r in range(2):
            for c in range(cols):
                along = jnp.where(c > col, last, first)
                out_ref[r * cols + c, span] = jnp.where(row == r, along, edge).astype(BF)


def rim_pick(row, col, cols, s, first, count, start, width):
    cell = first + lax.broadcasted_iota(jnp.int32, (count, width), 0)
    lane = start + lax.broadcasted_iota(jnp.int32, (count, width), 1)
    y, x = cell // 16 - 1, cell % 16 + s - 1
    up = jnp.where(y < 0, -1, jnp.where(y > 15, 1, 0))
    side = jnp.where(x < 0, -1, jnp.where(x > 15, 1, 0))
    there_r, there_c = row + up, col + side
    inside = (there_r >= 0) & (there_r < 2) & (there_c >= 0) & (there_c < cols)
    got = 256 + (there_r * cols + there_c) * 16 + jnp.where(up != 0, x - 16 * side, y)
    index = jnp.where((up == 0) & (side == 0), 16 * y + x, got)
    hit = inside & (index == lane)
    return jnp.where(hit, 1.0, 0.0).astype(BF)


def prepare_body(
    x_hbm, act_hbm, q_hbm, slices_ref, q_one_ref, y_ref, slope_ref, x_ref, act_ref, q_all, sems
):
    pairs = [(x_hbm, x_ref), (act_hbm, act_ref)]
    pairs += [(q_hbm.at[:, 640 * t : 640 * t + 640], q_all.at[t]) for t in range(9)]
    copies = fetch(pairs, sems)
    copies[0].wait()
    copies[1].wait()
    act = act_ref[...].astype(F32)
    sigma = 1.0 / (1.0 + jnp.exp(-act))
    hidden = (act * sigma).astype(BF)
    slope_ref[...] = sigma * (1.0 + act * (1.0 - sigma))
    for layer, value in enumerate((x_ref[...], hidden)):
        turned = value.astype(F32).T
        for k in range(4):
            pieces = [turned[160 * j + 40 * k : 160 * j + 40 * k + 40] for j in range(4)]
            slices_ref[4 * layer + k] = jnp.concatenate(pieces, axis=0).astype(BF)
    for b in range(3):
        shifted = jnp.zeros((64, 384), F32)
        for a in range(3):
            t = 3 * a + b
            copies[2 + t].wait()
            q = q_all[t]
            q_one_ref[b, 128 * a : 128 * a + 128] = stacked_halves(q[:64])
            y = dot(stacked_halves(q[64:]), hidden, NT)
            y = jnp.concatenate([y[:64] + y[64:], jnp.zeros((64, 128), F32)], axis=1)
            shifted = shifted + (pltpu.roll(y, 16 * (2 - a), 1) if a < 2 else y)
        y_ref[b] = stacked_halves(shifted)


def power_body(
    x_hbm, g_hbm, got_hbm, slope_hbm, q_hbm, y_hbm, w_hbm,
    keep_ref, swap_ref, p_keep_ref, p_swap_ref,
    x_ref, g_ref, got_ref, slope_ref, q_ref, y_ref, w_all,
    x_win, g_win, back, sems,
):
    pairs = [(got_hbm, got_ref), (g_hbm, g_ref), (x_hbm, x_ref)]
    pairs += [(y_hbm, y_ref), (q_hbm, q_ref), (slope_hbm, slope_ref)]
    pairs += [(w_hbm.at[t // 3, t % 3], w_all.at[t]) for t in range(9)]
    copies = fetch(pairs, sems)
    row, col = lax.axis_index("row"), lax.axis_index("col")
    cols = got_ref.shape[0] // 2
    width = 256 + 32 * cols
    picks = [rim_pick(row, col, cols, s, 0, 288, 0, width) for s in (0, 2)]
    ends = [rim_pick(row, col, cols, 1, r, 16, 256, 32 * cols) for r in (0, 272)]
    picks = [picks[0], jnp.concatenate(ends, axis=0), picks[1]]
    copies[0].wait()
    for i, (ref, win) in enumerate(((g_ref, g_win), (x_ref, x_win))):
        copies[1 + i].wait()
        rims = got_ref[:, 16 - 16 * i : 32 - 16 * i, :].reshape(-1, 640)
        lines = dot(picks[1], rims, NN).astype(BF)
        win[1, 0:16] = lines[:16]
        win[1, 16:272] = ref[...]
        win[1, 272:288] = lines[16:]
        cells = jnp.concatenate([ref[...], rims], axis=0)
        for s in (0, 2):
            win[s] = dot(picks[s], cells, NN).astype(BF)
    copies[3].wait()
    copies[4].wait()
    two, z_sum = 0.0, 0.0
    for b in range(3):
        two = two + dot(y_ref[b][:, :288], g_win[2 - b], NN)
        wide = dot(x_win[b], q_ref[b], NT)
        for a in range(3):
            z_sum = z_sum + wide[16 * a : 16 * a + 256, 128 * a : 128 * a + 128]
    z_sum = paired_halves(z_sum).astype(BF)
    for a in range(3):
        windows = [g_win[2 - b, 16 * (2 - a) : 16 * (2 - a) + 256, :] for b in range(3)]
        for b in range(3):
            copies[6 + 3 * a + b].wait()
        taps = jnp.concatenate([w_all[3 * a + b] for b in range(3)], axis=1)
        term = dot(jnp.concatenate(windows, axis=1), taps, NT)
        back[...] = term if a == 0 else back[...] + term
    copies[5].wait()
    grad = (back[...] * slope_ref[...]).astype(BF)
    keep_ref[...] = jnp.where(row == 0, grad, g_ref[...])
    swap_ref[...] = jnp.where(row == 0, g_ref[...], grad)
    one = dot(z_sum, grad, TN)
    one, two = one[:64] + one[64:], two[:64] + two[64:]
    each = p_keep_ref.shape[1]
    for ref, value in (
        (p_keep_ref, jnp.where(row == 0, one, two)),
        (p_swap_ref, jnp.where(row == 0, two, one)),
    ):
        for i in range(64 // each):
            ref[i] = value[i * each : (i + 1) * each]


def add_body(left_ref, right_ref, out_ref):
    out_ref[...] = left_ref[...] + right_ref[...]


def stage_body(keep_ref, out_ref):
    out_ref[...] = keep_ref[...]


def sum_body(got_ref, out_ref):
    total = jnp.sum(got_ref[...], axis=0)
    for i in range(out_ref.shape[0]):
        out_ref[i] = total


def project_body(got_ref, keep_ref, swap_ref, w_ref, p_ref):
    row = lax.axis_index("row")
    each = got_ref.shape[1]
    for i in range(8):
        rows = [got_ref[i * (8 // each) + j] for j in range(8 // each)]
        p_ref[8 * i : 8 * i + 8, :] = jnp.concatenate(rows, axis=0)
    factor = stacked_halves(p_ref[...])
    for start, ref in ((row, keep_ref), (1 - row, swap_ref)):
        out = paired_halves(dot(ref[...], factor, NT)).astype(BF)
        w_ref[pl.ds(pl.multiple_of(256 * start, 256), 256), :] = out


def factor_body(p_ref, inverse_ref, basis_ref, share_ref):
    high = lax.Precision.HIGHEST
    line = lax.broadcasted_iota(jnp.int32, (64, 128), 0)
    lane = lax.broadcasted_iota(jnp.int32, (64, 128), 1)
    p = p_ref[...]
    unit = jnp.where(lane == line + 64, 1.0, 0.0)
    table = jnp.concatenate([dot(p, p, NT, high), unit[:, 64:]], axis=1)
    for k in range(0, 64, 2):
        row_a, row_b = table[k : k + 1, :], table[k + 1 : k + 2, :]
        col_a = jnp.broadcast_to(table[:, k : k + 1], (64, 128))
        col_b = jnp.broadcast_to(table[:, k + 1 : k + 2], (64, 128))
        over = 1.0 / col_a[k : k + 1, :]
        first = col_a * over
        cross = col_b[k : k + 1, :]
        row_b = row_b - first[k + 1 : k + 2, :] * row_a
        col_b = col_b - first * cross
        second = col_b * (1.0 / col_b[k + 1 : k + 2, :])
        first = jnp.where(line > k, first, 0.0)
        second = jnp.where(line > k + 1, second, 0.0)
        table = table - first * row_a - second * row_b
    pivots = jnp.sum(jnp.where(line == lane, table, 0.0), axis=1, keepdims=True)
    inverse = table[:, 64:] / jnp.sqrt(pivots)
    inverse_ref[...] = inverse
    basis = dot(inverse, p, NN, high)
    basis_ref[...] = basis
    z = lax.axis_index("dp")
    part = basis[:, :160]
    for i in range(1, 4):
        part = jnp.where(z == i, basis[:, 160 * i : 160 * i + 160], part)
    share_ref[...] = part


def taps_body(own_order, *refs):
    w_refs, (x_ref, inverse_ref) = refs[:4], refs[4:6]
    out_refs, (w_ref, image, sums) = refs[6:10], refs[10:]
    col = lax.axis_index("col")
    for s in range(4):
        w_ref[lax.rem(col + 4 - s, 4)] = w_refs[s][...]
    zero = jnp.zeros((1, 4, 16, 384), BF)
    image[0:1] = zero
    image[33:34] = zero
    at = lax.broadcasted_iota(jnp.int32, (2048, 128), 0) % 64
    strips = [w_ref[c].astype(F32).reshape(32, 16, 128) for c in range(4)]
    flat = jnp.stack(strips, axis=1).reshape(2048, 128)
    left = jnp.where(at == 63, 0.0, pltpu.roll(flat, 2047, 0))
    right = jnp.where(at == 0, 0.0, pltpu.roll(flat, 1, 0))
    for i, value in enumerate((left, flat, right)):
        value = value.astype(BF).reshape(32, 4, 16, 128)
        image[1:33, :, :, 128 * i : 128 * i + 128] = value
    slices = jnp.concatenate([x_ref[4 * r + c] for c in range(4) for r in range(2)], axis=1)
    for a in range(3):
        windows = [image[2 - a : 34 - a, c].reshape(512, 384) for c in range(4)]
        total = dot(slices, jnp.concatenate(windows, axis=0), NN)
        for b in range(3):
            t = 3 * a + b
            value = total[:, 128 * b : 128 * b + 128]
            sums[160 * t : 160 * t + 160, :] = value + pltpu.roll(value, 64, 1)
    sums[1440:1472, :] = jnp.zeros((32, 128), F32)
    inverse = inverse_ref[...]
    for s in range(4):
        i = lax.rem(lax.axis_index("dp") + s, 4) if own_order else s
        part = sums[pl.ds(pl.multiple_of(360 * i, 8), 384), :][:, :64]
        out_refs[s][...] = dot(inverse, part, NT, lax.Precision.HIGHEST).astype(BF)


def total_body(a_ref, b_ref, c_ref, d_ref, out_ref):
    total = a_ref[...].astype(F32) + b_ref[...].astype(F32)
    total = total + (c_ref[...].astype(F32) + d_ref[...].astype(F32))
    out_ref[...] = total.astype(BF)


def place_body(*refs):
    own, other, shares = refs[:4], refs[4:8], refs[8:10]
    basis_ref, out_ref, held = refs[10:]
    row, col = lax.axis_index("row"), lax.axis_index("col")
    for layer, parts, share in ((row, own, shares[0]), (1 - row, other, shares[1])):
        basis_ref[layer] = share[...]
        for s in range(4):
            held[layer, lax.rem(col + 4 - s, 4)] = parts[s][...]
    for layer in range(2):
        for k in range(4):
            value = held[layer, k].astype(F32)
            for j in range(9):
                start = 160 * j + 40 * k
                out_ref[layer, :, start : start + 40] = value[:, 40 * j : 40 * j + 40]


def on_device(x_input, pre_act, out_grad, conv_weight, q_prev):
    shape = jax.ShapeDtypeStruct
    whole = pl.BlockSpec(memory_space=pltpu.VMEM)
    far = pl.BlockSpec(memory_space=pltpu.HBM)
    images, rows, cols = (lax.axis_size(a) for a in ALL)
    z, row = lax.axis_index("dp"), lax.axis_index("row")
    plane = rows * cols
    x, act, g = (v.reshape(256, 640) for v in (x_input, pre_act, out_grad))
    q_t = q_prev.transpose(1, 2, 0).reshape(128, 5760)

    sems = pltpu.SemaphoreType.DMA
    rims = call(
        rim_body,
        shape((plane, 32, 640), BF),
        1 << 24,
        1 << 20,
        vmem=62,
        in_specs=[far] * 2,
        scratch_shapes=[pltpu.VMEM((256, 640), BF)] * 2 + [sems((2,))],
    )(x, g)
    got = exchange(rims, PLANE)
    slices, q_one, y_two, slope = call(
        prepare_body,
        (
            shape((8, 160, 256), BF),
            shape((3, 384, 640), BF),
            shape((3, 128, 384), BF),
            shape((256, 640), F32),
        ),
        2 * 1152 * 640 * 256,
        8 << 20,
        vmem=62,
        in_specs=[far] * 3,
        scratch_shapes=[pltpu.VMEM((256, 640), BF)] * 2
        + [pltpu.VMEM((9, 128, 640), F32), sems((11,))],
    )(x, act, q_t)
    slices = exchange(slices, PLANE)

    strip = images * cols
    each = 64 // strip if 64 % strip == 0 and strip >= 8 else 8
    parts = 64 // each
    p_shape = shape((parts, each, 640), F32)
    keep, swap, p_keep, p_swap = call(
        power_body,
        (shape((256, 640), BF), shape((256, 640), BF), p_shape, p_shape),
        2 * 256 * 5760 * 1100,
        12 << 20,
        vmem=62,
        in_specs=[far] * 7,
        scratch_shapes=[
            pltpu.VMEM((256, 640), BF),
            pltpu.VMEM((256, 640), BF),
            pltpu.VMEM((plane, 32, 640), BF),
            pltpu.VMEM((256, 640), F32),
            pltpu.VMEM((3, 384, 640), BF),
            pltpu.VMEM((3, 128, 384), BF),
            pltpu.VMEM((9, 640, 640), BF),
            pltpu.VMEM((3, 288, 640), BF),
            pltpu.VMEM((3, 288, 640), BF),
            pltpu.VMEM((256, 640), F32),
            sems((15,)),
        ],
    )(x, g, got, slope, q_one, y_two, conv_weight)

    across = [(0, 1), (1, 0)]
    p_swap = lax.ppermute(p_swap, "row", across)
    p_keep = call(stage_body, p_shape, 0, 8 << 20)(p_keep)
    p_part = call(add_body, p_shape, 0, 1 << 20)(p_keep, p_swap)
    swap = lax.ppermute(swap, "row", across)
    keep = call(stage_body, shape((256, 640), BF), 0, 8 << 20)(keep)
    p_part, slices = lax.optimization_barrier((p_part, slices))
    if parts == strip:
        p_got = exchange(p_part, ("dp", "col"))
        p_got = call(sum_body, p_shape, 0, 1 << 20)(p_got)
        p_own = exchange(p_got, ("dp", "col"))
    else:
        p_own = lax.psum(p_part, ("dp", "col"))

    w_own, p_t = call(
        project_body,
        (shape((512, 128), BF), shape((64, 640), F32)),
        2 * 512 * 640 * 128,
        2 << 20,
    )(p_own, keep, swap)
    w_all = shifts([w_own] * 4, "col")
    inverse, basis, share = call(
        factor_body,
        (shape((64, 64), F32), shape((64, 640), F32), shape((64, 160), F32)),
        1 << 30,
        1 << 20,
    )(p_t)

    sums = call(
        functools.partial(taps_body, images == 4),
        (shape((64, 384), BF),) * 4,
        2 * 160 * 2048 * 1152,
        2 << 20,
        scratch_shapes=[
            pltpu.VMEM((4, 512, 128), BF),
            pltpu.VMEM((34, 4, 16, 384), BF),
            pltpu.VMEM((1472, 128), F32),
        ],
    )(*w_all, slices, inverse)

    if images == 4:
        other_share = lax.ppermute(share, "row", across)
        mine = call(total_body, shape((64, 384), BF), 0, 1 << 20)(*shifts(sums, "dp"))
        every = shifts([mine] * 4, "col")
        other = [lax.ppermute(part, "row", across) for part in every]
        basis_out, q_out = call(
            place_body,
            (shape((2, 64, 160), F32), shape((2, 64, 1440), F32)),
            0,
            1 << 20,
            scratch_shapes=[pltpu.VMEM((2, 4, 64, 384), BF)],
        )(*every, *other, share, other_share)
        return basis_out.transpose(2, 0, 1), q_out.transpose(2, 0, 1)
    sums = jnp.stack(sums)
    sums = lax.psum(sums[:, :, :360].astype(F32), "dp")
    every = lax.all_gather(sums, PLANE).reshape(rows, cols, 4, 64, 9, 40)
    every = every.transpose(2, 4, 1, 5, 0, 3).reshape(5760, 2, 64)
    q_out = lax.dynamic_slice_in_dim(every, z * (5760 // images), 5760 // images, 0)
    bases = lax.all_gather(basis, "row").transpose(2, 0, 1)
    return lax.dynamic_slice_in_dim(bases, z * (640 // images), 640 // images, 0), q_out


def solution(mesh):
    tiles = P("dp", "row", "col", None)
    return jax.shard_map(
        on_device,
        mesh=mesh,
        in_specs=(tiles, tiles, tiles, P(), P()),
        out_specs=(P("dp", None, None), P("dp", None, None)),
        check_vma=False,
    )
```
